32 devices in a mesh: shard: 8 (over z, x), tensor: 4 (over y, core).
Axes of the slice: x: 2, y: 2, z: 4, core: 2. Of those that a mesh axis runs over, the one named last changes fastest.
Arguments:
- acts: bfloat16 [16384, 2048], P('shard', 'tensor'), may hold values from -6 to 6
- out_grad: bfloat16 [16384, 1920], P('shard'), may hold values from -6 to 6
- sample_rows: int32 [512], P('shard'), may hold values from 0 to 2047
- own_a: int32 [4, 4], replicated, may hold values from 0 to 3, each once within a row
- own_g: int32 [4, 5], replicated, may hold values from 0 to 4, each once within a row
- a_state: float32 [4, 4, 128, 128], P('tensor'), as said below
- g_state: float32 [4, 5, 96, 96], P('tensor'), as said below
- momentum: float32 [1920, 2048], P('shard', 'tensor'), may hold values from -6 to 6
- weight: float32 [1920, 2048], P('shard', 'tensor'), may hold values from -6 to 6
Outputs:
- a_state_new: float32 [4, 4, 128, 128], P('tensor')
- g_state_new: float32 [4, 5, 96, 96], P('tensor')
- momentum_new: float32 [1920, 2048], P('shard', 'tensor')
- weight_new: float32 [1920, 2048], P('shard', 'tensor')
- weight_bf16: bfloat16 [1920, 2048], P(None, 'tensor')
The draws below stay inside these ranges and needn't reach their ends.
Inputs may be any that keep to these rules, and one draw needn't show every extreme that they name: `own_a`: slot s of a group is owned by the shard index s times the whole part of the shard axis's size over the group's number of slots. `own_g`: slot s of a group is owned by the shard index s times the whole part of the shard axis's size over the group's number of slots. `a_state`: every slot is symmetric positive definite. `g_state`: every slot is symmetric positive definite.
All inputs are finite; a program needn't handle non-finite values. Where the reference program divides by a largest or mean magnitude, that divisor is 1e-20 or more.
Results may differ from the reference program's by a relative error of at most 0.0004.
Values may be sent and summed in bfloat16 or wider, within the bound.
No kernel may reach another device: no remote copies, remote signals or barrier semaphores. Data moves between devices by JAX's collectives and lax.ppermute only.
A program may use at most 64 MiB of HBM per device.

```python
import math
import jax
import jax.numpy as jnp
from jax import lax

D = 2048
Q = 1920
BA = 128
BG = 96
TOK_DEV = 2048
S_DEV = 64
NS_IT = 5
TOKENS = 16384
SAMPLES = 512
ABLK_T = 4
GBLK_T = 5
N_TENSOR = 4


def draw_factor(key, count, width):
    noise_key, diag_key = jax.random.split(key)
    noise = jax.random.normal(noise_key, (N_TENSOR, count, width, width), jnp.float32)
    spread = (noise + jnp.swapaxes(noise, -1, -2)) * (0.3 / math.sqrt(width))
    diagonal = jax.random.uniform(diag_key, (N_TENSOR, count, width), jnp.float32, 1.0, 3.0)
    return spread + diagonal[..., None] * jnp.eye(width, dtype=jnp.float32)


def draw_a_state(key, part):
    return draw_factor(jax.random.fold_in(key, 31), ABLK_T, BA)


def draw_g_state(key, part):
    return draw_factor(jax.random.fold_in(key, 47), GBLK_T, BG)


def plant(array, rng, smallest, top_value):
    spot = [jax.random.randint(jax.random.fold_in(rng, axis), (), 0, length) for axis, length in enumerate(array.shape)]
    longest = array.shape.index(max(array.shape))
    neighbour = spot[:longest] + [(spot[longest] + 1) % array.shape[longest]] + spot[longest + 1:]
    return array.at[tuple(spot)].set(smallest).at[tuple(neighbour)].set(top_value)


def shard_levels(stream_key, shape, shards, least, top_value):
    def one(dim, shards_of):
        draws = jax.random.uniform(jax.random.fold_in(jax.random.fold_in(stream_key, 6), dim), (shards_of,), jnp.float32, least / len(shards), top_value / len(shards))
        return jnp.repeat(jnp.exp(draws), shape[dim] // shards_of).reshape((-1,) + (1,) * (len(shape) - dim - 1))

    gain = one(*shards[0])
    for cut in shards[1:]:
        gain = gain * one(*cut)
    return gain


def normal_values(rng, shape, deviation, most, shards=(), kind=jnp.bfloat16):
    factor_of = shard_levels(rng, shape, shards, -0.22, 0.18) if shards else 1.0
    array = jax.random.normal(rng, shape, jnp.float32) * deviation * factor_of
    return jnp.minimum(jnp.maximum(array, -most), most).astype(kind)


def setup_inputs(seed: int = 0) -> dict:
    key_list = jax.random.split(jax.random.key(seed), 10)
    acts = normal_values(key_list[0], (TOKENS, D), 1.0, 6.0, ((0, 8), (1, 4)))
    out_grad = normal_values(key_list[1], (TOKENS, Q), 1.0, 6.0, ((0, 8),))
    sample_rows = plant(jax.random.randint(key_list[2], (SAMPLES,), 0, TOK_DEV), jax.random.fold_in(key_list[2], 1), 0, TOK_DEV - 1).astype(jnp.int32)
    own_a = jax.vmap(lambda own: jax.random.permutation(own, ABLK_T))(jax.random.split(key_list[3], N_TENSOR)).reshape((N_TENSOR, ABLK_T)).astype(jnp.int32)
    own_g = jax.vmap(lambda own: jax.random.permutation(own, GBLK_T))(jax.random.split(key_list[4], N_TENSOR)).reshape((N_TENSOR, GBLK_T)).astype(jnp.int32)
    a_state = draw_a_state(jax.random.fold_in(key_list[9], 71), 0)
    g_state = draw_g_state(jax.random.fold_in(key_list[9], 71), 0)
    momentum = normal_values(key_list[7], (Q, D), 1.0, 6.0, ((0, 8), (1, 4)), jnp.float32)
    weight = normal_values(key_list[8], (Q, D), 1.0, 6.0, ((0, 8), (1, 4)), jnp.float32)
    return dict(acts=acts, out_grad=out_grad, sample_rows=sample_rows, own_a=own_a, own_g=own_g, a_state=a_state, g_state=g_state, momentum=momentum, weight=weight)


factor_decay = 0.8
damping_rate = 0.03
momentum_rate = 0.9
decay_rate = 0.01
learn_rate = 0.05
epsilon_sq = 1e-06
highest = lax.Precision.HIGHEST

def newton_inverse(factor):
    width = factor.shape[-1]
    identity = jnp.eye(width, dtype=jnp.float32)
    trace_mean = jnp.trace(factor, axis1=-2, axis2=-1) / width
    damped = factor + damping_rate * trace_mean[:, None, None] * identity
    bound = lax.optimization_barrier(jnp.max(lax.optimization_barrier(jnp.sum(jnp.abs(damped), axis=-1)), axis=-1))
    guess = identity[None] / bound[:, None, None]
    for iteration in range(NS_IT):
        product = jnp.einsum('bij,bjk->bik', damped, guess, precision=highest)
        guess = jnp.einsum('bij,bjk->bik', guess, 2.0 * identity - product, precision=highest)
    return guess

def block_stats(rows, width):
    blocks = rows.astype(jnp.float32).reshape(rows.shape[0], -1, width)
    return jnp.einsum('sbi,sbj->bij', blocks, blocks)

def reference(acts, out_grad, sample_rows, own_a, own_g, a_state, g_state, momentum, weight):
    offsets = jnp.arange(SAMPLES, dtype=jnp.int32) // S_DEV * TOK_DEV
    picks = (offsets + sample_rows).astype(jnp.int32)
    stats_a = block_stats(acts[picks], BA).reshape(N_TENSOR, ABLK_T, BA, BA)
    stats_g = block_stats(out_grad[picks], BG).reshape(N_TENSOR, GBLK_T, BG, BG)
    groups = jnp.arange(N_TENSOR, dtype=jnp.int32)[:, None]
    fac_a = factor_decay * a_state[groups, own_a] + (1.0 - factor_decay) / SAMPLES * stats_a
    fac_g = factor_decay * g_state[groups, own_g] + (1.0 - factor_decay) / SAMPLES * stats_g
    a_new = jnp.zeros_like(a_state).at[groups, own_a].set(fac_a)
    g_new = jnp.zeros_like(g_state).at[groups, own_g].set(fac_g)
    inv_a = newton_inverse(fac_a.reshape(-1, BA, BA))
    inv_g = newton_inverse(fac_g.reshape(-1, BG, BG))
    raw_product = jnp.dot(out_grad.T, acts, preferred_element_type=jnp.float32)
    left_done = jnp.einsum('bij,bjd->bid', inv_g, raw_product.reshape(Q // BG, BG, D), precision=highest).reshape(Q, D)
    precon = jnp.einsum('qbi,bij->qbj', left_done.reshape(Q, D // BA, BA), inv_a, precision=highest).reshape(Q, D)
    mean_sq = jnp.mean(precon * precon)
    update = precon / jnp.sqrt(mean_sq + epsilon_sq)
    momentum_new = momentum_rate * momentum + update + decay_rate * weight
    weight_new = weight - learn_rate * momentum_new
    return (a_new, g_new, momentum_new, weight_new, weight_new.astype(jnp.bfloat16))
```

```python
import jax
import jax.numpy as jnp
from jax import lax
from jax.experimental import pallas as pl
from jax.experimental.pallas import tpu as pltpu
from jax.sharding import PartitionSpec as P

NS_IT = 5


factor_decay = 0.8
damping_rate = 0.03
momentum_rate = 0.9
decay_rate = 0.01
learn_rate = 0.05
epsilon_sq = 1e-06
highest = lax.Precision.HIGHEST
f32 = jnp.float32
bf16 = jnp.bfloat16


def newton_inverse(factor):
    width = factor.shape[-1]
    identity = jnp.eye(width, dtype=jnp.float32)
    trace_mean = jnp.trace(factor, axis1=-2, axis2=-1) / width
    damped = factor + damping_rate * trace_mean[:, None, None] * identity
    bound = jnp.max(jnp.sum(jnp.abs(damped), axis=-1), axis=-1)
    guess = identity[None] / bound[:, None, None]
    for iteration in range(NS_IT):
        product = jnp.einsum("bij,bjk->bik", damped, guess, precision=highest)
        guess = jnp.einsum("bij,bjk->bik", guess, 2.0 * identity - product, precision=highest)
    return guess


def local_stats(rows, width):
    blocks = rows.reshape(rows.shape[0], -1, width)
    return jnp.einsum("sbi,sbj->bij", blocks, blocks, preferred_element_type=jnp.float32)


def owner_part(slots, shard_pos, shard_count):
    count = slots.shape[0]
    stride = shard_count // count
    slot_pos = jnp.minimum(shard_pos // stride, count - 1)
    mine = lax.dynamic_index_in_dim(slots, slot_pos, 0, keepdims=True)
    inverse = newton_inverse(mine)
    marker = (jnp.arange(count, dtype=jnp.int32) * stride == shard_pos).astype(jnp.float32)
    return marker[:, None, None] * inverse


def general(acts, out_grad, sample_rows, own_a, own_g, a_state, g_state, momentum, weight):
    shard_count = lax.axis_size("shard")
    tensor_count = lax.axis_size("tensor")
    shard_pos = lax.axis_index("shard")
    tensor_pos = lax.axis_index("tensor")
    block_a = a_state.shape[-1]
    block_g = g_state.shape[-1]
    samples = sample_rows.shape[0] * shard_count
    fresh_share = (1.0 - factor_decay) / samples
    picked_a = jnp.take(acts, sample_rows, axis=0)
    picked_g = jnp.take(out_grad, sample_rows, axis=0)
    group_cols = out_grad.shape[1] // tensor_count
    picked_g = lax.dynamic_slice_in_dim(picked_g, tensor_pos * group_cols, group_cols, 1)
    stats_a = local_stats(picked_a, block_a)
    stats_g = local_stats(picked_g, block_g)
    row_a = lax.dynamic_index_in_dim(own_a, tensor_pos, 0, keepdims=False)
    row_g = lax.dynamic_index_in_dim(own_g, tensor_pos, 0, keepdims=False)
    select_a = (row_a[None, :] == jnp.arange(row_a.shape[0], dtype=jnp.int32)[:, None]).astype(
        jnp.float32
    )
    select_g = (row_g[None, :] == jnp.arange(row_g.shape[0], dtype=jnp.int32)[:, None]).astype(
        jnp.float32
    )
    summed_a, summed_g = lax.psum((fresh_share * stats_a, fresh_share * stats_g), "shard")
    stored_a = jnp.einsum("sb,sij->bij", select_a, a_state[0], precision=highest)
    stored_g = jnp.einsum("sb,sij->bij", select_g, g_state[0], precision=highest)
    fac_a = factor_decay * stored_a + summed_a
    fac_g = factor_decay * stored_g + summed_g
    slots_a = jnp.einsum("sb,bij->sij", select_a, fac_a, precision=highest)
    slots_g = jnp.einsum("sb,bij->sij", select_g, fac_g, precision=highest)
    new_a_state = slots_a[None]
    new_g_state = slots_g[None]
    slot_inv_a, slot_inv_g = lax.psum(
        (owner_part(slots_a, shard_pos, shard_count), owner_part(slots_g, shard_pos, shard_count)),
        "shard",
    )
    inv_a = jnp.einsum("sb,sij->bij", select_a, slot_inv_a, precision=highest)
    local_inv_g = jnp.einsum("sb,sij->bij", select_g, slot_inv_g, precision=highest)
    inv_g = lax.all_gather(local_inv_g, "tensor", axis=0, tiled=True)
    raw_product = lax.dot_general(
        out_grad, acts, (((0,), (0,)), ((), ())), preferred_element_type=jnp.float32
    )
    left_done = jnp.einsum(
        "bij,bjd->bid", inv_g, raw_product.reshape(inv_g.shape[0], block_g, -1), precision=highest
    ).reshape(raw_product.shape)
    owned_rows = lax.psum_scatter(left_done, "shard", scatter_dimension=0, tiled=True)
    precon = jnp.einsum(
        "qbi,bij->qbj",
        owned_rows.reshape(owned_rows.shape[0], -1, block_a),
        inv_a,
        precision=highest,
    ).reshape(owned_rows.shape)
    square_total = lax.psum(jnp.sum(precon * precon), ("shard", "tensor"))
    mean_sq = square_total / (momentum.shape[0] * shard_count * momentum.shape[1] * tensor_count)
    update = precon / jnp.sqrt(mean_sq + epsilon_sq)
    momentum_new = momentum_rate * momentum + update + decay_rate * weight
    weight_new = weight - learn_rate * momentum_new
    gathered = lax.all_gather(weight_new.astype(jnp.bfloat16), "shard", axis=0, tiled=True)
    return (new_a_state, new_g_state, momentum_new, weight_new, gathered)


def swap(value, bit):
    return lax.ppermute(value, "shard", [(i, i ^ bit) for i in range(8)])


def swap_t(value, bit):
    return lax.ppermute(value, "tensor", [(i, i ^ bit) for i in range(4)])


def encode(value):
    top = jnp.max(jnp.abs(value))
    power = jnp.floor(jnp.log2(jnp.maximum(top, 1e-30)))
    scaled = (value * jnp.exp2(14.0 - power)).astype(jnp.float16)
    tail = jnp.full((16, value.shape[1]), power, jnp.float16)
    return jnp.concatenate([scaled, tail], axis=0)


def decode(packed):
    power = packed[-1, 0].astype(f32)
    return packed[:-16].astype(f32) * jnp.exp2(power - 14.0)


def pick(flag, if_zero, if_one):
    return jnp.where(flag == 0, if_zero, if_one)


def factor_kernel(
    share, info, picks, a_state, g_state, a_new, g_new, inv_a, inv_g
):
    count_a, width_a = a_state.shape[0], a_state.shape[1]
    count_g, width_g = g_state.shape[0], g_state.shape[1]
    errors, inverses, scales = [], [], []
    for index in range(count_a + count_g):
        is_a = index < count_a
        width = width_a if is_a else width_g
        place = index if is_a else index - count_a
        start = place * width_a if is_a else count_a * width_a + place * width_g
        rows = picks[:, start : start + width]
        stats = lax.dot_general(
            rows, rows, (((0,), (0,)), ((), ())), preferred_element_type=f32
        )
        slot = info[index]
        stored = (a_state if is_a else g_state)[slot]
        factor = factor_decay * stored + share * stats
        (a_new if is_a else g_new)[slot] = factor
        row = lax.broadcasted_iota(jnp.int32, (width, width), 0)
        col = lax.broadcasted_iota(jnp.int32, (width, width), 1)
        identity = (row == col).astype(f32)
        trace = jnp.sum(factor * identity) / width
        damped = factor + (damping_rate * trace) * identity
        bound = jnp.max(jnp.sum(jnp.abs(damped), axis=0))
        error = identity - damped / bound
        errors.append(error)
        inverses.append(identity + error)
        scales.append(bound)
    blocks = range(count_a + count_g)
    dot = lambda p, q: jnp.dot(p, q, preferred_element_type=f32, precision=highest)
    errors = [dot(errors[i], errors[i]) for i in blocks]
    for step in range(1, NS_IT - 1):
        grown = [dot(inverses[i], errors[i]) for i in blocks]
        squares = [dot(errors[i], errors[i]) for i in blocks]
        inverses = [inverses[i] + grown[i] for i in blocks]
        errors = squares
    inverses = [(inverses[i] + dot(inverses[i], errors[i])) / scales[i] for i in blocks]
    for index in blocks:
        if index < count_a:
            inv_a[index] = inverses[index]
        else:
            inv_g[index - count_a] = inverses[index]


def precon_kernel(info, part_a, part_b, inv_g, inv_a, top, mid, total):
    side = info[0]
    width_g, width_a = inv_g.shape[-1], inv_a.shape[-1]
    half = width_g // 2
    dot = lambda p, q: jnp.dot(p, q, preferred_element_type=f32, precision=highest)
    squares = jnp.zeros((width_g, width_a), f32)
    for piece, part in enumerate((part_a, part_b)):
        for place in range(2):
            for block in range(2):
                values = dot(
                    inv_g[place],
                    part[
                        place * width_g : (place + 1) * width_g,
                        block * width_a : (block + 1) * width_a,
                    ],
                )
                values = dot(values, inv_a[2 * piece + block])
                squares += values * values
                column = (2 * piece + block) * width_a
                top[place * width_g : (place + 1) * width_g, column : column + width_a] = values
        packed = part[2 * width_g : 2 * width_g + half, :]
        values = jnp.concatenate([packed[:, :width_a], packed[:, width_a:]], axis=0)
        values = dot(dot(inv_g[2], values), inv_a[2 * piece + side])
        squares += values * values
        mid[:, piece * width_a : (piece + 1) * width_a] = values
    total[...] = jnp.full(total.shape, jnp.sum(squares), f32)


def fast(acts, out_grad, sample_rows, own_a, own_g, a_state, g_state, momentum, weight):
    shard_pos = lax.axis_index("shard")
    tensor_pos = lax.axis_index("tensor")
    side, low, high = shard_pos & 1, (shard_pos >> 1) & 1, shard_pos >> 2
    count_a, width_a = a_state.shape[1], a_state.shape[2]
    count_g, width_g = g_state.shape[1], g_state.shape[2]
    group_cols = count_g * width_g
    cols = acts.shape[1]
    rows = momentum.shape[0]
    samples = sample_rows.shape[0] * 8
    share = (1.0 - factor_decay) / samples
    vmem = pl.BlockSpec(memory_space=pltpu.VMEM)
    smem = pl.BlockSpec(memory_space=pltpu.SMEM)

    picked_a = jnp.take(acts, sample_rows, axis=0)
    picked_g = jnp.take(out_grad, sample_rows, axis=0)
    picked_g = lax.dynamic_slice_in_dim(picked_g, tensor_pos * group_cols, group_cols, 1)
    picks = jnp.concatenate([picked_a, picked_g], axis=1)[None]
    for bit, flag in ((4, high), (2, low), (1, side)):
        other = swap(picks, bit)
        picks = jnp.stack([pick(flag, picks, other), pick(flag, other, picks)], axis=1)
        picks = picks.reshape((-1,) + picks.shape[2:])
    picks = picks.reshape(2, 2, 2, -1, picks.shape[-1]).transpose(0, 1, 2, 3, 4)
    picks = picks.reshape(samples, -1)

    row_a = lax.dynamic_index_in_dim(own_a, tensor_pos, 0, keepdims=False)
    row_g = lax.dynamic_index_in_dim(own_g, tensor_pos, 0, keepdims=False)
    new_a, new_g, inv_a, inv_g = pl.pallas_call(
        lambda *refs: factor_kernel(share, *refs),
        in_specs=[smem, vmem, vmem, vmem],
        out_specs=[vmem] * 4,
        out_shape=[
            jax.ShapeDtypeStruct(a_state.shape[1:], f32),
            jax.ShapeDtypeStruct(g_state.shape[1:], f32),
            jax.ShapeDtypeStruct(a_state.shape[1:], f32),
            jax.ShapeDtypeStruct(g_state.shape[1:], f32),
        ],
        compiler_params=pltpu.CompilerParams(vmem_limit_bytes=32 * 2**20),
        name="factors",
    )(jnp.concatenate([row_a, row_g]), picks, a_state[0], g_state[0])
    needed = pick(side, inv_g[jnp.array([0, 1, 2])], inv_g[jnp.array([3, 4, 2])])
    route = [
        ((2 * a + b) * 4 + c, (2 * c + b) * 4 + a)
        for a in range(4)
        for b in range(2)
        for c in range(4)
    ]
    inv_rows = lax.ppermute(needed, ("shard", "tensor"), route)

    half = cols // 2
    head = 2 * width_g
    mid = width_g // 2

    def units(first):
        raw = lax.dot_general(
            out_grad,
            acts[:, first : first + half],
            (((0,), (0,)), ((), ())),
            preferred_element_type=f32,
        )
        groups = raw.reshape(4, group_cols, half)
        middle = groups[:, head : head + width_g]
        left, right = middle[:, :, : half // 2], middle[:, :, half // 2 :]
        packed = [jnp.concatenate([m[:, :mid], m[:, mid:]], axis=2) for m in (left, right)]
        zero = jnp.concatenate([groups[:, :head], packed[0]], axis=1)
        one = jnp.concatenate([groups[:, head + width_g :], packed[1]], axis=1)
        return zero.reshape(2, 2, -1, half), one.reshape(2, 2, -1, half)

    def exchange(keep, send, bit):
        got = decode(swap(encode(send.reshape(-1, half)), bit))
        return keep + got.reshape(keep.shape)

    zero, one = units(0)
    part = exchange(pick(side, zero, one), pick(side, one, zero), 1)
    part = exchange(pick(low, part[:, 0], part[:, 1]), pick(low, part[:, 1], part[:, 0]), 2)
    part_a = exchange(pick(high, part[0], part[1]), pick(high, part[1], part[0]), 4)

    zero, one = units(half)
    both = jnp.stack([zero, one], axis=0)
    part = exchange(
        pick(low, both[:, :, 0], both[:, :, 1]), pick(low, both[:, :, 1], both[:, :, 0]), 2
    )
    part = exchange(pick(high, part[:, 0], part[:, 1]), pick(high, part[:, 1], part[:, 0]), 4)
    part_b = exchange(pick(side, part[0], part[1]), pick(side, part[1], part[0]), 1)

    top, middle, total = pl.pallas_call(
        precon_kernel,
        in_specs=[smem, vmem, vmem, vmem, vmem],
        out_specs=[vmem] * 3,
        out_shape=[
            jax.ShapeDtypeStruct((head, cols), f32),
            jax.ShapeDtypeStruct((width_g, half), f32),
            jax.ShapeDtypeStruct((8, half), f32),
        ],
        compiler_params=pltpu.CompilerParams(vmem_limit_bytes=32 * 2**20),
        name="precon",
    )(side.reshape(1), part_a, part_b, inv_rows, inv_a)

    total = total + swap_t(total, 1)
    total = total + swap_t(total, 2)
    own_mid = pick(side, middle[:mid], middle[mid:])
    give = pick(side, middle[mid:], middle[:mid])
    got = swap(jnp.concatenate([give, total], axis=0), 1)
    total = total + got[mid:]
    total = total + swap(total, 2)
    total = total + swap(total, 4)
    mean_sq = total[0, 0] / (rows * 8 * cols * 4)
    other_mid = got[:mid]
    quarter = half // 2
    pairs = []
    for piece in range(2):
        span = slice(piece * quarter, (piece + 1) * quarter)
        pairs += [
            pick(side, own_mid[:, span], other_mid[:, span]),
            pick(side, other_mid[:, span], own_mid[:, span]),
        ]
    middle_rows = jnp.concatenate(pairs, axis=1)
    precon = pick(
        side,
        jnp.concatenate([top, middle_rows], axis=0),
        jnp.concatenate([middle_rows, top], axis=0),
    )
    update = precon / jnp.sqrt(mean_sq + epsilon_sq)
    momentum_new = momentum_rate * momentum + update + decay_rate * weight
    weight_new = weight - learn_rate * momentum_new
    rounded = weight_new.astype(bf16)

    def spread(values, bit, flag, axis):
        other = swap(values, bit)
        return jnp.stack([pick(flag, values, other), pick(flag, other, values)], axis=axis)

    piece = rounded[:, :half]
    piece = spread(piece, 4, high, 0)
    piece = spread(piece, 2, low, 1)
    whole_a = spread(piece, 1, side, 2).reshape(-1, half)
    piece = rounded[:, half:]
    piece = spread(piece, 1, side, 0)
    piece = spread(piece, 4, high, 0)
    whole_b = spread(piece, 2, low, 1).reshape(-1, half)
    gathered = jnp.concatenate([whole_a, whole_b], axis=1)
    return (new_a[None], new_g[None], momentum_new, weight_new, gathered)


def local(acts, out_grad, sample_rows, own_a, own_g, a_state, g_state, momentum, weight):
    shapes_fit = (
        lax.axis_size("shard") == 8
        and lax.axis_size("tensor") == 4
        and a_state.shape[1:] == (4, 128, 128)
        and g_state.shape[1:] == (5, 96, 96)
    )
    plan = fast if shapes_fit else general
    return plan(acts, out_grad, sample_rows, own_a, own_g, a_state, g_state, momentum, weight)


def solution(mesh):
    return jax.shard_map(
        local,
        mesh=mesh,
        in_specs=(
            P("shard", "tensor"),
            P("shard", None),
            P("shard"),
            P(),
            P(),
            P("tensor", None, None, None),
            P("tensor", None, None, None),
            P("shard", "tensor"),
            P("shard", "tensor"),
        ),
        out_specs=(
            P("tensor", None, None, None),
            P("tensor", None, None, None),
            P("shard", "tensor"),
            P("shard", "tensor"),
            P(None, "tensor"),
        ),
        check_vma=False,
    )
```

```python
import jax
import jax.numpy as jnp
from jax import lax
from jax.experimental import pallas as pl
from jax.experimental.pallas import tpu as pltpu
from jax.sharding import PartitionSpec as P

NS_IT = 5


factor_decay = 0.8
damping_rate = 0.03
momentum_rate = 0.9
decay_rate = 0.01
learn_rate = 0.05
epsilon_sq = 1e-06
highest = lax.Precision.HIGHEST
f32 = jnp.float32
bf16 = jnp.bfloat16


def newton_inverse(factor):
    width = factor.shape[-1]
    identity = jnp.eye(width, dtype=jnp.float32)
    trace_mean = jnp.trace(factor, axis1=-2, axis2=-1) / width
    damped = factor + damping_rate * trace_mean[:, None, None] * identity
    bound = jnp.max(jnp.sum(jnp.abs(damped), axis=-1), axis=-1)
    guess = identity[None] / bound[:, None, None]
    for iteration in range(NS_IT):
        product = jnp.einsum("bij,bjk->bik", damped, guess, precision=highest)
        guess = jnp.einsum("bij,bjk->bik", guess, 2.0 * identity - product, precision=highest)
    return guess


def local_stats(rows, width):
    blocks = rows.reshape(rows.shape[0], -1, width)
    return jnp.einsum("sbi,sbj->bij", blocks, blocks, preferred_element_type=jnp.float32)


def owner_part(slots, shard_pos, shard_count):
    count = slots.shape[0]
    stride = shard_count // count
    slot_pos = jnp.minimum(shard_pos // stride, count - 1)
    mine = lax.dynamic_index_in_dim(slots, slot_pos, 0, keepdims=True)
    inverse = newton_inverse(mine)
    marker = (jnp.arange(count, dtype=jnp.int32) * stride == shard_pos).astype(jnp.float32)
    return marker[:, None, None] * inverse


def general(acts, out_grad, sample_rows, own_a, own_g, a_state, g_state, momentum, weight):
    shard_count = lax.axis_size("shard")
    tensor_count = lax.axis_size("tensor")
    shard_pos = lax.axis_index("shard")
    tensor_pos = lax.axis_index("tensor")
    block_a = a_state.shape[-1]
    block_g = g_state.shape[-1]
    samples = sample_rows.shape[0] * shard_count
    fresh_share = (1.0 - factor_decay) / samples
    picked_a = jnp.take(acts, sample_rows, axis=0)
    picked_g = jnp.take(out_grad, sample_rows, axis=0)
    group_cols = out_grad.shape[1] // tensor_count
    picked_g = lax.dynamic_slice_in_dim(picked_g, tensor_pos * group_cols, group_cols, 1)
    stats_a = local_stats(picked_a, block_a)
    stats_g = local_stats(picked_g, block_g)
    row_a = lax.dynamic_index_in_dim(own_a, tensor_pos, 0, keepdims=False)
    row_g = lax.dynamic_index_in_dim(own_g, tensor_pos, 0, keepdims=False)
    select_a = (row_a[None, :] == jnp.arange(row_a.shape[0], dtype=jnp.int32)[:, None]).astype(
        jnp.float32
    )
    select_g = (row_g[None, :] == jnp.arange(row_g.shape[0], dtype=jnp.int32)[:, None]).astype(
        jnp.float32
    )
    summed_a, summed_g = lax.psum((fresh_share * stats_a, fresh_share * stats_g), "shard")
    stored_a = jnp.einsum("sb,sij->bij", select_a, a_state[0], precision=highest)
    stored_g = jnp.einsum("sb,sij->bij", select_g, g_state[0], precision=highest)
    fac_a = factor_decay * stored_a + summed_a
    fac_g = factor_decay * stored_g + summed_g
    slots_a = jnp.einsum("sb,bij->sij", select_a, fac_a, precision=highest)
    slots_g = jnp.einsum("sb,bij->sij", select_g, fac_g, precision=highest)
    new_a_state = slots_a[None]
    new_g_state = slots_g[None]
    slot_inv_a, slot_inv_g = lax.psum(
        (owner_part(slots_a, shard_pos, shard_count), owner_part(slots_g, shard_pos, shard_count)),
        "shard",
    )
    inv_a = jnp.einsum("sb,sij->bij", select_a, slot_inv_a, precision=highest)
    local_inv_g = jnp.einsum("sb,sij->bij", select_g, slot_inv_g, precision=highest)
    inv_g = lax.all_gather(local_inv_g, "tensor", axis=0, tiled=True)
    raw_product = lax.dot_general(
        out_grad, acts, (((0,), (0,)), ((), ())), preferred_element_type=jnp.float32
    )
    left_done = jnp.einsum(
        "bij,bjd->bid", inv_g, raw_product.reshape(inv_g.shape[0], block_g, -1), precision=highest
    ).reshape(raw_product.shape)
    owned_rows = lax.psum_scatter(left_done, "shard", scatter_dimension=0, tiled=True)
    precon = jnp.einsum(
        "qbi,bij->qbj",
        owned_rows.reshape(owned_rows.shape[0], -1, block_a),
        inv_a,
        precision=highest,
    ).reshape(owned_rows.shape)
    square_total = lax.psum(jnp.sum(precon * precon), ("shard", "tensor"))
    mean_sq = square_total / (momentum.shape[0] * shard_count * momentum.shape[1] * tensor_count)
    update = precon / jnp.sqrt(mean_sq + epsilon_sq)
    momentum_new = momentum_rate * momentum + update + decay_rate * weight
    weight_new = weight - learn_rate * momentum_new
    gathered = lax.all_gather(weight_new.astype(jnp.bfloat16), "shard", axis=0, tiled=True)
    return (new_a_state, new_g_state, momentum_new, weight_new, gathered)


GROUP = 16
vmem = pl.BlockSpec(memory_space=pltpu.VMEM)
smem = pl.BlockSpec(memory_space=pltpu.SMEM)
anywhere = pl.BlockSpec(memory_space=pl.ANY)


def params(mib):
    return pltpu.CompilerParams(vmem_limit_bytes=mib * 2**20)


def shaped(shape, kind):
    return jax.ShapeDtypeStruct(shape, kind)


def swap(value, bit):
    return lax.ppermute(value, "shard", [(i, i ^ bit) for i in range(8)])


def swap_t(value, bit):
    return lax.ppermute(value, "tensor", [(i, i ^ bit) for i in range(4)])


def pick(flag, if_zero, if_one):
    return jnp.where(flag == 0, if_zero, if_one)


def encode(value, store):
    rows, width = value.shape
    powers = []
    for first in range(0, rows, GROUP):
        part = value[first : first + GROUP]
        top = jnp.max(jnp.abs(part), axis=0, keepdims=True)
        power = jnp.floor(jnp.log2(jnp.maximum(top, 1e-30)))
        scaled = jnp.clip(jnp.round(part * jnp.exp2(14.0 - power)), -32767.0, 32767.0)
        store(first, scaled.astype(jnp.int32).astype(jnp.int16))
        powers.append(power)
    powers += [jnp.zeros((1, width), f32)] * (GROUP - len(powers))
    store(rows, jnp.concatenate(powers, axis=0).astype(jnp.int32).astype(jnp.int16))


def decode(packed, rows):
    whole = packed.astype(jnp.int32).astype(f32)
    scales = jnp.exp2(whole[rows : rows + GROUP] - 14.0)
    parts = [
        whole[first : first + GROUP] * scales[first // GROUP : first // GROUP + 1]
        for first in range(0, rows, GROUP)
    ]
    return jnp.concatenate(parts, axis=0)


def encode_to(ref, index, value):
    def store(first, data):
        ref[index, first : first + GROUP, :] = data

    encode(value, store)


def picks_kernel(group_cols, info, sampled, acts, out_grad, picks, acts_buf, grad_buf, sems):
    group = info[0]
    block = 128
    span = grad_buf.shape[1]
    tokens, cols = acts.shape
    last = out_grad.shape[1] // block - span // block
    start = jnp.minimum((group * group_cols) // block, last)
    first = pltpu.make_async_copy(acts, acts_buf, sems.at[0])
    second = pltpu.make_async_copy(
        out_grad.at[:, pl.ds(pl.multiple_of(start * block, block), span)], grad_buf, sems.at[1]
    )
    first.start()
    second.start()
    place = lax.broadcasted_iota(jnp.int32, (sampled.shape[0], tokens), 1)
    chosen = (place == sampled[...]).astype(bf16)
    first.wait()
    picks[:, :cols] = jnp.dot(chosen, acts_buf[...], preferred_element_type=f32).astype(bf16)
    second.wait()
    grads = jnp.dot(chosen, grad_buf[...], preferred_element_type=f32)
    pad = jnp.zeros((grads.shape[0], picks.shape[1] - cols - group_cols), f32)
    for which in range(4):
        begin = min((which * group_cols) // block, last) * block
        offset = which * group_cols - begin

        @pl.when(group == which)
        def _():
            part = jnp.concatenate([grads[:, offset : offset + group_cols], pad], axis=1)
            picks[:, cols:] = part.astype(bf16)


def split_units(group, head, width_g):
    half = group.shape[1] // 2
    mid = width_g // 2
    middle = group[head : head + width_g]
    packed = [
        jnp.concatenate([middle[:mid, cols], middle[mid:, cols]], axis=1)
        for cols in (slice(0, half), slice(half, 2 * half))
    ]
    return (
        jnp.concatenate([group[:head], packed[0]], axis=0),
        jnp.concatenate([group[head + width_g :], packed[1]], axis=0),
    )


def partial_kernel_x(group_cols, width_g, info, out_grad, acts, send, keep, turned, raw):
    step = pl.program_id(0)
    side = info[1]
    head = 2 * width_g
    block = out_grad.shape[1]
    flipped = out_grad[...].T
    turned[...] = flipped
    first = pl.multiple_of(step * block, block)
    raw[pl.ds(first, block), :] = jnp.dot(flipped, acts[...], preferred_element_type=f32)

    @pl.when(step > 0)
    def _():
        place = step - 1
        start = pl.multiple_of(place * group_cols, 8)
        units = split_units(raw[pl.ds(start, group_cols), :], head, width_g)
        for x in range(2):

            @pl.when(side == x)
            def _():
                keep[place] = units[x]
                encode_to(send, place, units[1 - x])


def partial_kernel_l(width_g, info, turned, acts, send, keep):
    place = pl.program_id(0)
    low = info[2]
    raw = jnp.dot(turned[...], acts[...], preferred_element_type=f32)
    units = split_units(raw, 2 * width_g, width_g)
    high = place // 2

    @pl.when(place % 2 == low)
    def _():
        for x in range(2):
            keep[2 * high + x] = units[x]

    @pl.when(place % 2 != low)
    def _():
        for x in range(2):
            encode_to(send, 2 * high + x, units[x])


def add_kernel(bit_at, inner, info, got, held, send, keep):
    bit = info[bit_at]
    rows = held.shape[1]
    count = send.shape[0]

    def place(j, value):
        return 2 * j + value if inner else value * count + j

    for j in range(count):
        away = place(j, 1 - bit)
        encode_to(send, j, held[away] + decode(got[away], rows))
    for j in range(count):
        home = place(j, bit)
        keep[j] = held[home] + decode(got[home], rows)


def add_step(info, bit_at, inner, got, held):
    count = held.shape[0] // 2
    return pl.pallas_call(
        lambda *refs: add_kernel(bit_at, inner, *refs),
        in_specs=[smem, vmem, vmem],
        out_specs=[vmem, vmem],
        out_shape=[
            shaped((count,) + got.shape[1:], jnp.int16),
            shaped((count,) + held.shape[1:], f32),
        ],
        compiler_params=params(24),
        name="add",
    )(info, got, held)


def factor_kernel(
    share, info, own, one, two, four, a_state, g_state, a_new, g_new, inv_a, needed, picks, inv_g
):
    shard = info[3]
    picks[shard] = own[...]
    picks[shard ^ 4] = one[...]
    for j in range(2):
        picks[shard ^ 2 ^ (4 * j)] = two[j]
    for j in range(4):
        picks[shard ^ 1 ^ (4 * (j % 2)) ^ (2 * (j // 2))] = four[j]
    count_a, width_a = a_state.shape[0], a_state.shape[1]
    count_g, width_g = g_state.shape[0], g_state.shape[1]
    samples = picks.shape[0] * picks.shape[1]
    everything = picks[...].reshape(samples, picks.shape[2])
    errors, inverses, scales = [], [], []
    for index in range(count_a + count_g):
        is_a = index < count_a
        width = width_a if is_a else width_g
        place = index if is_a else index - count_a
        start = place * width_a if is_a else count_a * width_a + place * width_g
        rows = everything[:, start : start + width]
        stats = lax.dot_general(
            rows, rows, (((0,), (0,)), ((), ())), preferred_element_type=f32
        )
        slot = info[4 + index]
        stored = (a_state if is_a else g_state)[slot]
        factor = factor_decay * stored + share * stats
        (a_new if is_a else g_new)[slot] = factor
        row = lax.broadcasted_iota(jnp.int32, (width, width), 0)
        col = lax.broadcasted_iota(jnp.int32, (width, width), 1)
        identity = (row == col).astype(f32)
        trace = jnp.sum(factor * identity) / width
        damped = factor + (damping_rate * trace) * identity
        bound = jnp.max(jnp.sum(jnp.abs(damped), axis=0))
        error = identity - damped / bound
        errors.append(error)
        inverses.append(identity + error)
        scales.append(bound)
    blocks = range(count_a + count_g)
    dot = lambda p, q: jnp.dot(p, q, preferred_element_type=f32, precision=highest)
    errors = [dot(errors[i], errors[i]) for i in blocks]
    for step in range(1, NS_IT - 1):
        grown = [dot(inverses[i], errors[i]) for i in blocks]
        squares = [dot(errors[i], errors[i]) for i in blocks]
        inverses = [inverses[i] + grown[i] for i in blocks]
        errors = squares
    inverses = [(inverses[i] + dot(inverses[i], errors[i])) / scales[i] for i in blocks]
    for index in blocks:
        if index < count_a:
            inv_a[index] = inverses[index]
        else:
            inv_g[index - count_a] = inverses[index]
    side = info[1]
    needed[0] = inv_g[3 * side]
    needed[1] = inv_g[1 + 3 * side]
    needed[2] = inv_g[2]


def precon_kernel(info, got_a, held_a, got_b, held_b, inv_g, inv_a, top, mid, total):
    side = info[1]
    width_g, width_a = inv_g.shape[-1], inv_a.shape[-1]
    half = width_g // 2
    dot = lambda p, q: jnp.dot(p, q, preferred_element_type=f32, precision=highest)
    squares = jnp.zeros((width_g, width_a), f32)
    for piece, (got, held) in enumerate(((got_a, held_a), (got_b, held_b))):
        part = held[0] + decode(got[0], held.shape[1])
        for place in range(2):
            for block in range(2):
                values = dot(
                    inv_g[place],
                    part[
                        place * width_g : (place + 1) * width_g,
                        block * width_a : (block + 1) * width_a,
                    ],
                )
                values = dot(values, inv_a[2 * piece + block])
                squares += values * values
                column = (2 * piece + block) * width_a
                top[place * width_g : (place + 1) * width_g, column : column + width_a] = values
        packed = part[2 * width_g : 2 * width_g + half, :]
        values = jnp.concatenate([packed[:, :width_a], packed[:, width_a:]], axis=0)
        values = dot(dot(inv_g[2], values), inv_a[2 * piece + side])
        squares += values * values
        mid[:, piece * width_a : (piece + 1) * width_a] = values
    total[...] = jnp.full(total.shape, jnp.sum(squares), f32)


def fast(acts, out_grad, sample_rows, own_a, own_g, a_state, g_state, momentum, weight):
    shard_pos = lax.axis_index("shard")
    tensor_pos = lax.axis_index("tensor")
    side, low, high = shard_pos & 1, (shard_pos >> 1) & 1, shard_pos >> 2
    count_a, width_a = a_state.shape[1], a_state.shape[2]
    count_g, width_g = g_state.shape[1], g_state.shape[2]
    group_cols = count_g * width_g
    tokens, cols = acts.shape
    outs = out_grad.shape[1]
    rows = momentum.shape[0]
    drawn = sample_rows.shape[0]
    samples = drawn * 8
    share = (1.0 - factor_decay) / samples
    half = cols // 2
    head = 2 * width_g
    mid = width_g // 2
    row_a = lax.dynamic_index_in_dim(own_a, tensor_pos, 0, keepdims=False)
    row_g = lax.dynamic_index_in_dim(own_g, tensor_pos, 0, keepdims=False)
    info = jnp.concatenate(
        [jnp.stack([tensor_pos, side, low, shard_pos]), row_a, row_g, high.reshape(1)]
    )
    high_at = 4 + count_a + count_g

    wide = cols + -(-group_cols // 128) * 128
    picks = pl.pallas_call(
        lambda *refs: picks_kernel(group_cols, *refs),
        in_specs=[smem, vmem, anywhere, anywhere],
        out_specs=vmem,
        out_shape=shaped((drawn, wide), bf16),
        scratch_shapes=[
            pltpu.VMEM((tokens, cols), bf16),
            pltpu.VMEM((tokens, 640), bf16),
            pltpu.SemaphoreType.DMA((2,)),
        ],
        compiler_params=params(24),
        name="picks",
    )(info, sample_rows.reshape(-1, 1), acts, out_grad)
    one = swap(picks, 4)
    two = swap(jnp.stack([picks, one]), 2)
    four = swap(jnp.concatenate([picks[None], one[None], two]), 1)

    block = outs // 5
    send_a, keep_a, turned = pl.pallas_call(
        lambda *refs: partial_kernel_x(group_cols, width_g, *refs),
        grid=(5,),
        in_specs=[
            smem,
            pl.BlockSpec((tokens, block), lambda i: (0, i)),
            pl.BlockSpec((tokens, half), lambda i: (0, 0)),
        ],
        out_specs=[
            pl.BlockSpec((4, rows + GROUP, half), lambda i: (0, 0, 0)),
            pl.BlockSpec((4, rows, half), lambda i: (0, 0, 0)),
            pl.BlockSpec((block, tokens), lambda i: (i, 0)),
        ],
        out_shape=[
            shaped((4, rows + GROUP, half), jnp.int16),
            shaped((4, rows, half), f32),
            shaped((outs, tokens), bf16),
        ],
        scratch_shapes=[pltpu.VMEM((outs, half), f32)],
        compiler_params=params(40),
        name="partial_x",
    )(info, out_grad, acts)
    got_a = swap(send_a, 1)
    send_b, keep_b = pl.pallas_call(
        lambda *refs: partial_kernel_l(width_g, *refs),
        grid=(4,),
        in_specs=[
            smem,
            pl.BlockSpec((group_cols, tokens), lambda i: (i, 0)),
            pl.BlockSpec((tokens, half), lambda i: (0, 1)),
        ],
        out_specs=[
            pl.BlockSpec((4, rows + GROUP, half), lambda i: (0, 0, 0)),
            pl.BlockSpec((4, rows, half), lambda i: (0, 0, 0)),
        ],
        out_shape=[
            shaped((4, rows + GROUP, half), jnp.int16),
            shaped((4, rows, half), f32),
        ],
        compiler_params=params(40),
        name="partial_l",
    )(info, turned, acts)
    got_b = swap(send_b, 2)
    send_a, keep_a = add_step(info, 2, True, got_a, keep_a)
    got_a = swap(send_a, 2)
    send_b, keep_b = add_step(info, 1, True, got_b, keep_b)
    got_b = swap(send_b, 1)
    send_a, keep_a = add_step(info, high_at, True, got_a, keep_a)
    got_a = swap(send_a, 4)
    send_b, keep_b = add_step(info, high_at, True, got_b, keep_b)
    got_b = swap(send_b, 4)

    new_a, new_g, inv_a, needed = pl.pallas_call(
        lambda *refs: factor_kernel(share, *refs),
        in_specs=[smem] + [vmem] * 6,
        out_specs=[vmem] * 4,
        out_shape=[
            shaped(a_state.shape[1:], f32),
            shaped(g_state.shape[1:], f32),
            shaped(a_state.shape[1:], f32),
            shaped((3, width_g, width_g), f32),
        ],
        scratch_shapes=[
            pltpu.VMEM((8, drawn, wide), bf16),
            pltpu.VMEM(g_state.shape[1:], f32),
        ],
        compiler_params=params(24),
        name="factors",
    )(info, picks, one, two, four, a_state[0], g_state[0])
    route = [
        ((2 * a + b) * 4 + c, (2 * c + b) * 4 + a)
        for a in range(4)
        for b in range(2)
        for c in range(4)
    ]
    inv_rows = lax.ppermute(needed, ("shard", "tensor"), route)

    top, middle, total = pl.pallas_call(
        precon_kernel,
        in_specs=[smem] + [vmem] * 6,
        out_specs=[vmem] * 3,
        out_shape=[
            shaped((head, cols), f32),
            shaped((width_g, half), f32),
            shaped((8, half), f32),
        ],
        compiler_params=params(24),
        name="precon",
    )(info, got_a, keep_a, got_b, keep_b, inv_rows, inv_a)

    total = total + swap_t(total, 1)
    total = total + swap_t(total, 2)
    own_mid = pick(side, middle[:mid], middle[mid:])
    give = pick(side, middle[mid:], middle[:mid])
    got = swap(jnp.concatenate([give, total], axis=0), 1)
    total = total + got[mid:]
    total = total + swap(total, 2)
    total = total + swap(total, 4)
    mean_sq = total[0, 0] / (rows * 8 * cols * 4)
    other_mid = got[:mid]
    quarter = half // 2
    pairs = []
    for piece in range(2):
        span = slice(piece * quarter, (piece + 1) * quarter)
        pairs += [
            pick(side, own_mid[:, span], other_mid[:, span]),
            pick(side, other_mid[:, span], own_mid[:, span]),
        ]
    middle_rows = jnp.concatenate(pairs, axis=1)
    precon = pick(
        side,
        jnp.concatenate([top, middle_rows], axis=0),
        jnp.concatenate([middle_rows, top], axis=0),
    )
    update = precon / jnp.sqrt(mean_sq + epsilon_sq)
    momentum_new = momentum_rate * momentum + update + decay_rate * weight
    weight_new = weight - learn_rate * momentum_new
    rounded = weight_new.astype(bf16)

    def spread(values, bit, flag, axis):
        other = swap(values, bit)
        return jnp.stack([pick(flag, values, other), pick(flag, other, values)], axis=axis)

    piece = rounded[:, :half]
    piece = spread(piece, 4, high, 0)
    piece = spread(piece, 2, low, 1)
    whole_a = spread(piece, 1, side, 2).reshape(-1, half)
    piece = rounded[:, half:]
    piece = spread(piece, 1, side, 0)
    piece = spread(piece, 4, high, 0)
    whole_b = spread(piece, 2, low, 1).reshape(-1, half)
    gathered = jnp.concatenate([whole_a, whole_b], axis=1)
    return (new_a[None], new_g[None], momentum_new, weight_new, gathered)


def local(acts, out_grad, sample_rows, own_a, own_g, a_state, g_state, momentum, weight):
    shapes_fit = (
        lax.axis_size("shard") == 8
        and lax.axis_size("tensor") == 4
        and a_state.shape[1:] == (4, 128, 128)
        and g_state.shape[1:] == (5, 96, 96)
    )
    plan = fast if shapes_fit else general
    return plan(acts, out_grad, sample_rows, own_a, own_g, a_state, g_state, momentum, weight)


def solution(mesh):
    return jax.shard_map(
        local,
        mesh=mesh,
        in_specs=(
            P("shard", "tensor"),
            P("shard", None),
            P("shard"),
            P(),
            P(),
            P("tensor", None, None, None),
            P("tensor", None, None, None),
            P("shard", "tensor"),
            P("shard", "tensor"),
        ),
        out_specs=(
            P("tensor", None, None, None),
            P("tensor", None, None, None),
            P("shard", "tensor"),
            P("shard", "tensor"),
            P(None, "tensor"),
        ),
        check_vma=False,
    )
```

```python
import jax
import jax.numpy as jnp
from jax import lax
from jax.experimental import pallas as pl
from jax.experimental.pallas import tpu as pltpu
from jax.sharding import PartitionSpec as P

NS_IT = 5


factor_decay = 0.8
damping_rate = 0.03
momentum_rate = 0.9
decay_rate = 0.01
learn_rate = 0.05
epsilon_sq = 1e-06
highest = lax.Precision.HIGHEST
f32 = jnp.float32
bf16 = jnp.bfloat16


def newton_inverse(factor):
    width = factor.shape[-1]
    identity = jnp.eye(width, dtype=jnp.float32)
    trace_mean = jnp.trace(factor, axis1=-2, axis2=-1) / width
    damped = factor + damping_rate * trace_mean[:, None, None] * identity
    bound = jnp.max(jnp.sum(jnp.abs(damped), axis=-1), axis=-1)
    guess = identity[None] / bound[:, None, None]
    for iteration in range(NS_IT):
        product = jnp.einsum("bij,bjk->bik", damped, guess, precision=highest)
        guess = jnp.einsum("bij,bjk->bik", guess, 2.0 * identity - product, precision=highest)
    return guess


def local_stats(rows, width):
    blocks = rows.reshape(rows.shape[0], -1, width)
    return jnp.einsum("sbi,sbj->bij", blocks, blocks, preferred_element_type=jnp.float32)


def owner_part(slots, shard_pos, shard_count):
    count = slots.shape[0]
    stride = shard_count // count
    slot_pos = jnp.minimum(shard_pos // stride, count - 1)
    mine = lax.dynamic_index_in_dim(slots, slot_pos, 0, keepdims=True)
    inverse = newton_inverse(mine)
    marker = (jnp.arange(count, dtype=jnp.int32) * stride == shard_pos).astype(jnp.float32)
    return marker[:, None, None] * inverse


def general(acts, out_grad, sample_rows, own_a, own_g, a_state, g_state, momentum, weight):
    shard_count = lax.axis_size("shard")
    tensor_count = lax.axis_size("tensor")
    shard_pos = lax.axis_index("shard")
    tensor_pos = lax.axis_index("tensor")
    block_a = a_state.shape[-1]
    block_g = g_state.shape[-1]
    samples = sample_rows.shape[0] * shard_count
    fresh_share = (1.0 - factor_decay) / samples
    picked_a = jnp.take(acts, sample_rows, axis=0)
    picked_g = jnp.take(out_grad, sample_rows, axis=0)
    group_cols = out_grad.shape[1] // tensor_count
    picked_g = lax.dynamic_slice_in_dim(picked_g, tensor_pos * group_cols, group_cols, 1)
    stats_a = local_stats(picked_a, block_a)
    stats_g = local_stats(picked_g, block_g)
    row_a = lax.dynamic_index_in_dim(own_a, tensor_pos, 0, keepdims=False)
    row_g = lax.dynamic_index_in_dim(own_g, tensor_pos, 0, keepdims=False)
    select_a = (row_a[None, :] == jnp.arange(row_a.shape[0], dtype=jnp.int32)[:, None]).astype(
        jnp.float32
    )
    select_g = (row_g[None, :] == jnp.arange(row_g.shape[0], dtype=jnp.int32)[:, None]).astype(
        jnp.float32
    )
    summed_a, summed_g = lax.psum((fresh_share * stats_a, fresh_share * stats_g), "shard")
    stored_a = jnp.einsum("sb,sij->bij", select_a, a_state[0], precision=highest)
    stored_g = jnp.einsum("sb,sij->bij", select_g, g_state[0], precision=highest)
    fac_a = factor_decay * stored_a + summed_a
    fac_g = factor_decay * stored_g + summed_g
    slots_a = jnp.einsum("sb,bij->sij", select_a, fac_a, precision=highest)
    slots_g = jnp.einsum("sb,bij->sij", select_g, fac_g, precision=highest)
    new_a_state = slots_a[None]
    new_g_state = slots_g[None]
    slot_inv_a, slot_inv_g = lax.psum(
        (owner_part(slots_a, shard_pos, shard_count), owner_part(slots_g, shard_pos, shard_count)),
        "shard",
    )
    inv_a = jnp.einsum("sb,sij->bij", select_a, slot_inv_a, precision=highest)
    local_inv_g = jnp.einsum("sb,sij->bij", select_g, slot_inv_g, precision=highest)
    inv_g = lax.all_gather(local_inv_g, "tensor", axis=0, tiled=True)
    raw_product = lax.dot_general(
        out_grad, acts, (((0,), (0,)), ((), ())), preferred_element_type=jnp.float32
    )
    left_done = jnp.einsum(
        "bij,bjd->bid", inv_g, raw_product.reshape(inv_g.shape[0], block_g, -1), precision=highest
    ).reshape(raw_product.shape)
    owned_rows = lax.psum_scatter(left_done, "shard", scatter_dimension=0, tiled=True)
    precon = jnp.einsum(
        "qbi,bij->qbj",
        owned_rows.reshape(owned_rows.shape[0], -1, block_a),
        inv_a,
        precision=highest,
    ).reshape(owned_rows.shape)
    square_total = lax.psum(jnp.sum(precon * precon), ("shard", "tensor"))
    mean_sq = square_total / (momentum.shape[0] * shard_count * momentum.shape[1] * tensor_count)
    update = precon / jnp.sqrt(mean_sq + epsilon_sq)
    momentum_new = momentum_rate * momentum + update + decay_rate * weight
    weight_new = weight - learn_rate * momentum_new
    gathered = lax.all_gather(weight_new.astype(jnp.bfloat16), "shard", axis=0, tiled=True)
    return (new_a_state, new_g_state, momentum_new, weight_new, gathered)


GROUP = 16
vmem = pl.BlockSpec(memory_space=pltpu.VMEM)
smem = pl.BlockSpec(memory_space=pltpu.SMEM)
main = pl.BlockSpec(memory_space=pl.ANY)


def params(mib):
    return pltpu.CompilerParams(vmem_limit_bytes=mib * 2**20)


def shaped(shape, kind):
    return jax.ShapeDtypeStruct(shape, kind)


def cost(flops, moved):
    return pl.CostEstimate(flops=flops, bytes_accessed=moved, transcendentals=0)


def swap(value, bit):
    return lax.ppermute(value, "shard", [(i, i ^ bit) for i in range(8)])


def swap_t(value, bit):
    return lax.ppermute(value, "tensor", [(i, i ^ bit) for i in range(4)])


def pick(flag, if_zero, if_one):
    return jnp.where(flag == 0, if_zero, if_one)


def encode(value, store):
    rows, width = value.shape
    powers = []
    for first in range(0, rows, GROUP):
        part = value[first : first + GROUP]
        top = jnp.max(jnp.abs(part), axis=0, keepdims=True)
        power = jnp.floor(jnp.log2(jnp.maximum(top, 1e-30)))
        scaled = jnp.clip(jnp.round(part * jnp.exp2(14.0 - power)), -32767.0, 32767.0)
        store(first, scaled.astype(jnp.int32).astype(jnp.int16))
        powers.append(power)
    powers += [jnp.zeros((1, width), f32)] * (GROUP - len(powers))
    store(rows, jnp.concatenate(powers, axis=0).astype(jnp.int32).astype(jnp.int16))


def decode(packed, rows):
    whole = packed.astype(jnp.int32).astype(f32)
    scales = jnp.exp2(whole[rows : rows + GROUP] - 14.0)
    parts = [
        whole[first : first + GROUP] * scales[first // GROUP : first // GROUP + 1]
        for first in range(0, rows, GROUP)
    ]
    return jnp.concatenate(parts, axis=0)


def encode_to(ref, index, value):
    def store(first, data):
        ref[index, first : first + GROUP, :] = data

    encode(value, store)


def picks_kernel(group_cols, info, sampled, acts, out_grad, picks, acts_buf, grad_buf, sems):
    group = info[0]
    block = 128
    span = grad_buf.shape[1]
    tokens, cols = acts.shape
    chunk = tokens // 4
    last = out_grad.shape[1] // block - span // block
    start = pl.multiple_of(jnp.minimum((group * group_cols) // block, last) * block, block)
    copies = []
    for part in range(4):
        some = pl.ds(part * chunk, chunk)
        copies.append(
            (
                pltpu.make_async_copy(acts.at[some, :], acts_buf.at[some, :], sems.at[part]),
                pltpu.make_async_copy(
                    out_grad.at[some, pl.ds(start, span)], grad_buf.at[some, :], sems.at[4 + part]
                ),
            )
        )
        for copy in copies[-1]:
            copy.start()
    drawn = sampled.shape[1]
    row = lax.broadcasted_iota(jnp.int32, (drawn, drawn), 0)
    col = lax.broadcasted_iota(jnp.int32, (drawn, drawn), 1)
    upright = jnp.sum(jnp.where(row == col, sampled[...], 0), axis=1, keepdims=True)
    found = jnp.zeros((drawn, cols), f32)
    grads = jnp.zeros((drawn, span), f32)
    for part in range(4):
        place = lax.broadcasted_iota(jnp.int32, (drawn, chunk), 1) + part * chunk
        chosen = (place == upright).astype(bf16)
        some = slice(part * chunk, (part + 1) * chunk)
        copies[part][0].wait()
        found += jnp.dot(chosen, acts_buf[some, :], preferred_element_type=f32)
        copies[part][1].wait()
        grads += jnp.dot(chosen, grad_buf[some, :], preferred_element_type=f32)
    picks[:, :cols] = found.astype(bf16)
    pad = jnp.zeros((drawn, picks.shape[1] - cols - group_cols), f32)
    for which in range(4):
        begin = min((which * group_cols) // block, last) * block
        offset = which * group_cols - begin

        @pl.when(group == which)
        def _():
            part = jnp.concatenate([grads[:, offset : offset + group_cols], pad], axis=1)
            picks[:, cols:] = part.astype(bf16)


def split_units(group, head, width_g):
    half = group.shape[1] // 2
    mid = width_g // 2
    middle = group[head : head + width_g]
    packed = [
        jnp.concatenate([middle[:mid, cols], middle[mid:, cols]], axis=1)
        for cols in (slice(0, half), slice(half, 2 * half))
    ]
    return (
        jnp.concatenate([group[:head], packed[0]], axis=0),
        jnp.concatenate([group[head + width_g :], packed[1]], axis=0),
    )


def partial_kernel(
    group_cols, width_g, info, out_grad, acts, send_a, keep_a, send_b, keep_b, grad_buf, acts_buf,
    raw, sems
):
    side, low = info[1], info[2]
    head = 2 * width_g
    outs = out_grad.shape[1]
    half = acts.shape[1] // 2
    block = outs // 5
    first = pltpu.make_async_copy(acts, acts_buf, sems.at[5])
    first.start()
    copies = []
    for step in range(5):
        columns = pl.ds(step * block, block)
        copies.append(
            pltpu.make_async_copy(out_grad.at[:, columns], grad_buf.at[:, columns], sems.at[step])
        )
        copies[-1].start()
    first.wait()
    for step in range(5):
        copies[step].wait()
        columns = slice(step * block, (step + 1) * block)
        raw[columns, :] = jnp.dot(
            grad_buf[:, columns].T, acts_buf[...], preferred_element_type=f32
        )
        if step > 0:
            place = step - 1
            span = slice(place * group_cols, (place + 1) * group_cols)
            units = split_units(raw[span, :half], head, width_g)
            for x in range(2):

                @pl.when(side == x)
                def _():
                    keep_a[place] = units[x]
                    encode_to(send_a, place, units[1 - x])

            units = split_units(raw[span, half:], head, width_g)
            high = place // 2

            @pl.when(place % 2 == low)
            def _():
                for x in range(2):
                    keep_b[2 * high + x] = units[x]

            @pl.when(place % 2 != low)
            def _():
                for x in range(2):
                    encode_to(send_b, 2 * high + x, units[x])


def add_kernel(bit_at, inner, info, got, held, send, keep):
    bit = info[bit_at]
    rows = held.shape[1]
    count = send.shape[0]

    def place(j, value):
        return 2 * j + value if inner else value * count + j

    for j in range(count):
        away = place(j, 1 - bit)
        encode_to(send, j, held[away] + decode(got[away], rows))
    for j in range(count):
        home = place(j, bit)
        keep[j] = held[home] + decode(got[home], rows)


def add_step(info, bit_at, inner, got, held):
    count = held.shape[0] // 2
    return pl.pallas_call(
        lambda *refs: add_kernel(bit_at, inner, *refs),
        in_specs=[smem, vmem, vmem],
        out_specs=[vmem, vmem],
        out_shape=[
            shaped((count,) + got.shape[1:], jnp.int16),
            shaped((count,) + held.shape[1:], f32),
        ],
        compiler_params=params(24),
        name="add",
    )(info, got, held)


def factor_kernel(
    share, info, own_a, own_g, own, one, two, four, a_state, g_state, a_new, g_new, inv_a, needed, picks, inv_g
):
    group, shard = info[0], info[3]
    picks[shard] = own[...]
    picks[shard ^ 4] = one[...]
    for j in range(2):
        picks[shard ^ 2 ^ (4 * j)] = two[j]
    for j in range(4):
        picks[shard ^ 1 ^ (4 * (j % 2)) ^ (2 * (j // 2))] = four[j]
    count_a, width_a = a_state.shape[0], a_state.shape[1]
    count_g, width_g = g_state.shape[0], g_state.shape[1]
    samples = picks.shape[0] * picks.shape[1]
    everything = picks[...].reshape(samples, picks.shape[2])
    errors, inverses, scales = [], [], []
    for index in range(count_a + count_g):
        is_a = index < count_a
        width = width_a if is_a else width_g
        place = index if is_a else index - count_a
        start = place * width_a if is_a else count_a * width_a + place * width_g
        rows = everything[:, start : start + width]
        stats = lax.dot_general(
            rows, rows, (((0,), (0,)), ((), ())), preferred_element_type=f32
        )
        slot = own_a[group, place] if is_a else own_g[group, place]
        stored = (a_state if is_a else g_state)[slot]
        factor = factor_decay * stored + share * stats
        (a_new if is_a else g_new)[slot] = factor
        row = lax.broadcasted_iota(jnp.int32, (width, width), 0)
        col = lax.broadcasted_iota(jnp.int32, (width, width), 1)
        identity = (row == col).astype(f32)
        trace = jnp.sum(factor * identity) / width
        damped = factor + (damping_rate * trace) * identity
        bound = jnp.max(jnp.sum(jnp.abs(damped), axis=0))
        error = identity - damped / bound
        errors.append(error)
        inverses.append(identity + error)
        scales.append(bound)
    blocks = range(count_a + count_g)
    dot = lambda p, q: jnp.dot(p, q, preferred_element_type=f32, precision=highest)
    errors = [dot(errors[i], errors[i]) for i in blocks]
    for step in range(1, NS_IT - 1):
        grown = [dot(inverses[i], errors[i]) for i in blocks]
        squares = [dot(errors[i], errors[i]) for i in blocks]
        inverses = [inverses[i] + grown[i] for i in blocks]
        errors = squares
    inverses = [(inverses[i] + dot(inverses[i], errors[i])) / scales[i] for i in blocks]
    for index in blocks:
        if index < count_a:
            inv_a[index] = inverses[index]
        else:
            inv_g[index - count_a] = inverses[index]
    side = info[1]
    needed[0] = inv_g[3 * side]
    needed[1] = inv_g[1 + 3 * side]
    needed[2] = inv_g[2]


def precon_kernel(info, got_a, held_a, got_b, held_b, inv_g, inv_a, top, mid, total):
    side = info[1]
    width_g, width_a = inv_g.shape[-1], inv_a.shape[-1]
    half = width_g // 2
    dot = lambda p, q: jnp.dot(p, q, preferred_element_type=f32, precision=highest)
    squares = jnp.zeros((width_g, width_a), f32)
    for piece, (got, held) in enumerate(((got_a, held_a), (got_b, held_b))):
        part = held[0] + decode(got[0], held.shape[1])
        for place in range(2):
            for block in range(2):
                values = dot(
                    inv_g[place],
                    part[
                        place * width_g : (place + 1) * width_g,
                        block * width_a : (block + 1) * width_a,
                    ],
                )
                values = dot(values, inv_a[2 * piece + block])
                squares += values * values
                column = (2 * piece + block) * width_a
                top[place * width_g : (place + 1) * width_g, column : column + width_a] = values
        packed = part[2 * width_g : 2 * width_g + half, :]
        values = jnp.concatenate([packed[:, :width_a], packed[:, width_a:]], axis=0)
        values = dot(dot(inv_g[2], values), inv_a[2 * piece + side])
        squares += values * values
        mid[:, piece * width_a : (piece + 1) * width_a] = values
    total[...] = jnp.full(total.shape, jnp.sum(squares), f32)


def update_kernel(
    entries, info, total, got_total, top, middle, got, momentum, weight, momentum_new, weight_new,
    rounded_a, rounded_b
):
    rows, cols = momentum.shape
    half = cols // 2
    quarter = half // 2
    head = top.shape[0]
    mid = rows - head
    mean_sq = (total[0:1, :] + got_total[0:1, :]) / entries
    factor = 1.0 / jnp.sqrt(mean_sq + epsilon_sq)
    factor = jnp.concatenate([factor, factor], axis=1)

    def step(place, precon):
        span = slice(place, place + precon.shape[0])
        moved = momentum_rate * momentum[span, :] + precon * factor + decay_rate * weight[span, :]
        fresh = weight[span, :] - learn_rate * moved
        momentum_new[span, :] = moved
        weight_new[span, :] = fresh
        rounded_a[span, :] = fresh[:, :half].astype(bf16)
        rounded_b[span, :] = fresh[:, half:].astype(bf16)

    for x in range(2):

        @pl.when(info[1] == x)
        def _():
            own = middle[mid * x : mid * (x + 1), :]
            pairs = []
            for piece in range(2):
                columns = slice(piece * quarter, (piece + 1) * quarter)
                both = [own[:, columns], got[:mid, columns]]
                pairs += both if x == 0 else both[::-1]
            step(head * (1 - x), jnp.concatenate(pairs, axis=1))
            step(mid * x, top[...])


def fast(acts, out_grad, sample_rows, own_a, own_g, a_state, g_state, momentum, weight):
    shard_pos = lax.axis_index("shard")
    tensor_pos = lax.axis_index("tensor")
    side, low, high = shard_pos & 1, (shard_pos >> 1) & 1, shard_pos >> 2
    count_a, width_a = a_state.shape[1], a_state.shape[2]
    count_g, width_g = g_state.shape[1], g_state.shape[2]
    group_cols = count_g * width_g
    tokens, cols = acts.shape
    outs = out_grad.shape[1]
    rows = momentum.shape[0]
    drawn = sample_rows.shape[0]
    samples = drawn * 8
    share = (1.0 - factor_decay) / samples
    half = cols // 2
    head = 2 * width_g
    mid = width_g // 2
    info = jnp.stack([tensor_pos, side, low, shard_pos, high])
    high_at = 4

    wide = cols + -(-group_cols // 128) * 128
    picks = pl.pallas_call(
        lambda *refs: picks_kernel(group_cols, *refs),
        in_specs=[smem, vmem, main, main],
        out_specs=vmem,
        out_shape=shaped((drawn, wide), bf16),
        scratch_shapes=[
            pltpu.VMEM((tokens, cols), bf16),
            pltpu.VMEM((tokens, 640), bf16),
            pltpu.SemaphoreType.DMA((8,)),
        ],
        compiler_params=params(60),
        cost_estimate=cost(2 * drawn * tokens * (cols + 640), 5 * 2**20),
        name="picks",
    )(info, sample_rows.reshape(1, -1), acts, out_grad)
    one = swap(picks, 4)

    send_a, keep_a, send_b, keep_b = pl.pallas_call(
        lambda *refs: partial_kernel(group_cols, width_g, *refs),
        in_specs=[smem, main, main],
        out_specs=[vmem] * 4,
        out_shape=[
            shaped((4, rows + GROUP, half), jnp.int16),
            shaped((4, rows, half), f32),
        ]
        * 2,
        scratch_shapes=[
            pltpu.VMEM((tokens, outs), bf16),
            pltpu.VMEM((tokens, cols), bf16),
            pltpu.VMEM((outs, cols), f32),
            pltpu.SemaphoreType.DMA((6,)),
        ],
        compiler_params=params(60),
        cost_estimate=cost(2 * outs * tokens * cols, 10 * 2**20),
        name="partial",
    )(info, out_grad, acts)
    one, send_a, send_b = lax.optimization_barrier((one, send_a, send_b))
    got_a = swap(send_a, 1)
    got_b = swap(send_b, 2)
    two = swap(jnp.stack([picks, one]), 2)
    four = swap(jnp.concatenate([picks[None], one[None], two]), 1)
    send_a, keep_a = add_step(info, 2, True, got_a, keep_a)
    got_a = swap(send_a, 2)
    send_b, keep_b = add_step(info, 1, True, got_b, keep_b)
    got_b = swap(send_b, 1)
    send_a, keep_a = add_step(info, high_at, True, got_a, keep_a)
    got_a = swap(send_a, 4)
    send_b, keep_b = add_step(info, high_at, True, got_b, keep_b)
    got_b = swap(send_b, 4)

    new_a, new_g, inv_a, needed = pl.pallas_call(
        lambda *refs: factor_kernel(share, *refs),
        in_specs=[smem] * 3 + [vmem] * 6,
        out_specs=[vmem] * 4,
        out_shape=[
            shaped(a_state.shape[1:], f32),
            shaped(g_state.shape[1:], f32),
            shaped(a_state.shape[1:], f32),
            shaped((3, width_g, width_g), f32),
        ],
        scratch_shapes=[
            pltpu.VMEM((8, drawn, wide), bf16),
            pltpu.VMEM(g_state.shape[1:], f32),
        ],
        compiler_params=params(24),
        name="factors",
    )(info, own_a, own_g, picks, one, two, four, a_state[0], g_state[0])
    route = [
        ((2 * a + b) * 4 + c, (2 * c + b) * 4 + a)
        for a in range(4)
        for b in range(2)
        for c in range(4)
    ]
    inv_rows = lax.ppermute(needed, ("shard", "tensor"), route)

    top, middle, total = pl.pallas_call(
        precon_kernel,
        in_specs=[smem] + [vmem] * 6,
        out_specs=[vmem] * 3,
        out_shape=[
            shaped((head, cols), f32),
            shaped((width_g, half), f32),
            shaped((8, half), f32),
        ],
        compiler_params=params(24),
        name="precon",
    )(info, got_a, keep_a, got_b, keep_b, inv_rows, inv_a)

    total = total + swap_t(total, 1)
    total = total + swap_t(total, 2)
    give = pick(side, middle[mid:], middle[:mid])
    got = swap(jnp.concatenate([give, total], axis=0), 1)
    total = total + got[mid:]
    total = total + swap(total, 2)
    momentum_new, weight_new, rounded_a, rounded_b = pl.pallas_call(
        lambda *refs: update_kernel(rows * 8 * cols * 4, *refs),
        in_specs=[smem] + [vmem] * 7,
        out_specs=[vmem] * 4,
        out_shape=[
            shaped((rows, cols), f32),
            shaped((rows, cols), f32),
            shaped((rows, half), bf16),
            shaped((rows, half), bf16),
        ],
        compiler_params=params(24),
        name="update",
    )(info, total, swap(total, 4), top, middle, got, momentum, weight)

    def spread(values, bit, flag, axis):
        other = swap(values, bit)
        return jnp.stack([pick(flag, values, other), pick(flag, other, values)], axis=axis)

    piece = rounded_a
    piece = spread(piece, 4, high, 0)
    piece = spread(piece, 2, low, 1)
    whole_a = spread(piece, 1, side, 2).reshape(-1, half)
    piece = rounded_b
    piece = spread(piece, 1, side, 0)
    piece = spread(piece, 4, high, 0)
    whole_b = spread(piece, 2, low, 1).reshape(-1, half)
    gathered = jnp.concatenate([whole_a, whole_b], axis=1)
    return (new_a[None], new_g[None], momentum_new, weight_new, gathered)


def local(acts, out_grad, sample_rows, own_a, own_g, a_state, g_state, momentum, weight):
    shapes_fit = (
        lax.axis_size("shard") == 8
        and lax.axis_size("tensor") == 4
        and a_state.shape[1:] == (4, 128, 128)
        and g_state.shape[1:] == (5, 96, 96)
    )
    plan = fast if shapes_fit else general
    return plan(acts, out_grad, sample_rows, own_a, own_g, a_state, g_state, momentum, weight)


def solution(mesh):
    return jax.shard_map(
        local,
        mesh=mesh,
        in_specs=(
            P("shard", "tensor"),
            P("shard", None),
            P("shard"),
            P(),
            P(),
            P("tensor", None, None, None),
            P("tensor", None, None, None),
            P("shard", "tensor"),
            P("shard", "tensor"),
        ),
        out_specs=(
            P("tensor", None, None, None),
            P("tensor", None, None, None),
            P("shard", "tensor"),
            P("shard", "tensor"),
            P(None, "tensor"),
        ),
        check_vma=False,
    )
```

```python
import jax
import jax.numpy as jnp
from jax import lax
from jax.experimental import pallas as pl
from jax.experimental.pallas import tpu as pltpu
from jax.sharding import PartitionSpec as P

NS_IT = 5


factor_decay = 0.8
damping_rate = 0.03
momentum_rate = 0.9
decay_rate = 0.01
learn_rate = 0.05
epsilon_sq = 1e-06
highest = lax.Precision.HIGHEST
f32 = jnp.float32
bf16 = jnp.bfloat16


def newton_inverse(factor):
    width = factor.shape[-1]
    identity = jnp.eye(width, dtype=jnp.float32)
    trace_mean = jnp.trace(factor, axis1=-2, axis2=-1) / width
    damped = factor + damping_rate * trace_mean[:, None, None] * identity
    bound = jnp.max(jnp.sum(jnp.abs(damped), axis=-1), axis=-1)
    guess = identity[None] / bound[:, None, None]
    for iteration in range(NS_IT):
        product = jnp.einsum("bij,bjk->bik", damped, guess, precision=highest)
        guess = jnp.einsum("bij,bjk->bik", guess, 2.0 * identity - product, precision=highest)
    return guess


def local_stats(rows, width):
    blocks = rows.reshape(rows.shape[0], -1, width)
    return jnp.einsum("sbi,sbj->bij", blocks, blocks, preferred_element_type=jnp.float32)


def owner_part(slots, shard_pos, shard_count):
    count = slots.shape[0]
    stride = shard_count // count
    slot_pos = jnp.minimum(shard_pos // stride, count - 1)
    mine = lax.dynamic_index_in_dim(slots, slot_pos, 0, keepdims=True)
    inverse = newton_inverse(mine)
    marker = (jnp.arange(count, dtype=jnp.int32) * stride == shard_pos).astype(jnp.float32)
    return marker[:, None, None] * inverse


def general(acts, out_grad, sample_rows, own_a, own_g, a_state, g_state, momentum, weight):
    shard_count = lax.axis_size("shard")
    tensor_count = lax.axis_size("tensor")
    shard_pos = lax.axis_index("shard")
    tensor_pos = lax.axis_index("tensor")
    block_a = a_state.shape[-1]
    block_g = g_state.shape[-1]
    samples = sample_rows.shape[0] * shard_count
    fresh_share = (1.0 - factor_decay) / samples
    picked_a = jnp.take(acts, sample_rows, axis=0)
    picked_g = jnp.take(out_grad, sample_rows, axis=0)
    group_cols = out_grad.shape[1] // tensor_count
    picked_g = lax.dynamic_slice_in_dim(picked_g, tensor_pos * group_cols, group_cols, 1)
    stats_a = local_stats(picked_a, block_a)
    stats_g = local_stats(picked_g, block_g)
    row_a = lax.dynamic_index_in_dim(own_a, tensor_pos, 0, keepdims=False)
    row_g = lax.dynamic_index_in_dim(own_g, tensor_pos, 0, keepdims=False)
    select_a = (row_a[None, :] == jnp.arange(row_a.shape[0], dtype=jnp.int32)[:, None]).astype(
        jnp.float32
    )
    select_g = (row_g[None, :] == jnp.arange(row_g.shape[0], dtype=jnp.int32)[:, None]).astype(
        jnp.float32
    )
    summed_a, summed_g = lax.psum((fresh_share * stats_a, fresh_share * stats_g), "shard")
    stored_a = jnp.einsum("sb,sij->bij", select_a, a_state[0], precision=highest)
    stored_g = jnp.einsum("sb,sij->bij", select_g, g_state[0], precision=highest)
    fac_a = factor_decay * stored_a + summed_a
    fac_g = factor_decay * stored_g + summed_g
    slots_a = jnp.einsum("sb,bij->sij", select_a, fac_a, precision=highest)
    slots_g = jnp.einsum("sb,bij->sij", select_g, fac_g, precision=highest)
    new_a_state = slots_a[None]
    new_g_state = slots_g[None]
    slot_inv_a, slot_inv_g = lax.psum(
        (owner_part(slots_a, shard_pos, shard_count), owner_part(slots_g, shard_pos, shard_count)),
        "shard",
    )
    inv_a = jnp.einsum("sb,sij->bij", select_a, slot_inv_a, precision=highest)
    local_inv_g = jnp.einsum("sb,sij->bij", select_g, slot_inv_g, precision=highest)
    inv_g = lax.all_gather(local_inv_g, "tensor", axis=0, tiled=True)
    raw_product = lax.dot_general(
        out_grad, acts, (((0,), (0,)), ((), ())), preferred_element_type=jnp.float32
    )
    left_done = jnp.einsum(
        "bij,bjd->bid", inv_g, raw_product.reshape(inv_g.shape[0], block_g, -1), precision=highest
    ).reshape(raw_product.shape)
    owned_rows = lax.psum_scatter(left_done, "shard", scatter_dimension=0, tiled=True)
    precon = jnp.einsum(
        "qbi,bij->qbj",
        owned_rows.reshape(owned_rows.shape[0], -1, block_a),
        inv_a,
        precision=highest,
    ).reshape(owned_rows.shape)
    square_total = lax.psum(jnp.sum(precon * precon), ("shard", "tensor"))
    mean_sq = square_total / (momentum.shape[0] * shard_count * momentum.shape[1] * tensor_count)
    update = precon / jnp.sqrt(mean_sq + epsilon_sq)
    momentum_new = momentum_rate * momentum + update + decay_rate * weight
    weight_new = weight - learn_rate * momentum_new
    gathered = lax.all_gather(weight_new.astype(jnp.bfloat16), "shard", axis=0, tiled=True)
    return (new_a_state, new_g_state, momentum_new, weight_new, gathered)


GROUP = 16
vmem = pl.BlockSpec(memory_space=pltpu.VMEM)
smem = pl.BlockSpec(memory_space=pltpu.SMEM)
main = pl.BlockSpec(memory_space=pl.ANY)


def params(mib):
    return pltpu.CompilerParams(vmem_limit_bytes=mib * 2**20)


def shaped(shape, kind):
    return jax.ShapeDtypeStruct(shape, kind)


def cost(flops, moved):
    return pl.CostEstimate(flops=flops, bytes_accessed=moved, transcendentals=0)


def swap(value, bit):
    return lax.ppermute(value, "shard", [(i, i ^ bit) for i in range(8)])


def swap_t(value, bit):
    return lax.ppermute(value, "tensor", [(i, i ^ bit) for i in range(4)])


def pick(flag, if_zero, if_one):
    return jnp.where(flag == 0, if_zero, if_one)


def encode(value, store):
    rows, width = value.shape
    powers = []
    for first in range(0, rows, GROUP):
        part = value[first : first + GROUP]
        top = jnp.max(jnp.abs(part), axis=0, keepdims=True)
        power = jnp.floor(jnp.log2(jnp.maximum(top, 1e-30)))
        scaled = jnp.clip(jnp.round(part * jnp.exp2(14.0 - power)), -32767.0, 32767.0)
        store(first, scaled.astype(jnp.int32).astype(jnp.int16))
        powers.append(power)
    powers += [jnp.zeros((1, width), f32)] * (GROUP - len(powers))
    store(rows, jnp.concatenate(powers, axis=0).astype(jnp.int32).astype(jnp.int16))


def decode(packed, rows):
    whole = packed.astype(jnp.int32).astype(f32)
    scales = jnp.exp2(whole[rows : rows + GROUP] - 14.0)
    parts = [
        whole[first : first + GROUP] * scales[first // GROUP : first // GROUP + 1]
        for first in range(0, rows, GROUP)
    ]
    return jnp.concatenate(parts, axis=0)


def encode_to(ref, index, value):
    def store(first, data):
        ref[index, first : first + GROUP, :] = data

    encode(value, store)


def picks_kernel(group_cols, info, sampled, acts, out_grad, picks, acts_buf, grad_buf, sems):
    group = info[0]
    block = 128
    span = grad_buf.shape[1]
    tokens, cols = acts.shape
    chunk = tokens // 4
    last = out_grad.shape[1] // block - span // block
    start = pl.multiple_of(jnp.minimum((group * group_cols) // block, last) * block, block)
    copies = []
    for part in range(4):
        some = pl.ds(part * chunk, chunk)
        copies.append(
            (
                pltpu.make_async_copy(acts.at[some, :], acts_buf.at[some, :], sems.at[part]),
                pltpu.make_async_copy(
                    out_grad.at[some, pl.ds(start, span)], grad_buf.at[some, :], sems.at[4 + part]
                ),
            )
        )
        for copy in copies[-1]:
            copy.start()
    drawn = sampled.shape[1]
    row = lax.broadcasted_iota(jnp.int32, (drawn, drawn), 0)
    col = lax.broadcasted_iota(jnp.int32, (drawn, drawn), 1)
    upright = jnp.sum(jnp.where(row == col, sampled[...], 0), axis=1, keepdims=True)
    found = jnp.zeros((drawn, cols), f32)
    grads = jnp.zeros((drawn, span), f32)
    for part in range(4):
        place = lax.broadcasted_iota(jnp.int32, (drawn, chunk), 1) + part * chunk
        chosen = (place == upright).astype(bf16)
        some = slice(part * chunk, (part + 1) * chunk)
        copies[part][0].wait()
        found += jnp.dot(chosen, acts_buf[some, :], preferred_element_type=f32)
        copies[part][1].wait()
        grads += jnp.dot(chosen, grad_buf[some, :], preferred_element_type=f32)
    picks[:, :cols] = found.astype(bf16)
    pad = jnp.zeros((drawn, picks.shape[1] - cols - group_cols), f32)
    for which in range(4):
        begin = min((which * group_cols) // block, last) * block
        offset = which * group_cols - begin

        @pl.when(group == which)
        def _():
            part = jnp.concatenate([grads[:, offset : offset + group_cols], pad], axis=1)
            picks[:, cols:] = part.astype(bf16)


def split_units(group, head, width_g):
    half = group.shape[1] // 2
    mid = width_g // 2
    middle = group[head : head + width_g]
    packed = [
        jnp.concatenate([middle[:mid, cols], middle[mid:, cols]], axis=1)
        for cols in (slice(0, half), slice(half, 2 * half))
    ]
    return (
        jnp.concatenate([group[:head], packed[0]], axis=0),
        jnp.concatenate([group[head + width_g :], packed[1]], axis=0),
    )


def partial_kernel(
    group_cols, width_g, info, out_grad, acts, send_a, keep_a, send_b, keep_b, grad_buf, acts_buf,
    raw, sems
):
    side, low = info[1], info[2]
    head = 2 * width_g
    outs = out_grad.shape[1]
    half = acts.shape[1] // 2
    block = outs // 5
    first = pltpu.make_async_copy(acts, acts_buf, sems.at[5])
    first.start()
    copies = []
    for step in range(5):
        columns = pl.ds(step * block, block)
        copies.append(
            pltpu.make_async_copy(out_grad.at[:, columns], grad_buf.at[:, columns], sems.at[step])
        )
        copies[-1].start()
    first.wait()
    for step in range(5):
        copies[step].wait()
        columns = slice(step * block, (step + 1) * block)
        raw[columns, :] = jnp.dot(
            grad_buf[:, columns].T, acts_buf[...], preferred_element_type=f32
        )
        if step == 0:
            continue
        place = step - 1
        span = slice(place * group_cols, (place + 1) * group_cols)
        zero, one = split_units(raw[span, :half], head, width_g)
        keep_a[place] = jnp.where(side == 0, zero, one)
        encode_to(send_a, place, jnp.where(side == 0, one, zero))
        if place % 2 == 0:
            continue
        before = slice((place - 1) * group_cols, place * group_cols)
        zero = split_units(raw[before, half:], head, width_g)
        one = split_units(raw[span, half:], head, width_g)
        for x in range(2):
            keep_b[place - 1 + x] = jnp.where(low == 0, zero[x], one[x])
            encode_to(send_b, place - 1 + x, jnp.where(low == 0, one[x], zero[x]))


def add_kernel(bit_at, inner, info, got, held, send, keep):
    bit = info[bit_at]
    rows = held.shape[1]
    count = send.shape[0]

    def place(j, value):
        return 2 * j + value if inner else value * count + j

    for j in range(count):
        away = place(j, 1 - bit)
        encode_to(send, j, held[away] + decode(got[away], rows))
    for j in range(count):
        home = place(j, bit)
        keep[j] = held[home] + decode(got[home], rows)


def last_add_kernel(info, got_a, held_a, got_b, held_b, send, keep):
    high = info[4]
    rows = keep.shape[1]
    for piece, (got, held) in enumerate(((got_a, held_a), (got_b, held_b))):
        encode_to(send, piece, held[1 - high] + decode(got[1 - high], rows))
        keep[piece] = held[high] + decode(got[high], rows)


def add_step(info, bit_at, inner, got, held):
    count = held.shape[0] // 2
    return pl.pallas_call(
        lambda *refs: add_kernel(bit_at, inner, *refs),
        in_specs=[smem, vmem, vmem],
        out_specs=[vmem, vmem],
        out_shape=[
            shaped((count,) + got.shape[1:], jnp.int16),
            shaped((count,) + held.shape[1:], f32),
        ],
        compiler_params=params(24),
        name="add",
    )(info, got, held)


def block_places(count_a, width_a, count_g, width_g):
    blocks, column, row = [], 0, 0
    for is_a, count, width in ((True, count_a, width_a), (False, count_g, width_g)):
        for place in range(count):
            blocks.append((is_a, place, width, column, row))
            column += width
            row += width + GROUP
    return blocks, row


def stats_kernel(blocks, info, own, one, two, packed, picks):
    place = info[3] >> 1
    picks[place] = own[...]
    picks[place ^ 2] = one[...]
    picks[place ^ 1] = two[0]
    picks[place ^ 3] = two[1]
    everything = picks[...].reshape(picks.shape[0] * picks.shape[1], picks.shape[2])
    for _, _, width, column, row in blocks:
        rows = everything[:, column : column + width]
        stats = lax.dot_general(
            rows, rows, (((0,), (0,)), ((), ())), preferred_element_type=f32
        )
        missing = packed.shape[1] - width
        if missing:
            stats = jnp.concatenate([stats, jnp.zeros((width, missing), f32)], axis=1)

        def store(first, data):
            packed[row + first : row + first + GROUP, :] = data

        encode(stats, store)


def factor_kernel(
    share, blocks, info, own_a, own_g, packed, got, a_state, g_state, a_new, g_new, inv_a, needed,
    inv_g
):
    group = info[0]
    count_a, count_g = a_state.shape[0], g_state.shape[0]
    errors, inverses, scales = [], [], []
    for is_a, place, width, _, first in blocks:
        span = slice(first, first + width + GROUP)
        stats = decode(packed[span, :], width) + decode(got[span, :], width)
        stats = stats[:, :width]
        slot = own_a[group, place] if is_a else own_g[group, place]
        stored = (a_state if is_a else g_state)[slot]
        factor = factor_decay * stored + share * stats
        (a_new if is_a else g_new)[slot] = factor
        row = lax.broadcasted_iota(jnp.int32, (width, width), 0)
        col = lax.broadcasted_iota(jnp.int32, (width, width), 1)
        identity = (row == col).astype(f32)
        trace = jnp.sum(factor * identity) / width
        damped = factor + (damping_rate * trace) * identity
        bound = jnp.max(jnp.sum(jnp.abs(damped), axis=0))
        error = identity - damped / bound
        errors.append(error)
        inverses.append(identity + error)
        scales.append(bound)
    every = range(count_a + count_g)
    dot = lambda p, q: jnp.dot(p, q, preferred_element_type=f32, precision=highest)
    errors = [dot(errors[i], errors[i]) for i in every]
    for step in range(1, NS_IT - 1):
        grown = [dot(inverses[i], errors[i]) for i in every]
        squares = [dot(errors[i], errors[i]) for i in every]
        inverses = [inverses[i] + grown[i] for i in every]
        errors = squares
    inverses = [(inverses[i] + dot(inverses[i], errors[i])) / scales[i] for i in every]
    for index in every:
        if index < count_a:
            inv_a[index] = inverses[index]
        else:
            inv_g[index - count_a] = inverses[index]
    side = info[1]
    needed[0] = inv_g[3 * side]
    needed[1] = inv_g[1 + 3 * side]
    needed[2] = inv_g[2]


def precon_kernel(info, got, held, inv_g, inv_a, top, mid, total):
    side = info[1]
    width_g, width_a = inv_g.shape[-1], inv_a.shape[-1]
    half = width_g // 2
    dot = lambda p, q: jnp.dot(p, q, preferred_element_type=f32, precision=highest)
    squares = jnp.zeros((width_g, width_a), f32)
    for piece in range(2):
        part = held[piece] + decode(got[piece], held.shape[1])
        for place in range(2):
            for block in range(2):
                values = dot(
                    inv_g[place],
                    part[
                        place * width_g : (place + 1) * width_g,
                        block * width_a : (block + 1) * width_a,
                    ],
                )
                values = dot(values, inv_a[2 * piece + block])
                squares += values * values
                column = (2 * piece + block) * width_a
                top[place * width_g : (place + 1) * width_g, column : column + width_a] = values
        packed = part[2 * width_g : 2 * width_g + half, :]
        values = jnp.concatenate([packed[:, :width_a], packed[:, width_a:]], axis=0)
        values = dot(dot(inv_g[2], values), inv_a[2 * piece + side])
        squares += values * values
        mid[:, piece * width_a : (piece + 1) * width_a] = values
    total[...] = jnp.full(total.shape, jnp.sum(squares), f32)


def update_kernel(
    entries, info, total, got_total, top, middle, got, momentum, weight, momentum_new, weight_new,
    rounded_a, rounded_b
):
    rows, cols = momentum.shape
    half = cols // 2
    quarter = half // 2
    head = top.shape[0]
    mid = rows - head
    mean_sq = (total[0:1, :] + got_total[0:1, :]) / entries
    factor = 1.0 / jnp.sqrt(mean_sq + epsilon_sq)
    factor = jnp.concatenate([factor, factor], axis=1)

    def step(place, precon):
        span = slice(place, place + precon.shape[0])
        moved = momentum_rate * momentum[span, :] + precon * factor + decay_rate * weight[span, :]
        fresh = weight[span, :] - learn_rate * moved
        momentum_new[span, :] = moved
        weight_new[span, :] = fresh
        rounded_a[span, :] = fresh[:, :half].astype(bf16)
        rounded_b[span, :] = fresh[:, half:].astype(bf16)

    for x in range(2):

        @pl.when(info[1] == x)
        def _():
            own = middle[mid * x : mid * (x + 1), :]
            pairs = []
            for piece in range(2):
                columns = slice(piece * quarter, (piece + 1) * quarter)
                both = [own[:, columns], got[:mid, columns]]
                pairs += both if x == 0 else both[::-1]
            step(head * (1 - x), jnp.concatenate(pairs, axis=1))
            step(mid * x, top[...])


def fast(acts, out_grad, sample_rows, own_a, own_g, a_state, g_state, momentum, weight):
    shard_pos = lax.axis_index("shard")
    tensor_pos = lax.axis_index("tensor")
    side, low, high = shard_pos & 1, (shard_pos >> 1) & 1, shard_pos >> 2
    count_a, width_a = a_state.shape[1], a_state.shape[2]
    count_g, width_g = g_state.shape[1], g_state.shape[2]
    group_cols = count_g * width_g
    tokens, cols = acts.shape
    outs = out_grad.shape[1]
    rows = momentum.shape[0]
    drawn = sample_rows.shape[0]
    samples = drawn * 8
    share = (1.0 - factor_decay) / samples
    half = cols // 2
    head = 2 * width_g
    mid = width_g // 2
    info = jnp.stack([tensor_pos, side, low, shard_pos, high])

    wide = cols + -(-group_cols // 128) * 128
    picks = pl.pallas_call(
        lambda *refs: picks_kernel(group_cols, *refs),
        in_specs=[smem, vmem, main, main],
        out_specs=vmem,
        out_shape=shaped((drawn, wide), bf16),
        scratch_shapes=[
            pltpu.VMEM((tokens, cols), bf16),
            pltpu.VMEM((tokens, 640), bf16),
            pltpu.SemaphoreType.DMA((8,)),
        ],
        compiler_params=params(60),
        name="picks",
    )(info, sample_rows.reshape(1, -1), acts, out_grad)
    one = swap(picks, 4)

    send_a, keep_a, send_b, keep_b = pl.pallas_call(
        lambda *refs: partial_kernel(group_cols, width_g, *refs),
        in_specs=[smem, main, main],
        out_specs=[vmem] * 4,
        out_shape=[
            shaped((4, rows + GROUP, half), jnp.int16),
            shaped((4, rows, half), f32),
        ]
        * 2,
        scratch_shapes=[
            pltpu.VMEM((tokens, outs), bf16),
            pltpu.VMEM((tokens, cols), bf16),
            pltpu.VMEM((outs, cols), f32),
            pltpu.SemaphoreType.DMA((6,)),
        ],
        compiler_params=params(56),
        name="partial",
    )(info, out_grad, acts)
    one, send_a, send_b = lax.optimization_barrier((one, send_a, send_b))
    got_a = swap(send_a, 1)
    two = swap(jnp.stack([picks, one]), 2)
    got_b = swap(send_b, 2)

    send_a, keep_a = add_step(info, 2, True, got_a, keep_a)
    got_a = swap(send_a, 2)
    blocks, packed_rows = block_places(count_a, width_a, count_g, width_g)
    packed = pl.pallas_call(
        lambda *refs: stats_kernel(blocks, *refs),
        in_specs=[smem] + [vmem] * 3,
        out_specs=vmem,
        out_shape=shaped((packed_rows, width_a), jnp.int16),
        scratch_shapes=[pltpu.VMEM((4, drawn, wide), bf16)],
        compiler_params=params(16),
        name="stats",
    )(info, picks, one, two)
    got_packed = swap(packed, 1)
    send_b, keep_b = add_step(info, 1, True, got_b, keep_b)
    got_b = swap(send_b, 1)

    send, keep = pl.pallas_call(
        last_add_kernel,
        in_specs=[smem] + [vmem] * 4,
        out_specs=[vmem, vmem],
        out_shape=[
            shaped((2, rows + GROUP, half), jnp.int16),
            shaped((2, rows, half), f32),
        ],
        compiler_params=params(24),
        name="last_add",
    )(info, got_a, keep_a, got_b, keep_b)
    got = swap(send, 4)

    new_a, new_g, inv_a, needed = pl.pallas_call(
        lambda *refs: factor_kernel(share, blocks, *refs),
        in_specs=[smem] * 3 + [vmem] * 4,
        out_specs=[vmem] * 4,
        out_shape=[
            shaped(a_state.shape[1:], f32),
            shaped(g_state.shape[1:], f32),
            shaped(a_state.shape[1:], f32),
            shaped((3, width_g, width_g), f32),
        ],
        scratch_shapes=[pltpu.VMEM(g_state.shape[1:], f32)],
        compiler_params=params(24),
        name="factors",
    )(info, own_a, own_g, packed, got_packed, a_state[0], g_state[0])
    route = [
        ((2 * a + b) * 4 + c, (2 * c + b) * 4 + a)
        for a in range(4)
        for b in range(2)
        for c in range(4)
    ]
    inv_rows = lax.ppermute(needed, ("shard", "tensor"), route)

    top, middle, total = pl.pallas_call(
        precon_kernel,
        in_specs=[smem] + [vmem] * 4,
        out_specs=[vmem] * 3,
        out_shape=[
            shaped((head, cols), f32),
            shaped((width_g, half), f32),
            shaped((8, half), f32),
        ],
        compiler_params=params(24),
        name="precon",
    )(info, got, keep, inv_rows, inv_a)

    total = total + swap_t(total, 1)
    total = total + swap_t(total, 2)
    give = pick(side, middle[mid:], middle[:mid])
    got = swap(jnp.concatenate([give, total], axis=0), 1)
    total = total + got[mid:]
    total = total + swap(total, 2)
    momentum_new, weight_new, rounded_a, rounded_b = pl.pallas_call(
        lambda *refs: update_kernel(rows * 8 * cols * 4, *refs),
        in_specs=[smem] + [vmem] * 7,
        out_specs=[vmem] * 4,
        out_shape=[
            shaped((rows, cols), f32),
            shaped((rows, cols), f32),
            shaped((rows, half), bf16),
            shaped((rows, half), bf16),
        ],
        compiler_params=params(24),
        name="update",
    )(info, total, swap(total, 4), top, middle, got, momentum, weight)

    def spread(values, bit, flag, axis):
        other = swap(values, bit)
        return jnp.stack([pick(flag, values, other), pick(flag, other, values)], axis=axis)

    piece = rounded_a
    piece = spread(piece, 4, high, 0)
    piece = spread(piece, 2, low, 1)
    whole_a = spread(piece, 1, side, 2).reshape(-1, half)
    piece = rounded_b
    piece = spread(piece, 1, side, 0)
    piece = spread(piece, 4, high, 0)
    whole_b = spread(piece, 2, low, 1).reshape(-1, half)
    gathered = jnp.concatenate([whole_a, whole_b], axis=1)
    return (new_a[None], new_g[None], momentum_new, weight_new, gathered)


def local(acts, out_grad, sample_rows, own_a, own_g, a_state, g_state, momentum, weight):
    shapes_fit = (
        lax.axis_size("shard") == 8
        and lax.axis_size("tensor") == 4
        and a_state.shape[1:] == (4, 128, 128)
        and g_state.shape[1:] == (5, 96, 96)
    )
    plan = fast if shapes_fit else general
    return plan(acts, out_grad, sample_rows, own_a, own_g, a_state, g_state, momentum, weight)


def solution(mesh):
    return jax.shard_map(
        local,
        mesh=mesh,
        in_specs=(
            P("shard", "tensor"),
            P("shard", None),
            P("shard"),
            P(),
            P(),
            P("tensor", None, None, None),
            P("tensor", None, None, None),
            P("shard", "tensor"),
            P("shard", "tensor"),
        ),
        out_specs=(
            P("tensor", None, None, None),
            P("tensor", None, None, None),
            P("shard", "tensor"),
            P("shard", "tensor"),
            P(None, "tensor"),
        ),
        check_vma=False,
    )
```

```python
import jax
import jax.numpy as jnp
from jax import lax
from jax.experimental import pallas as pl
from jax.experimental.pallas import tpu as pltpu
from jax.sharding import PartitionSpec as P

NS_IT = 5


factor_decay = 0.8
damping_rate = 0.03
momentum_rate = 0.9
decay_rate = 0.01
learn_rate = 0.05
epsilon_sq = 1e-06
highest = lax.Precision.HIGHEST
f32 = jnp.float32
bf16 = jnp.bfloat16


def newton_inverse(factor):
    width = factor.shape[-1]
    identity = jnp.eye(width, dtype=jnp.float32)
    trace_mean = jnp.trace(factor, axis1=-2, axis2=-1) / width
    damped = factor + damping_rate * trace_mean[:, None, None] * identity
    bound = jnp.max(jnp.sum(jnp.abs(damped), axis=-1), axis=-1)
    guess = identity[None] / bound[:, None, None]
    for iteration in range(NS_IT):
        product = jnp.einsum("bij,bjk->bik", damped, guess, precision=highest)
        guess = jnp.einsum("bij,bjk->bik", guess, 2.0 * identity - product, precision=highest)
    return guess


def local_stats(rows, width):
    blocks = rows.reshape(rows.shape[0], -1, width)
    return jnp.einsum("sbi,sbj->bij", blocks, blocks, preferred_element_type=jnp.float32)


def owner_part(slots, shard_pos, shard_count):
    count = slots.shape[0]
    stride = shard_count // count
    slot_pos = jnp.minimum(shard_pos // stride, count - 1)
    mine = lax.dynamic_index_in_dim(slots, slot_pos, 0, keepdims=True)
    inverse = newton_inverse(mine)
    marker = (jnp.arange(count, dtype=jnp.int32) * stride == shard_pos).astype(jnp.float32)
    return marker[:, None, None] * inverse


def general(acts, out_grad, sample_rows, own_a, own_g, a_state, g_state, momentum, weight):
    shard_count = lax.axis_size("shard")
    tensor_count = lax.axis_size("tensor")
    shard_pos = lax.axis_index("shard")
    tensor_pos = lax.axis_index("tensor")
    block_a = a_state.shape[-1]
    block_g = g_state.shape[-1]
    samples = sample_rows.shape[0] * shard_count
    fresh_share = (1.0 - factor_decay) / samples
    picked_a = jnp.take(acts, sample_rows, axis=0)
    picked_g = jnp.take(out_grad, sample_rows, axis=0)
    group_cols = out_grad.shape[1] // tensor_count
    picked_g = lax.dynamic_slice_in_dim(picked_g, tensor_pos * group_cols, group_cols, 1)
    stats_a = local_stats(picked_a, block_a)
    stats_g = local_stats(picked_g, block_g)
    row_a = lax.dynamic_index_in_dim(own_a, tensor_pos, 0, keepdims=False)
    row_g = lax.dynamic_index_in_dim(own_g, tensor_pos, 0, keepdims=False)
    select_a = (row_a[None, :] == jnp.arange(row_a.shape[0], dtype=jnp.int32)[:, None]).astype(
        jnp.float32
    )
    select_g = (row_g[None, :] == jnp.arange(row_g.shape[0], dtype=jnp.int32)[:, None]).astype(
        jnp.float32
    )
    summed_a, summed_g = lax.psum((fresh_share * stats_a, fresh_share * stats_g), "shard")
    stored_a = jnp.einsum("sb,sij->bij", select_a, a_state[0], precision=highest)
    stored_g = jnp.einsum("sb,sij->bij", select_g, g_state[0], precision=highest)
    fac_a = factor_decay * stored_a + summed_a
    fac_g = factor_decay * stored_g + summed_g
    slots_a = jnp.einsum("sb,bij->sij", select_a, fac_a, precision=highest)
    slots_g = jnp.einsum("sb,bij->sij", select_g, fac_g, precision=highest)
    new_a_state = slots_a[None]
    new_g_state = slots_g[None]
    slot_inv_a, slot_inv_g = lax.psum(
        (owner_part(slots_a, shard_pos, shard_count), owner_part(slots_g, shard_pos, shard_count)),
        "shard",
    )
    inv_a = jnp.einsum("sb,sij->bij", select_a, slot_inv_a, precision=highest)
    local_inv_g = jnp.einsum("sb,sij->bij", select_g, slot_inv_g, precision=highest)
    inv_g = lax.all_gather(local_inv_g, "tensor", axis=0, tiled=True)
    raw_product = lax.dot_general(
        out_grad, acts, (((0,), (0,)), ((), ())), preferred_element_type=jnp.float32
    )
    left_done = jnp.einsum(
        "bij,bjd->bid", inv_g, raw_product.reshape(inv_g.shape[0], block_g, -1), precision=highest
    ).reshape(raw_product.shape)
    owned_rows = lax.psum_scatter(left_done, "shard", scatter_dimension=0, tiled=True)
    precon = jnp.einsum(
        "qbi,bij->qbj",
        owned_rows.reshape(owned_rows.shape[0], -1, block_a),
        inv_a,
        precision=highest,
    ).reshape(owned_rows.shape)
    square_total = lax.psum(jnp.sum(precon * precon), ("shard", "tensor"))
    mean_sq = square_total / (momentum.shape[0] * shard_count * momentum.shape[1] * tensor_count)
    update = precon / jnp.sqrt(mean_sq + epsilon_sq)
    momentum_new = momentum_rate * momentum + update + decay_rate * weight
    weight_new = weight - learn_rate * momentum_new
    gathered = lax.all_gather(weight_new.astype(jnp.bfloat16), "shard", axis=0, tiled=True)
    return (new_a_state, new_g_state, momentum_new, weight_new, gathered)


GROUP = 16
vmem = pl.BlockSpec(memory_space=pltpu.VMEM)
smem = pl.BlockSpec(memory_space=pltpu.SMEM)
main = pl.BlockSpec(memory_space=pl.ANY)


def params(mib):
    return pltpu.CompilerParams(vmem_limit_bytes=mib * 2**20)


def shaped(shape, kind):
    return jax.ShapeDtypeStruct(shape, kind)


def cost(flops, moved):
    return pl.CostEstimate(flops=flops, bytes_accessed=moved, transcendentals=0)


def swap(value, bit):
    return lax.ppermute(value, "shard", [(i, i ^ bit) for i in range(8)])


def swap_t(value, bit):
    return lax.ppermute(value, "tensor", [(i, i ^ bit) for i in range(4)])


def swap_both(value, bit, bit_t):
    route = [(4 * s + t, 4 * (s ^ bit) + (t ^ bit_t)) for s in range(8) for t in range(4)]
    return lax.ppermute(value, ("shard", "tensor"), route)


def pick(flag, if_zero, if_one):
    return jnp.where(flag == 0, if_zero, if_one)


def encode(value, store):
    rows, width = value.shape
    powers = []
    for first in range(0, rows, GROUP):
        part = value[first : first + GROUP]
        top = jnp.max(jnp.abs(part), axis=0, keepdims=True)
        power = jnp.floor(jnp.log2(jnp.maximum(top, 1e-30)))
        scaled = jnp.clip(jnp.round(part * jnp.exp2(14.0 - power)), -32767.0, 32767.0)
        store(first, scaled.astype(jnp.int32).astype(jnp.int16))
        powers.append(power)
    powers += [jnp.zeros((1, width), f32)] * (GROUP - len(powers))
    store(rows, jnp.concatenate(powers, axis=0).astype(jnp.int32).astype(jnp.int16))


def decode(packed, rows):
    whole = packed.astype(jnp.int32).astype(f32)
    scales = jnp.exp2(whole[rows : rows + GROUP] - 14.0)
    parts = [
        whole[first : first + GROUP] * scales[first // GROUP : first // GROUP + 1]
        for first in range(0, rows, GROUP)
    ]
    return jnp.concatenate(parts, axis=0)


def encode_to(ref, index, value):
    def store(first, data):
        ref[index, first : first + GROUP, :] = data

    encode(value, store)


FINE = 8
FULL = 32767.0
STEPS = 128.0


def encode_fine(value, ref):
    rows, width = value.shape
    powers = []
    for first in range(0, rows, 2 * FINE):
        scaled = []
        for start in (first, first + FINE):
            part = value[start : start + FINE]
            top = jnp.max(jnp.abs(part), axis=0, keepdims=True)
            power = jnp.ceil(jnp.log2(jnp.maximum(top, 1e-30)) * STEPS)
            scale = jnp.exp2(power * (-1.0 / STEPS)) * FULL
            scaled.append(jnp.clip(jnp.round(part * scale), -FULL, FULL))
            powers.append(power)
        ref[first : first + 2 * FINE, :] = (
            jnp.concatenate(scaled, axis=0).astype(jnp.int32).astype(jnp.int16)
        )
    powers += [jnp.zeros((1, width), f32)] * (-len(powers) % (2 * FINE))
    for first in range(0, len(powers), 2 * FINE):
        ref[rows + first : rows + first + 2 * FINE, :] = (
            jnp.concatenate(powers[first : first + 2 * FINE], axis=0)
            .astype(jnp.int32)
            .astype(jnp.int16)
        )


def decode_fine(ref, rows):
    values = ref[:rows, :].astype(jnp.int32).astype(f32)
    powers = ref[rows:, :].astype(jnp.int32).astype(f32)
    scales = jnp.exp2(powers * (1.0 / STEPS)) * (1.0 / FULL)
    parts = [
        values[first : first + FINE] * scales[first // FINE : first // FINE + 1]
        for first in range(0, rows, FINE)
    ]
    return jnp.concatenate(parts, axis=0)


def fine_rows(rows):
    return rows + -(-(rows // FINE) // (2 * FINE)) * 2 * FINE


def base_kernel(momentum, weight, packed):
    kept = momentum_rate * momentum[...] + decay_rate * weight[...]
    encode_fine(weight[...] - learn_rate * kept, packed)


def parts_of(value):
    upper = value.astype(bf16)
    return upper, (value - upper.astype(f32)).astype(bf16)


def dot_of(left, right):
    dot = lambda p, q: jnp.dot(p, q, preferred_element_type=f32)
    small = dot(left[0], right[1]) + dot(left[1], right[0])
    return dot(left[0], right[0]) + small


def picks_kernel(group_cols, info, sampled, acts, out_grad, picks, acts_buf, grad_buf, sems):
    group = info[0]
    block = 128
    span = grad_buf.shape[1]
    tokens, cols = acts.shape
    chunk = tokens // 4
    last = out_grad.shape[1] // block - span // block
    start = pl.multiple_of(jnp.minimum((group * group_cols) // block, last) * block, block)
    copies = []
    for part in range(4):
        some = pl.ds(part * chunk, chunk)
        copies.append(
            (
                pltpu.make_async_copy(acts.at[some, :], acts_buf.at[some, :], sems.at[part]),
                pltpu.make_async_copy(
                    out_grad.at[some, pl.ds(start, span)], grad_buf.at[some, :], sems.at[4 + part]
                ),
            )
        )
        for copy in copies[-1]:
            copy.start()
    drawn = sampled.shape[1]
    row = lax.broadcasted_iota(jnp.int32, (drawn, drawn), 0)
    col = lax.broadcasted_iota(jnp.int32, (drawn, drawn), 1)
    upright = jnp.sum(jnp.where(row == col, sampled[...], 0), axis=1, keepdims=True)
    found = jnp.zeros((drawn, cols), f32)
    grads = jnp.zeros((drawn, span), f32)
    for part in range(4):
        place = lax.broadcasted_iota(jnp.int32, (drawn, chunk), 1) + part * chunk
        chosen = (place == upright).astype(bf16)
        some = slice(part * chunk, (part + 1) * chunk)
        copies[part][0].wait()
        found += jnp.dot(chosen, acts_buf[some, :], preferred_element_type=f32)
        copies[part][1].wait()
        grads += jnp.dot(chosen, grad_buf[some, :], preferred_element_type=f32)
    picks[:, :cols] = found.astype(bf16)
    pad = jnp.zeros((drawn, picks.shape[1] - cols - group_cols), f32)
    for which in range(4):
        begin = min((which * group_cols) // block, last) * block
        offset = which * group_cols - begin

        @pl.when(group == which)
        def _():
            part = jnp.concatenate([grads[:, offset : offset + group_cols], pad], axis=1)
            picks[:, cols:] = part.astype(bf16)


def split_units(group, head, width_g):
    half = group.shape[1] // 2
    mid = width_g // 2
    middle = group[head : head + width_g]
    packed = [
        jnp.concatenate([middle[:mid, cols], middle[mid:, cols]], axis=1)
        for cols in (slice(0, half), slice(half, 2 * half))
    ]
    return (
        jnp.concatenate([group[:head], packed[0]], axis=0),
        jnp.concatenate([group[head + width_g :], packed[1]], axis=0),
    )


def partial_kernel(
    group_cols, width_g, info, out_grad, acts, send_a, keep_a, send_b, keep_b, grad_buf, acts_buf,
    raw, sems
):
    side, low = info[1], info[2]
    head = 2 * width_g
    outs = out_grad.shape[1]
    half = acts.shape[1] // 2
    block = outs // 5
    first = pltpu.make_async_copy(acts, acts_buf, sems.at[5])
    first.start()
    copies = []
    for step in range(5):
        columns = pl.ds(step * block, block)
        copies.append(
            pltpu.make_async_copy(out_grad.at[:, columns], grad_buf.at[:, columns], sems.at[step])
        )
        copies[-1].start()
    first.wait()
    for step in range(5):
        copies[step].wait()
        columns = slice(step * block, (step + 1) * block)
        raw[columns, :] = jnp.dot(
            grad_buf[:, columns].T, acts_buf[...], preferred_element_type=f32
        )
        if step == 0:
            continue
        place = step - 1
        span = slice(place * group_cols, (place + 1) * group_cols)
        zero, one = split_units(raw[span, :half], head, width_g)
        keep_a[place] = jnp.where(side == 0, zero, one)
        encode_to(send_a, place, jnp.where(side == 0, one, zero))
        if place % 2 == 0:
            continue
        before = slice((place - 1) * group_cols, place * group_cols)
        zero = split_units(raw[before, half:], head, width_g)
        one = split_units(raw[span, half:], head, width_g)
        for x in range(2):
            keep_b[place - 1 + x] = jnp.where(low == 0, zero[x], one[x])
            encode_to(send_b, place - 1 + x, jnp.where(low == 0, one[x], zero[x]))


def add_kernel(bit_at, inner, info, got, held, send, keep):
    bit = info[bit_at]
    rows = held.shape[1]
    count = send.shape[0]

    def place(j, value):
        return 2 * j + value if inner else value * count + j

    for j in range(count):
        away = place(j, 1 - bit)
        encode_to(send, j, held[away] + decode(got[away], rows))
    for j in range(count):
        home = place(j, bit)
        keep[j] = held[home] + decode(got[home], rows)


def last_add_kernel(info, got_a, held_a, got_b, held_b, send, keep):
    high = info[4]
    rows = keep.shape[1]
    for piece, (got, held) in enumerate(((got_a, held_a), (got_b, held_b))):
        encode_to(send, piece, held[1 - high] + decode(got[1 - high], rows))
        keep[piece] = held[high] + decode(got[high], rows)


def add_step(info, bit_at, inner, got, held):
    count = held.shape[0] // 2
    return pl.pallas_call(
        lambda *refs: add_kernel(bit_at, inner, *refs),
        in_specs=[smem, vmem, vmem],
        out_specs=[vmem, vmem],
        out_shape=[
            shaped((count,) + got.shape[1:], jnp.int16),
            shaped((count,) + held.shape[1:], f32),
        ],
        compiler_params=params(24),
        name="add",
    )(info, got, held)


def block_places(count_a, width_a, count_g, width_g):
    blocks, column, row = [], 0, 0
    for is_a, count, width in ((True, count_a, width_a), (False, count_g, width_g)):
        for place in range(count):
            blocks.append((is_a, place, width, column, row))
            column += width
            row += width + GROUP
    return blocks, row


def stats_kernel(blocks, info, own, one, two, packed, picks):
    place = 2 * info[4] + info[1]
    picks[place] = own[...]
    picks[place ^ 2] = one[...]
    picks[place ^ 1] = two[0]
    picks[place ^ 3] = two[1]
    everything = picks[...].reshape(picks.shape[0] * picks.shape[1], picks.shape[2])
    for _, _, width, column, row in blocks:
        rows = everything[:, column : column + width]
        stats = lax.dot_general(
            rows, rows, (((0,), (0,)), ((), ())), preferred_element_type=f32
        )
        missing = packed.shape[1] - width
        if missing:
            stats = jnp.concatenate([stats, jnp.zeros((width, missing), f32)], axis=1)

        def store(first, data):
            packed[row + first : row + first + GROUP, :] = data

        encode(stats, store)


def factor_kernel(
    share, blocks, info, own_a, own_g, packed, got, a_state, g_state, a_new, g_new, inv_a, needed,
    inv_g
):
    group = info[0]
    count_a, count_g = a_state.shape[0], g_state.shape[0]
    errors, inverses, scales = [], [], []
    for is_a, place, width, _, first in blocks:
        span = slice(first, first + width + GROUP)
        stats = decode(packed[span, :], width) + decode(got[span, :], width)
        stats = stats[:, :width]
        slot = own_a[group, place] if is_a else own_g[group, place]
        stored = (a_state if is_a else g_state)[slot]
        factor = factor_decay * stored + share * stats
        (a_new if is_a else g_new)[slot] = factor
        row = lax.broadcasted_iota(jnp.int32, (width, width), 0)
        col = lax.broadcasted_iota(jnp.int32, (width, width), 1)
        identity = (row == col).astype(f32)
        trace = jnp.sum(factor * identity) / width
        damped = factor + (damping_rate * trace) * identity
        bound = jnp.max(jnp.sum(jnp.abs(damped), axis=0))
        error = identity - damped / bound
        errors.append(error)
        inverses.append(identity + error)
        scales.append(bound)
    every = range(count_a + count_g)
    errors = [parts_of(errors[i]) for i in every]
    errors = [parts_of(dot_of(errors[i], errors[i])) for i in every]
    for step in range(1, NS_IT - 1):
        grown = [dot_of(parts_of(inverses[i]), errors[i]) for i in every]
        squares = [dot_of(errors[i], errors[i]) for i in every]
        inverses = [inverses[i] + grown[i] for i in every]
        errors = [parts_of(squares[i]) for i in every]
    grown = [dot_of(parts_of(inverses[i]), errors[i]) for i in every]
    inverses = [(inverses[i] + grown[i]) / scales[i] for i in every]
    for index in every:
        if index < count_a:
            inv_a[index] = inverses[index]
        else:
            inv_g[index - count_a] = inverses[index]
    side = info[1]
    for index, place in enumerate((3 * side, 1 + 3 * side, 2)):
        encode_to(needed, index, inv_g[place])


def precon_kernel(info, got, held, inv_g, inv_a, top, mid, total, coded):
    side = info[1]
    width_g, width_a = inv_g.shape[-1], inv_a.shape[-1]
    half = width_g // 2
    dot = lambda p, q: dot_of(parts_of(p), parts_of(q))
    left = [decode(inv_g[place], width_g) for place in range(3)]
    squares = jnp.zeros((width_g, width_a), f32)
    for piece in range(2):
        part = held[piece] + decode(got[piece], held.shape[1])
        for place in range(2):
            for block in range(2):
                values = dot(
                    left[place],
                    part[
                        place * width_g : (place + 1) * width_g,
                        block * width_a : (block + 1) * width_a,
                    ],
                )
                values = dot(values, inv_a[2 * piece + block])
                squares += values * values
                column = (2 * piece + block) * width_a
                top[place * width_g : (place + 1) * width_g, column : column + width_a] = values
        packed = part[2 * width_g : 2 * width_g + half, :]
        values = jnp.concatenate([packed[:, :width_a], packed[:, width_a:]], axis=0)
        values = dot(dot(left[2], values), inv_a[2 * piece + side])
        squares += values * values
        mid[:, piece * width_a : (piece + 1) * width_a] = values
    total[...] = jnp.full(total.shape, jnp.sum(squares), f32)
    encode_fine(top[...], coded)


def middle_kernel(info, middle, got, total, along_y, along_both, rest, packed, sums):
    mid, cols = rest.shape
    quarter = cols // 4
    sums[...] = (total[...] + got[mid:, :]) + (along_y[...] + along_both[...])
    for x in range(2):

        @pl.when(info[1] == x)
        def _():
            own = middle[mid * x : mid * (x + 1), :]
            pairs = []
            for piece in range(2):
                columns = slice(piece * quarter, (piece + 1) * quarter)
                both = [own[:, columns], got[:mid, columns]]
                pairs += both if x == 0 else both[::-1]
            rest[...] = jnp.concatenate(pairs, axis=1)

    encode_fine(rest[...], packed)


def update_kernel(
    entries, info, total, along_l, along_h, along_both, top, rest, momentum, weight, base, base_far,
    scaled, scaled_far, small, small_far, momentum_new, weight_new, rounded_a, rounded_b
):
    rows, cols = momentum.shape
    half = cols // 2
    head, mid = top.shape[0], rest.shape[0]
    sums = [each[0:1, :] for each in (total, along_l, along_h, along_both)]
    mean_sq = ((sums[0] + sums[1]) + (sums[2] + sums[3])) / entries
    factor = 1.0 / jnp.sqrt(mean_sq + epsilon_sq)
    factor = jnp.concatenate([factor, factor], axis=1)
    fixed = [decode_fine(base, rows), decode_fine(base_far, rows)]
    moving = [
        (decode_fine(scaled, head), decode_fine(small, mid)),
        (decode_fine(scaled_far, head), decode_fine(small_far, mid)),
    ]

    def step(order):
        precon = jnp.concatenate([(top, rest)[which][...] for which in order], axis=0)
        moved = momentum_rate * momentum[...] + precon * factor + decay_rate * weight[...]
        momentum_new[...] = moved
        weight_new[...] = weight[...] - learn_rate * moved
        for place in range(2):
            change = jnp.concatenate([moving[place][which] for which in order], axis=0)
            fresh = fixed[place] - (learn_rate * factor) * change
            rounded_a[place] = fresh[:, :half].astype(bf16)
            rounded_b[place] = fresh[:, half:].astype(bf16)

    for x, order in enumerate(((0, 1), (1, 0))):

        @pl.when(info[1] == x)
        def _():
            step(order)


def place_kernel(rows, info, *refs):
    parts, out = refs[:6], refs[6]
    shard = info[3]
    half = out.shape[1] // 2
    codes = ((0, 4), (2, 6), (1, 5, 3, 7), (0, 4), (1, 5), (2, 6, 3, 7))
    for index, (part, units) in enumerate(zip(parts, codes)):
        first = half * (index // 3)
        for place, code in enumerate(units):
            start = pl.multiple_of((shard ^ code) * rows, 16)
            out[pl.ds(start, rows), first : first + half] = part[place]


def fast(acts, out_grad, sample_rows, own_a, own_g, a_state, g_state, momentum, weight):
    shard_pos = lax.axis_index("shard")
    tensor_pos = lax.axis_index("tensor")
    side, low, high = shard_pos & 1, (shard_pos >> 1) & 1, shard_pos >> 2
    count_a, width_a = a_state.shape[1], a_state.shape[2]
    count_g, width_g = g_state.shape[1], g_state.shape[2]
    group_cols = count_g * width_g
    tokens, cols = acts.shape
    outs = out_grad.shape[1]
    rows = momentum.shape[0]
    drawn = sample_rows.shape[0]
    samples = drawn * 8
    share = (1.0 - factor_decay) / samples
    half = cols // 2
    head = 2 * width_g
    mid = width_g // 2
    info = jnp.stack([tensor_pos, side, low, shard_pos, high])

    wide = cols + -(-group_cols // 128) * 128
    picks = pl.pallas_call(
        lambda *refs: picks_kernel(group_cols, *refs),
        in_specs=[smem, vmem, main, main],
        out_specs=vmem,
        out_shape=shaped((drawn, wide), bf16),
        scratch_shapes=[
            pltpu.VMEM((tokens, cols), bf16),
            pltpu.VMEM((tokens, 640), bf16),
            pltpu.SemaphoreType.DMA((8,)),
        ],
        compiler_params=params(60),
        name="picks",
    )(info, sample_rows.reshape(1, -1), acts, out_grad)
    one = swap(picks, 4)

    send_a, keep_a, send_b, keep_b = pl.pallas_call(
        lambda *refs: partial_kernel(group_cols, width_g, *refs),
        in_specs=[smem, main, main],
        out_specs=[vmem] * 4,
        out_shape=[
            shaped((4, rows + GROUP, half), jnp.int16),
            shaped((4, rows, half), f32),
        ]
        * 2,
        scratch_shapes=[
            pltpu.VMEM((tokens, outs), bf16),
            pltpu.VMEM((tokens, cols), bf16),
            pltpu.VMEM((outs, cols), f32),
            pltpu.SemaphoreType.DMA((6,)),
        ],
        compiler_params=params(56),
        name="partial",
    )(info, out_grad, acts)
    base = pl.pallas_call(
        base_kernel,
        in_specs=[vmem, vmem],
        out_specs=vmem,
        out_shape=shaped((fine_rows(rows), cols), jnp.int16),
        compiler_params=params(16),
        name="base",
    )(momentum, weight)
    one, send_a, send_b, base = lax.optimization_barrier((one, send_a, send_b, base))
    base_far = swap(base, 4)
    got_a = swap(send_a, 1)
    two = swap(jnp.stack([picks, one]), 1)
    got_b = swap(send_b, 2)

    send_a, keep_a = add_step(info, 2, True, got_a, keep_a)
    got_a = swap(send_a, 2)
    blocks, packed_rows = block_places(count_a, width_a, count_g, width_g)
    packed = pl.pallas_call(
        lambda *refs: stats_kernel(blocks, *refs),
        in_specs=[smem] + [vmem] * 3,
        out_specs=vmem,
        out_shape=shaped((packed_rows, width_a), jnp.int16),
        scratch_shapes=[pltpu.VMEM((4, drawn, wide), bf16)],
        compiler_params=params(16),
        name="stats",
    )(info, picks, one, two)
    got_packed = swap(packed, 2)
    send_b, keep_b = add_step(info, 1, True, got_b, keep_b)
    got_b = swap(send_b, 1)

    got_a, base_far = lax.optimization_barrier((got_a, base_far))
    send, keep = pl.pallas_call(
        last_add_kernel,
        in_specs=[smem] + [vmem] * 4,
        out_specs=[vmem, vmem],
        out_shape=[
            shaped((2, rows + GROUP, half), jnp.int16),
            shaped((2, rows, half), f32),
        ],
        compiler_params=params(24),
        name="last_add",
    )(info, got_a, keep_a, got_b, keep_b)
    got = swap(send, 4)

    new_a, new_g, inv_a, needed = pl.pallas_call(
        lambda *refs: factor_kernel(share, blocks, *refs),
        in_specs=[smem] * 3 + [vmem] * 4,
        out_specs=[vmem] * 4,
        out_shape=[
            shaped(a_state.shape[1:], f32),
            shaped(g_state.shape[1:], f32),
            shaped(a_state.shape[1:], f32),
            shaped((3, width_g + GROUP, width_g), jnp.int16),
        ],
        scratch_shapes=[pltpu.VMEM(g_state.shape[1:], f32)],
        compiler_params=params(24),
        name="factors",
    )(info, own_a, own_g, packed, got_packed, a_state[0], g_state[0])
    route = [
        ((2 * a + b) * 4 + c, (2 * c + b) * 4 + a)
        for a in range(4)
        for b in range(2)
        for c in range(4)
    ]
    inv_rows = lax.ppermute(needed, ("shard", "tensor"), route)

    top, middle, total, scaled = pl.pallas_call(
        precon_kernel,
        in_specs=[smem] + [vmem] * 4,
        out_specs=[vmem] * 4,
        out_shape=[
            shaped((head, cols), f32),
            shaped((width_g, half), f32),
            shaped((8, half), f32),
            shaped((fine_rows(head), cols), jnp.int16),
        ],
        compiler_params=params(24),
        name="precon",
    )(info, got, keep, inv_rows, inv_a)

    scaled_far = swap(scaled, 4)
    give = pick(side, middle[mid:], middle[:mid])
    got = swap(jnp.concatenate([give, total], axis=0), 1)
    along_y = swap_t(total, 2)
    along_both = swap_both(total, 1, 2)
    rest, small, total = pl.pallas_call(
        middle_kernel,
        in_specs=[smem] + [vmem] * 5,
        out_specs=[vmem] * 3,
        out_shape=[
            shaped((mid, cols), f32),
            shaped((fine_rows(mid), cols), jnp.int16),
            shaped((8, half), f32),
        ],
        compiler_params=params(16),
        name="middle",
    )(info, middle, got, total, along_y, along_both)
    small_far = swap(small, 4)
    total = total + swap_t(total, 1)
    others = [swap(total, bits) for bits in (2, 4, 6)]
    momentum_new, weight_new, rounded_a, rounded_b = pl.pallas_call(
        lambda *refs: update_kernel(rows * 8 * cols * 4, *refs),
        in_specs=[smem] + [vmem] * 14,
        out_specs=[vmem] * 4,
        out_shape=[
            shaped((rows, cols), f32),
            shaped((rows, cols), f32),
            shaped((2, rows, half), bf16),
            shaped((2, rows, half), bf16),
        ],
        compiler_params=params(24),
        name="update",
    )(
        info, total, *others, top, rest, momentum, weight, base, base_far, scaled, scaled_far,
        small, small_far,
    )

    along_l = swap(rounded_a, 2)
    along_x = swap(rounded_b, 1)
    rest_a = swap(jnp.concatenate([rounded_a, along_l]), 1)
    rest_b = swap(jnp.concatenate([rounded_b, along_x]), 2)
    gathered = pl.pallas_call(
        lambda *refs: place_kernel(rows, *refs),
        in_specs=[smem] + [vmem] * 6,
        out_specs=vmem,
        out_shape=shaped((rows * 8, cols), bf16),
        compiler_params=params(16),
        name="place",
    )(info, rounded_a, along_l, rest_a, rounded_b, along_x, rest_b)
    return (new_a[None], new_g[None], momentum_new, weight_new, gathered)


def local(acts, out_grad, sample_rows, own_a, own_g, a_state, g_state, momentum, weight):
    shapes_fit = (
        lax.axis_size("shard") == 8
        and lax.axis_size("tensor") == 4
        and a_state.shape[1:] == (4, 128, 128)
        and g_state.shape[1:] == (5, 96, 96)
    )
    plan = fast if shapes_fit else general
    return plan(acts, out_grad, sample_rows, own_a, own_g, a_state, g_state, momentum, weight)


def solution(mesh):
    return jax.shard_map(
        local,
        mesh=mesh,
        in_specs=(
            P("shard", "tensor"),
            P("shard", None),
            P("shard"),
            P(),
            P(),
            P("tensor", None, None, None),
            P("tensor", None, None, None),
            P("shard", "tensor"),
            P("shard", "tensor"),
        ),
        out_specs=(
            P("tensor", None, None, None),
            P("tensor", None, None, None),
            P("shard", "tensor"),
            P("shard", "tensor"),
            P(None, "tensor"),
        ),
        check_vma=False,
    )
```

```python
import jax
import jax.numpy as jnp
from jax import lax
from jax.experimental import pallas as pl
from jax.experimental.pallas import tpu as pltpu
from jax.sharding import PartitionSpec as P

NS_IT = 5


factor_decay = 0.8
damping_rate = 0.03
momentum_rate = 0.9
decay_rate = 0.01
learn_rate = 0.05
epsilon_sq = 1e-06
highest = lax.Precision.HIGHEST
f32 = jnp.float32
bf16 = jnp.bfloat16


def newton_inverse(factor):
    width = factor.shape[-1]
    identity = jnp.eye(width, dtype=jnp.float32)
    trace_mean = jnp.trace(factor, axis1=-2, axis2=-1) / width
    damped = factor + damping_rate * trace_mean[:, None, None] * identity
    bound = jnp.max(jnp.sum(jnp.abs(damped), axis=-1), axis=-1)
    guess = identity[None] / bound[:, None, None]
    for iteration in range(NS_IT):
        product = jnp.einsum("bij,bjk->bik", damped, guess, precision=highest)
        guess = jnp.einsum("bij,bjk->bik", guess, 2.0 * identity - product, precision=highest)
    return guess


def local_stats(rows, width):
    blocks = rows.reshape(rows.shape[0], -1, width)
    return jnp.einsum("sbi,sbj->bij", blocks, blocks, preferred_element_type=jnp.float32)


def owner_part(slots, shard_pos, shard_count):
    count = slots.shape[0]
    stride = shard_count // count
    slot_pos = jnp.minimum(shard_pos // stride, count - 1)
    mine = lax.dynamic_index_in_dim(slots, slot_pos, 0, keepdims=True)
    inverse = newton_inverse(mine)
    marker = (jnp.arange(count, dtype=jnp.int32) * stride == shard_pos).astype(jnp.float32)
    return marker[:, None, None] * inverse


def general(acts, out_grad, sample_rows, own_a, own_g, a_state, g_state, momentum, weight):
    shard_count = lax.axis_size("shard")
    tensor_count = lax.axis_size("tensor")
    shard_pos = lax.axis_index("shard")
    tensor_pos = lax.axis_index("tensor")
    block_a = a_state.shape[-1]
    block_g = g_state.shape[-1]
    samples = sample_rows.shape[0] * shard_count
    fresh_share = (1.0 - factor_decay) / samples
    picked_a = jnp.take(acts, sample_rows, axis=0)
    picked_g = jnp.take(out_grad, sample_rows, axis=0)
    group_cols = out_grad.shape[1] // tensor_count
    picked_g = lax.dynamic_slice_in_dim(picked_g, tensor_pos * group_cols, group_cols, 1)
    stats_a = local_stats(picked_a, block_a)
    stats_g = local_stats(picked_g, block_g)
    row_a = lax.dynamic_index_in_dim(own_a, tensor_pos, 0, keepdims=False)
    row_g = lax.dynamic_index_in_dim(own_g, tensor_pos, 0, keepdims=False)
    select_a = (row_a[None, :] == jnp.arange(row_a.shape[0], dtype=jnp.int32)[:, None]).astype(
        jnp.float32
    )
    select_g = (row_g[None, :] == jnp.arange(row_g.shape[0], dtype=jnp.int32)[:, None]).astype(
        jnp.float32
    )
    summed_a, summed_g = lax.psum((fresh_share * stats_a, fresh_share * stats_g), "shard")
    stored_a = jnp.einsum("sb,sij->bij", select_a, a_state[0], precision=highest)
    stored_g = jnp.einsum("sb,sij->bij", select_g, g_state[0], precision=highest)
    fac_a = factor_decay * stored_a + summed_a
    fac_g = factor_decay * stored_g + summed_g
    slots_a = jnp.einsum("sb,bij->sij", select_a, fac_a, precision=highest)
    slots_g = jnp.einsum("sb,bij->sij", select_g, fac_g, precision=highest)
    new_a_state = slots_a[None]
    new_g_state = slots_g[None]
    slot_inv_a, slot_inv_g = lax.psum(
        (owner_part(slots_a, shard_pos, shard_count), owner_part(slots_g, shard_pos, shard_count)),
        "shard",
    )
    inv_a = jnp.einsum("sb,sij->bij", select_a, slot_inv_a, precision=highest)
    local_inv_g = jnp.einsum("sb,sij->bij", select_g, slot_inv_g, precision=highest)
    inv_g = lax.all_gather(local_inv_g, "tensor", axis=0, tiled=True)
    raw_product = lax.dot_general(
        out_grad, acts, (((0,), (0,)), ((), ())), preferred_element_type=jnp.float32
    )
    left_done = jnp.einsum(
        "bij,bjd->bid", inv_g, raw_product.reshape(inv_g.shape[0], block_g, -1), precision=highest
    ).reshape(raw_product.shape)
    owned_rows = lax.psum_scatter(left_done, "shard", scatter_dimension=0, tiled=True)
    precon = jnp.einsum(
        "qbi,bij->qbj",
        owned_rows.reshape(owned_rows.shape[0], -1, block_a),
        inv_a,
        precision=highest,
    ).reshape(owned_rows.shape)
    square_total = lax.psum(jnp.sum(precon * precon), ("shard", "tensor"))
    mean_sq = square_total / (momentum.shape[0] * shard_count * momentum.shape[1] * tensor_count)
    update = precon / jnp.sqrt(mean_sq + epsilon_sq)
    momentum_new = momentum_rate * momentum + update + decay_rate * weight
    weight_new = weight - learn_rate * momentum_new
    gathered = lax.all_gather(weight_new.astype(jnp.bfloat16), "shard", axis=0, tiled=True)
    return (new_a_state, new_g_state, momentum_new, weight_new, gathered)


GROUP = 16
vmem = pl.BlockSpec(memory_space=pltpu.VMEM)
smem = pl.BlockSpec(memory_space=pltpu.SMEM)
main = pl.BlockSpec(memory_space=pl.ANY)


def params(mib):
    return pltpu.CompilerParams(vmem_limit_bytes=mib * 2**20)


def shaped(shape, kind):
    return jax.ShapeDtypeStruct(shape, kind)


def cost(flops, moved):
    return pl.CostEstimate(flops=flops, bytes_accessed=moved, transcendentals=0)


def swap(value, bit):
    return lax.ppermute(value, "shard", [(i, i ^ bit) for i in range(8)])


def swap_t(value, bit):
    return lax.ppermute(value, "tensor", [(i, i ^ bit) for i in range(4)])


def swap_both(value, bit, bit_t):
    route = [(4 * s + t, 4 * (s ^ bit) + (t ^ bit_t)) for s in range(8) for t in range(4)]
    return lax.ppermute(value, ("shard", "tensor"), route)


def pick(flag, if_zero, if_one):
    return jnp.where(flag == 0, if_zero, if_one)


def encode(value, store):
    rows, width = value.shape
    powers = []
    for first in range(0, rows, GROUP):
        part = value[first : first + GROUP]
        top = jnp.max(jnp.abs(part), axis=0, keepdims=True)
        power = jnp.floor(jnp.log2(jnp.maximum(top, 1e-30)))
        scaled = jnp.clip(jnp.round(part * jnp.exp2(14.0 - power)), -32767.0, 32767.0)
        store(first, scaled.astype(jnp.int32).astype(jnp.int16))
        powers.append(power)
    powers += [jnp.zeros((1, width), f32)] * (GROUP - len(powers))
    store(rows, jnp.concatenate(powers, axis=0).astype(jnp.int32).astype(jnp.int16))


def decode(packed, rows):
    whole = packed.astype(jnp.int32).astype(f32)
    scales = jnp.exp2(whole[rows : rows + GROUP] - 14.0)
    parts = [
        whole[first : first + GROUP] * scales[first // GROUP : first // GROUP + 1]
        for first in range(0, rows, GROUP)
    ]
    return jnp.concatenate(parts, axis=0)


def encode_to(ref, index, value):
    def store(first, data):
        ref[index, first : first + GROUP, :] = data

    encode(value, store)


FINE = 8
FULL = 32767.0
STEPS = 128.0


def encode_fine(value, ref):
    rows, width = value.shape
    powers = []
    for first in range(0, rows, 2 * FINE):
        scaled = []
        for start in (first, first + FINE):
            part = value[start : start + FINE]
            top = jnp.max(jnp.abs(part), axis=0, keepdims=True)
            power = jnp.ceil(jnp.log2(jnp.maximum(top, 1e-30)) * STEPS)
            scale = jnp.exp2(power * (-1.0 / STEPS)) * FULL
            scaled.append(jnp.clip(jnp.round(part * scale), -FULL, FULL))
            powers.append(power)
        ref[first : first + 2 * FINE, :] = (
            jnp.concatenate(scaled, axis=0).astype(jnp.int32).astype(jnp.int16)
        )
    powers += [jnp.zeros((1, width), f32)] * (-len(powers) % (2 * FINE))
    for first in range(0, len(powers), 2 * FINE):
        ref[rows + first : rows + first + 2 * FINE, :] = (
            jnp.concatenate(powers[first : first + 2 * FINE], axis=0)
            .astype(jnp.int32)
            .astype(jnp.int16)
        )


def decode_fine(ref, rows):
    values = ref[:rows, :].astype(jnp.int32).astype(f32)
    powers = ref[rows:, :].astype(jnp.int32).astype(f32)
    scales = jnp.exp2(powers * (1.0 / STEPS)) * (1.0 / FULL)
    parts = [
        values[first : first + FINE] * scales[first // FINE : first // FINE + 1]
        for first in range(0, rows, FINE)
    ]
    return jnp.concatenate(parts, axis=0)


def fine_rows(rows):
    return rows + -(-(rows // FINE) // (2 * FINE)) * 2 * FINE


def base_kernel(momentum, weight, packed):
    kept = momentum_rate * momentum[...] + decay_rate * weight[...]
    encode_fine(weight[...] - learn_rate * kept, packed)


def parts_of(value):
    upper = value.astype(bf16)
    return upper, (value - upper.astype(f32)).astype(bf16)


def dot_of(left, right):
    dot = lambda p, q: jnp.dot(p, q, preferred_element_type=f32)
    small = dot(left[0], right[1]) + dot(left[1], right[0])
    return dot(left[0], right[0]) + small


def picks_kernel(group_cols, info, sampled, acts, out_grad, picks, acts_buf, grad_buf, sems):
    group = info[0]
    block = 128
    span = grad_buf.shape[1]
    tokens, cols = acts.shape
    chunk = tokens // 4
    last = out_grad.shape[1] // block - span // block
    start = pl.multiple_of(jnp.minimum((group * group_cols) // block, last) * block, block)
    copies = []
    for part in range(4):
        some = pl.ds(part * chunk, chunk)
        copies.append(
            (
                pltpu.make_async_copy(acts.at[some, :], acts_buf.at[some, :], sems.at[part]),
                pltpu.make_async_copy(
                    out_grad.at[some, pl.ds(start, span)], grad_buf.at[some, :], sems.at[4 + part]
                ),
            )
        )
        for copy in copies[-1]:
            copy.start()
    drawn = sampled.shape[1]
    row = lax.broadcasted_iota(jnp.int32, (drawn, drawn), 0)
    col = lax.broadcasted_iota(jnp.int32, (drawn, drawn), 1)
    upright = jnp.sum(jnp.where(row == col, sampled[...], 0), axis=1, keepdims=True)
    found = jnp.zeros((drawn, cols), f32)
    grads = jnp.zeros((drawn, span), f32)
    for part in range(4):
        place = lax.broadcasted_iota(jnp.int32, (drawn, chunk), 1) + part * chunk
        chosen = (place == upright).astype(bf16)
        some = slice(part * chunk, (part + 1) * chunk)
        copies[part][0].wait()
        found += jnp.dot(chosen, acts_buf[some, :], preferred_element_type=f32)
        copies[part][1].wait()
        grads += jnp.dot(chosen, grad_buf[some, :], preferred_element_type=f32)
    picks[:, :cols] = found.astype(bf16)
    pad = jnp.zeros((drawn, picks.shape[1] - cols - group_cols), f32)
    for which in range(4):
        begin = min((which * group_cols) // block, last) * block
        offset = which * group_cols - begin

        @pl.when(group == which)
        def _():
            part = jnp.concatenate([grads[:, offset : offset + group_cols], pad], axis=1)
            picks[:, cols:] = part.astype(bf16)


def split_units(group, head, width_g):
    half = group.shape[1] // 2
    mid = width_g // 2
    middle = group[head : head + width_g]
    packed = [
        jnp.concatenate([middle[:mid, cols], middle[mid:, cols]], axis=1)
        for cols in (slice(0, half), slice(half, 2 * half))
    ]
    return (
        jnp.concatenate([group[:head], packed[0]], axis=0),
        jnp.concatenate([group[head + width_g :], packed[1]], axis=0),
    )


def partial_kernel(
    group_cols, width_g, info, out_grad, acts, send_a, keep_a, send_b, keep_b, grad_buf, acts_buf,
    raw, sems
):
    side, low = info[1], info[2]
    head = 2 * width_g
    outs = out_grad.shape[1]
    half = acts.shape[1] // 2
    block = outs // 5
    first = pltpu.make_async_copy(acts, acts_buf, sems.at[5])
    first.start()
    copies = []
    for step in range(5):
        columns = pl.ds(step * block, block)
        copies.append(
            pltpu.make_async_copy(out_grad.at[:, columns], grad_buf.at[:, columns], sems.at[step])
        )
        copies[-1].start()
    first.wait()
    for step in range(5):
        copies[step].wait()
        columns = slice(step * block, (step + 1) * block)
        raw[columns, :] = jnp.dot(
            grad_buf[:, columns].T, acts_buf[...], preferred_element_type=f32
        )
        if step == 0:
            continue
        place = step - 1
        span = slice(place * group_cols, (place + 1) * group_cols)
        zero, one = split_units(raw[span, :half], head, width_g)
        keep_a[place] = jnp.where(side == 0, zero, one)
        encode_to(send_a, place, jnp.where(side == 0, one, zero))
        if place % 2 == 0:
            continue
        before = slice((place - 1) * group_cols, place * group_cols)
        zero = split_units(raw[before, half:], head, width_g)
        one = split_units(raw[span, half:], head, width_g)
        for x in range(2):
            keep_b[place - 1 + x] = jnp.where(low == 0, zero[x], one[x])
            encode_to(send_b, place - 1 + x, jnp.where(low == 0, one[x], zero[x]))


def add_kernel(bit_at, inner, info, got, held, send, keep):
    bit = info[bit_at]
    rows = held.shape[1]
    count = send.shape[0]

    def place(j, value):
        return 2 * j + value if inner else value * count + j

    for j in range(count):
        away = place(j, 1 - bit)
        encode_to(send, j, held[away] + decode(got[away], rows))
    for j in range(count):
        home = place(j, bit)
        keep[j] = held[home] + decode(got[home], rows)


def last_add_kernel(info, got_a, held_a, got_b, held_b, send, keep):
    high = info[4]
    rows = keep.shape[1]
    for piece, (got, held) in enumerate(((got_a, held_a), (got_b, held_b))):
        encode_to(send, piece, held[1 - high] + decode(got[1 - high], rows))
        keep[piece] = held[high] + decode(got[high], rows)


def add_step(info, bit_at, inner, got, held):
    count = held.shape[0] // 2
    return pl.pallas_call(
        lambda *refs: add_kernel(bit_at, inner, *refs),
        in_specs=[smem, vmem, vmem],
        out_specs=[vmem, vmem],
        out_shape=[
            shaped((count,) + got.shape[1:], jnp.int16),
            shaped((count,) + held.shape[1:], f32),
        ],
        compiler_params=params(24),
        name="add",
    )(info, got, held)


def block_places(count_a, width_a, count_g, width_g):
    blocks, column, row = [], 0, 0
    for is_a, count, width in ((True, count_a, width_a), (False, count_g, width_g)):
        for place in range(count):
            blocks.append((is_a, place, width, column, row))
            column += width
            row += width + GROUP
    return blocks, row


def stats_kernel(blocks, info, own, one, two, packed, picks):
    place = 2 * info[4] + info[1]
    picks[place] = own[...]
    picks[place ^ 2] = one[...]
    picks[place ^ 1] = two[0]
    picks[place ^ 3] = two[1]
    everything = picks[...].reshape(picks.shape[0] * picks.shape[1], picks.shape[2])
    for _, _, width, column, row in blocks:
        rows = everything[:, column : column + width]
        stats = lax.dot_general(
            rows, rows, (((0,), (0,)), ((), ())), preferred_element_type=f32
        )
        missing = packed.shape[1] - width
        if missing:
            stats = jnp.concatenate([stats, jnp.zeros((width, missing), f32)], axis=1)

        def store(first, data):
            packed[row + first : row + first + GROUP, :] = data

        encode(stats, store)


def factor_kernel(
    share, blocks, info, own_a, own_g, packed, got, a_state, g_state, a_new, g_new, inv_a, needed,
    inv_g
):
    group = info[0]
    count_a, count_g = a_state.shape[0], g_state.shape[0]
    errors, inverses, scales = [], [], []
    for is_a, place, width, _, first in blocks:
        span = slice(first, first + width + GROUP)
        stats = decode(packed[span, :], width) + decode(got[span, :], width)
        stats = stats[:, :width]
        slot = own_a[group, place] if is_a else own_g[group, place]
        stored = (a_state if is_a else g_state)[slot]
        factor = factor_decay * stored + share * stats
        (a_new if is_a else g_new)[slot] = factor
        row = lax.broadcasted_iota(jnp.int32, (width, width), 0)
        col = lax.broadcasted_iota(jnp.int32, (width, width), 1)
        identity = (row == col).astype(f32)
        trace = jnp.sum(factor * identity) / width
        damped = factor + (damping_rate * trace) * identity
        bound = jnp.max(jnp.sum(jnp.abs(damped), axis=0))
        error = identity - damped / bound
        errors.append(error)
        inverses.append(identity + error)
        scales.append(bound)
    every = range(count_a + count_g)
    errors = [parts_of(errors[i]) for i in every]
    errors = [parts_of(dot_of(errors[i], errors[i])) for i in every]
    for step in range(1, NS_IT - 1):
        grown = [dot_of(parts_of(inverses[i]), errors[i]) for i in every]
        squares = [dot_of(errors[i], errors[i]) for i in every]
        inverses = [inverses[i] + grown[i] for i in every]
        errors = [parts_of(squares[i]) for i in every]
    grown = [dot_of(parts_of(inverses[i]), errors[i]) for i in every]
    inverses = [(inverses[i] + grown[i]) / scales[i] for i in every]
    for index in every:
        if index < count_a:
            inv_a[index] = inverses[index]
        else:
            inv_g[index - count_a] = inverses[index]
    side = info[1]
    for index, place in enumerate((3 * side, 1 + 3 * side, 2)):
        encode_to(needed, index, inv_g[place])


def precon_kernel(info, got, held, inv_g, inv_a, top, mid, total, coded):
    side = info[1]
    width_g, width_a = inv_g.shape[-1], inv_a.shape[-1]
    half = width_g // 2
    dot = lambda p, q: dot_of(parts_of(p), parts_of(q))
    left = [decode(inv_g[place], width_g) for place in range(3)]
    squares = jnp.zeros((width_g, width_a), f32)
    for piece in range(2):
        part = held[piece] + decode(got[piece], held.shape[1])
        for place in range(2):
            for block in range(2):
                values = dot(
                    left[place],
                    part[
                        place * width_g : (place + 1) * width_g,
                        block * width_a : (block + 1) * width_a,
                    ],
                )
                values = dot(values, inv_a[2 * piece + block])
                squares += values * values
                column = (2 * piece + block) * width_a
                top[place * width_g : (place + 1) * width_g, column : column + width_a] = values
        packed = part[2 * width_g : 2 * width_g + half, :]
        values = jnp.concatenate([packed[:, :width_a], packed[:, width_a:]], axis=0)
        values = dot(dot(left[2], values), inv_a[2 * piece + side])
        squares += values * values
        mid[:, piece * width_a : (piece + 1) * width_a] = values
    total[...] = jnp.full(total.shape, jnp.sum(squares), f32)
    encode_fine(top[...], coded)


def middle_kernel(info, middle, got, total, along_y, along_both, rest, packed, sums):
    mid, cols = rest.shape
    quarter = cols // 4
    sums[...] = (total[...] + got[mid:, :]) + (along_y[...] + along_both[...])
    for x in range(2):

        @pl.when(info[1] == x)
        def _():
            own = middle[mid * x : mid * (x + 1), :]
            pairs = []
            for piece in range(2):
                columns = slice(piece * quarter, (piece + 1) * quarter)
                both = [own[:, columns], got[:mid, columns]]
                pairs += both if x == 0 else both[::-1]
            rest[...] = jnp.concatenate(pairs, axis=1)

    encode_fine(rest[...], packed)


def update_kernel(
    entries, info, total, along_l, along_h, along_both, top, rest, momentum, weight, base, base_far,
    scaled, scaled_far, small, small_far, momentum_new, weight_new, rounded_a, rounded_b
):
    rows, cols = momentum.shape
    half = cols // 2
    head, mid = top.shape[0], rest.shape[0]
    sums = [each[0:1, :] for each in (total, along_l, along_h, along_both)]
    mean_sq = ((sums[0] + sums[1]) + (sums[2] + sums[3])) / entries
    factor = 1.0 / jnp.sqrt(mean_sq + epsilon_sq)
    factor = jnp.concatenate([factor, factor], axis=1)
    fixed = [decode_fine(base, rows), decode_fine(base_far, rows)]
    moving = [
        (decode_fine(scaled, head), decode_fine(small, mid)),
        (decode_fine(scaled_far, head), decode_fine(small_far, mid)),
    ]

    def step(order):
        precon = jnp.concatenate([(top, rest)[which][...] for which in order], axis=0)
        moved = momentum_rate * momentum[...] + precon * factor + decay_rate * weight[...]
        momentum_new[...] = moved
        weight_new[...] = weight[...] - learn_rate * moved
        for place in range(2):
            change = jnp.concatenate([moving[place][which] for which in order], axis=0)
            fresh = fixed[place] - (learn_rate * factor) * change
            rounded_a[place] = fresh[:, :half].astype(bf16)
            rounded_b[place] = fresh[:, half:].astype(bf16)

    for x, order in enumerate(((0, 1), (1, 0))):

        @pl.when(info[1] == x)
        def _():
            step(order)


def place_kernel(rows, info, *refs):
    parts, out = refs[:6], refs[6]
    shard = info[3]
    half = out.shape[1] // 2
    codes = ((0, 4), (2, 6), (1, 5, 3, 7), (0, 4), (1, 5), (2, 6, 3, 7))
    for index, (part, units) in enumerate(zip(parts, codes)):
        first = half * (index // 3)
        for place, code in enumerate(units):
            start = pl.multiple_of((shard ^ code) * rows, 16)
            out[pl.ds(start, rows), first : first + half] = part[place]


def fast(acts, out_grad, sample_rows, own_a, own_g, a_state, g_state, momentum, weight):
    shard_pos = lax.axis_index("shard")
    tensor_pos = lax.axis_index("tensor")
    side, low, high = shard_pos & 1, (shard_pos >> 1) & 1, shard_pos >> 2
    count_a, width_a = a_state.shape[1], a_state.shape[2]
    count_g, width_g = g_state.shape[1], g_state.shape[2]
    group_cols = count_g * width_g
    tokens, cols = acts.shape
    outs = out_grad.shape[1]
    rows = momentum.shape[0]
    drawn = sample_rows.shape[0]
    samples = drawn * 8
    share = (1.0 - factor_decay) / samples
    half = cols // 2
    head = 2 * width_g
    mid = width_g // 2
    info = jnp.stack([tensor_pos, side, low, shard_pos, high])

    send_a, keep_a, send_b, keep_b = pl.pallas_call(
        lambda *refs: partial_kernel(group_cols, width_g, *refs),
        in_specs=[smem, main, main],
        out_specs=[vmem] * 4,
        out_shape=[
            shaped((4, rows + GROUP, half), jnp.int16),
            shaped((4, rows, half), f32),
        ]
        * 2,
        scratch_shapes=[
            pltpu.VMEM((tokens, outs), bf16),
            pltpu.VMEM((tokens, cols), bf16),
            pltpu.VMEM((outs, cols), f32),
            pltpu.SemaphoreType.DMA((6,)),
        ],
        compiler_params=params(56),
        name="partial",
    )(info, out_grad, acts)
    sample_rows, send_a, send_b = lax.optimization_barrier((sample_rows, send_a, send_b))
    got_a = swap(send_a, 1)
    got_b = swap(send_b, 2)

    wide = cols + -(-group_cols // 128) * 128
    picks = pl.pallas_call(
        lambda *refs: picks_kernel(group_cols, *refs),
        in_specs=[smem, vmem, main, main],
        out_specs=vmem,
        out_shape=shaped((drawn, wide), bf16),
        scratch_shapes=[
            pltpu.VMEM((tokens, cols), bf16),
            pltpu.VMEM((tokens, 640), bf16),
            pltpu.SemaphoreType.DMA((8,)),
        ],
        compiler_params=params(60),
        name="picks",
    )(info, sample_rows.reshape(1, -1), acts, out_grad)
    one = swap(picks, 4)

    base = pl.pallas_call(
        base_kernel,
        in_specs=[vmem, vmem],
        out_specs=vmem,
        out_shape=shaped((fine_rows(rows), cols), jnp.int16),
        compiler_params=params(16),
        name="base",
    )(momentum, weight)
    base_far = swap(base, 4)
    two = swap(jnp.stack([picks, one]), 1)

    send_a, keep_a = add_step(info, 2, True, got_a, keep_a)
    got_a = swap(send_a, 2)
    blocks, packed_rows = block_places(count_a, width_a, count_g, width_g)
    packed = pl.pallas_call(
        lambda *refs: stats_kernel(blocks, *refs),
        in_specs=[smem] + [vmem] * 3,
        out_specs=vmem,
        out_shape=shaped((packed_rows, width_a), jnp.int16),
        scratch_shapes=[pltpu.VMEM((4, drawn, wide), bf16)],
        compiler_params=params(16),
        name="stats",
    )(info, picks, one, two)
    got_packed = swap(packed, 2)
    got_b, base_far = lax.optimization_barrier((got_b, base_far))
    send_b, keep_b = add_step(info, 1, True, got_b, keep_b)
    got_b = swap(send_b, 1)

    send, keep = pl.pallas_call(
        last_add_kernel,
        in_specs=[smem] + [vmem] * 4,
        out_specs=[vmem, vmem],
        out_shape=[
            shaped((2, rows + GROUP, half), jnp.int16),
            shaped((2, rows, half), f32),
        ],
        compiler_params=params(24),
        name="last_add",
    )(info, got_a, keep_a, got_b, keep_b)
    got = swap(send, 4)

    new_a, new_g, inv_a, needed = pl.pallas_call(
        lambda *refs: factor_kernel(share, blocks, *refs),
        in_specs=[smem] * 3 + [vmem] * 4,
        out_specs=[vmem] * 4,
        out_shape=[
            shaped(a_state.shape[1:], f32),
            shaped(g_state.shape[1:], f32),
            shaped(a_state.shape[1:], f32),
            shaped((3, width_g + GROUP, width_g), jnp.int16),
        ],
        scratch_shapes=[pltpu.VMEM(g_state.shape[1:], f32)],
        compiler_params=params(24),
        name="factors",
    )(info, own_a, own_g, packed, got_packed, a_state[0], g_state[0])
    route = [
        ((2 * a + b) * 4 + c, (2 * c + b) * 4 + a)
        for a in range(4)
        for b in range(2)
        for c in range(4)
    ]
    inv_rows = lax.ppermute(needed, ("shard", "tensor"), route)

    top, middle, total, scaled = pl.pallas_call(
        precon_kernel,
        in_specs=[smem] + [vmem] * 4,
        out_specs=[vmem] * 4,
        out_shape=[
            shaped((head, cols), f32),
            shaped((width_g, half), f32),
            shaped((8, half), f32),
            shaped((fine_rows(head), cols), jnp.int16),
        ],
        compiler_params=params(24),
        name="precon",
    )(info, got, keep, inv_rows, inv_a)

    scaled_far = swap(scaled, 4)
    give = pick(side, middle[mid:], middle[:mid])
    got = swap(jnp.concatenate([give, total], axis=0), 1)
    along_y = swap_t(total, 2)
    along_both = swap_both(total, 1, 2)
    rest, small, total = pl.pallas_call(
        middle_kernel,
        in_specs=[smem] + [vmem] * 5,
        out_specs=[vmem] * 3,
        out_shape=[
            shaped((mid, cols), f32),
            shaped((fine_rows(mid), cols), jnp.int16),
            shaped((8, half), f32),
        ],
        compiler_params=params(16),
        name="middle",
    )(info, middle, got, total, along_y, along_both)
    small_far = swap(small, 4)
    total = total + swap_t(total, 1)
    others = [swap(total, bits) for bits in (2, 4, 6)]
    momentum_new, weight_new, rounded_a, rounded_b = pl.pallas_call(
        lambda *refs: update_kernel(rows * 8 * cols * 4, *refs),
        in_specs=[smem] + [vmem] * 14,
        out_specs=[vmem] * 4,
        out_shape=[
            shaped((rows, cols), f32),
            shaped((rows, cols), f32),
            shaped((2, rows, half), bf16),
            shaped((2, rows, half), bf16),
        ],
        compiler_params=params(24),
        name="update",
    )(
        info, total, *others, top, rest, momentum, weight, base, base_far, scaled, scaled_far,
        small, small_far,
    )

    along_l = swap(rounded_a, 2)
    along_x = swap(rounded_b, 1)
    rest_a = swap(jnp.concatenate([rounded_a, along_l]), 1)
    rest_b = swap(jnp.concatenate([rounded_b, along_x]), 2)
    gathered = pl.pallas_call(
        lambda *refs: place_kernel(rows, *refs),
        in_specs=[smem] + [vmem] * 6,
        out_specs=vmem,
        out_shape=shaped((rows * 8, cols), bf16),
        compiler_params=params(16),
        name="place",
    )(info, rounded_a, along_l, rest_a, rounded_b, along_x, rest_b)
    return (new_a[None], new_g[None], momentum_new, weight_new, gathered)


def local(acts, out_grad, sample_rows, own_a, own_g, a_state, g_state, momentum, weight):
    shapes_fit = (
        lax.axis_size("shard") == 8
        and lax.axis_size("tensor") == 4
        and a_state.shape[1:] == (4, 128, 128)
        and g_state.shape[1:] == (5, 96, 96)
    )
    plan = fast if shapes_fit else general
    return plan(acts, out_grad, sample_rows, own_a, own_g, a_state, g_state, momentum, weight)


def solution(mesh):
    return jax.shard_map(
        local,
        mesh=mesh,
        in_specs=(
            P("shard", "tensor"),
            P("shard", None),
            P("shard"),
            P(),
            P(),
            P("tensor", None, None, None),
            P("tensor", None, None, None),
            P("shard", "tensor"),
            P("shard", "tensor"),
        ),
        out_specs=(
            P("tensor", None, None, None),
            P("tensor", None, None, None),
            P("shard", "tensor"),
            P("shard", "tensor"),
            P(None, "tensor"),
        ),
        check_vma=False,
    )
```

```python
import jax
import jax.numpy as jnp
from jax import lax
from jax.experimental import pallas as pl
from jax.experimental.pallas import tpu as pltpu
from jax.sharding import PartitionSpec as P

NS_IT = 5


factor_decay = 0.8
damping_rate = 0.03
momentum_rate = 0.9
decay_rate = 0.01
learn_rate = 0.05
epsilon_sq = 1e-06
highest = lax.Precision.HIGHEST
f32 = jnp.float32
bf16 = jnp.bfloat16


def newton_inverse(factor):
    width = factor.shape[-1]
    identity = jnp.eye(width, dtype=jnp.float32)
    trace_mean = jnp.trace(factor, axis1=-2, axis2=-1) / width
    damped = factor + damping_rate * trace_mean[:, None, None] * identity
    bound = jnp.max(jnp.sum(jnp.abs(damped), axis=-1), axis=-1)
    guess = identity[None] / bound[:, None, None]
    for iteration in range(NS_IT):
        product = jnp.einsum("bij,bjk->bik", damped, guess, precision=highest)
        guess = jnp.einsum("bij,bjk->bik", guess, 2.0 * identity - product, precision=highest)
    return guess


def local_stats(rows, width):
    blocks = rows.reshape(rows.shape[0], -1, width)
    return jnp.einsum("sbi,sbj->bij", blocks, blocks, preferred_element_type=jnp.float32)


def owner_part(slots, shard_pos, shard_count):
    count = slots.shape[0]
    stride = shard_count // count
    slot_pos = jnp.minimum(shard_pos // stride, count - 1)
    mine = lax.dynamic_index_in_dim(slots, slot_pos, 0, keepdims=True)
    inverse = newton_inverse(mine)
    marker = (jnp.arange(count, dtype=jnp.int32) * stride == shard_pos).astype(jnp.float32)
    return marker[:, None, None] * inverse


def general(acts, out_grad, sample_rows, own_a, own_g, a_state, g_state, momentum, weight):
    shard_count = lax.axis_size("shard")
    tensor_count = lax.axis_size("tensor")
    shard_pos = lax.axis_index("shard")
    tensor_pos = lax.axis_index("tensor")
    block_a = a_state.shape[-1]
    block_g = g_state.shape[-1]
    samples = sample_rows.shape[0] * shard_count
    fresh_share = (1.0 - factor_decay) / samples
    picked_a = jnp.take(acts, sample_rows, axis=0)
    picked_g = jnp.take(out_grad, sample_rows, axis=0)
    group_cols = out_grad.shape[1] // tensor_count
    picked_g = lax.dynamic_slice_in_dim(picked_g, tensor_pos * group_cols, group_cols, 1)
    stats_a = local_stats(picked_a, block_a)
    stats_g = local_stats(picked_g, block_g)
    row_a = lax.dynamic_index_in_dim(own_a, tensor_pos, 0, keepdims=False)
    row_g = lax.dynamic_index_in_dim(own_g, tensor_pos, 0, keepdims=False)
    select_a = (row_a[None, :] == jnp.arange(row_a.shape[0], dtype=jnp.int32)[:, None]).astype(
        jnp.float32
    )
    select_g = (row_g[None, :] == jnp.arange(row_g.shape[0], dtype=jnp.int32)[:, None]).astype(
        jnp.float32
    )
    summed_a, summed_g = lax.psum((fresh_share * stats_a, fresh_share * stats_g), "shard")
    stored_a = jnp.einsum("sb,sij->bij", select_a, a_state[0], precision=highest)
    stored_g = jnp.einsum("sb,sij->bij", select_g, g_state[0], precision=highest)
    fac_a = factor_decay * stored_a + summed_a
    fac_g = factor_decay * stored_g + summed_g
    slots_a = jnp.einsum("sb,bij->sij", select_a, fac_a, precision=highest)
    slots_g = jnp.einsum("sb,bij->sij", select_g, fac_g, precision=highest)
    new_a_state = slots_a[None]
    new_g_state = slots_g[None]
    slot_inv_a, slot_inv_g = lax.psum(
        (owner_part(slots_a, shard_pos, shard_count), owner_part(slots_g, shard_pos, shard_count)),
        "shard",
    )
    inv_a = jnp.einsum("sb,sij->bij", select_a, slot_inv_a, precision=highest)
    local_inv_g = jnp.einsum("sb,sij->bij", select_g, slot_inv_g, precision=highest)
    inv_g = lax.all_gather(local_inv_g, "tensor", axis=0, tiled=True)
    raw_product = lax.dot_general(
        out_grad, acts, (((0,), (0,)), ((), ())), preferred_element_type=jnp.float32
    )
    left_done = jnp.einsum(
        "bij,bjd->bid", inv_g, raw_product.reshape(inv_g.shape[0], block_g, -1), precision=highest
    ).reshape(raw_product.shape)
    owned_rows = lax.psum_scatter(left_done, "shard", scatter_dimension=0, tiled=True)
    precon = jnp.einsum(
        "qbi,bij->qbj",
        owned_rows.reshape(owned_rows.shape[0], -1, block_a),
        inv_a,
        precision=highest,
    ).reshape(owned_rows.shape)
    square_total = lax.psum(jnp.sum(precon * precon), ("shard", "tensor"))
    mean_sq = square_total / (momentum.shape[0] * shard_count * momentum.shape[1] * tensor_count)
    update = precon / jnp.sqrt(mean_sq + epsilon_sq)
    momentum_new = momentum_rate * momentum + update + decay_rate * weight
    weight_new = weight - learn_rate * momentum_new
    gathered = lax.all_gather(weight_new.astype(jnp.bfloat16), "shard", axis=0, tiled=True)
    return (new_a_state, new_g_state, momentum_new, weight_new, gathered)


GROUP = 16
vmem = pl.BlockSpec(memory_space=pltpu.VMEM)
smem = pl.BlockSpec(memory_space=pltpu.SMEM)
main = pl.BlockSpec(memory_space=pl.ANY)


def params(mib):
    return pltpu.CompilerParams(vmem_limit_bytes=mib * 2**20)


def shaped(shape, kind):
    return jax.ShapeDtypeStruct(shape, kind)


def cost(flops, moved):
    return pl.CostEstimate(flops=flops, bytes_accessed=moved, transcendentals=0)


def swap(value, bit):
    return lax.ppermute(value, "shard", [(i, i ^ bit) for i in range(8)])


def swap_t(value, bit):
    return lax.ppermute(value, "tensor", [(i, i ^ bit) for i in range(4)])


def swap_both(value, bit, bit_t):
    route = [(4 * s + t, 4 * (s ^ bit) + (t ^ bit_t)) for s in range(8) for t in range(4)]
    return lax.ppermute(value, ("shard", "tensor"), route)


def pick(flag, if_zero, if_one):
    return jnp.where(flag == 0, if_zero, if_one)


def encode(value, store):
    rows, width = value.shape
    powers = []
    for first in range(0, rows, GROUP):
        part = value[first : first + GROUP]
        top = jnp.max(jnp.abs(part), axis=0, keepdims=True)
        power = jnp.floor(jnp.log2(jnp.maximum(top, 1e-30)))
        scaled = jnp.clip(jnp.round(part * jnp.exp2(14.0 - power)), -32767.0, 32767.0)
        store(first, scaled.astype(jnp.int32).astype(jnp.int16))
        powers.append(power)
    powers += [jnp.zeros((1, width), f32)] * (GROUP - len(powers))
    store(rows, jnp.concatenate(powers, axis=0).astype(jnp.int32).astype(jnp.int16))


def decode(packed, rows):
    whole = packed.astype(jnp.int32).astype(f32)
    scales = jnp.exp2(whole[rows : rows + GROUP] - 14.0)
    parts = [
        whole[first : first + GROUP] * scales[first // GROUP : first // GROUP + 1]
        for first in range(0, rows, GROUP)
    ]
    return jnp.concatenate(parts, axis=0)


def encode_to(ref, index, value):
    def store(first, data):
        ref[index, first : first + GROUP, :] = data

    encode(value, store)


FINE = 8
FULL = 32767.0
STEPS = 128.0


def encode_fine(value, ref):
    rows, width = value.shape
    powers = []
    for first in range(0, rows, 2 * FINE):
        scaled = []
        for start in (first, first + FINE):
            part = value[start : start + FINE]
            top = jnp.max(jnp.abs(part), axis=0, keepdims=True)
            power = jnp.ceil(jnp.log2(jnp.maximum(top, 1e-30)) * STEPS)
            scale = jnp.exp2(power * (-1.0 / STEPS)) * FULL
            scaled.append(jnp.clip(jnp.round(part * scale), -FULL, FULL))
            powers.append(power)
        ref[first : first + 2 * FINE, :] = (
            jnp.concatenate(scaled, axis=0).astype(jnp.int32).astype(jnp.int16)
        )
    powers += [jnp.zeros((1, width), f32)] * (-len(powers) % (2 * FINE))
    for first in range(0, len(powers), 2 * FINE):
        ref[rows + first : rows + first + 2 * FINE, :] = (
            jnp.concatenate(powers[first : first + 2 * FINE], axis=0)
            .astype(jnp.int32)
            .astype(jnp.int16)
        )


def decode_fine(ref, rows):
    values = ref[:rows, :].astype(jnp.int32).astype(f32)
    powers = ref[rows:, :].astype(jnp.int32).astype(f32)
    scales = jnp.exp2(powers * (1.0 / STEPS)) * (1.0 / FULL)
    parts = [
        values[first : first + FINE] * scales[first // FINE : first // FINE + 1]
        for first in range(0, rows, FINE)
    ]
    return jnp.concatenate(parts, axis=0)


def fine_rows(rows):
    return rows + -(-(rows // FINE) // (2 * FINE)) * 2 * FINE


def fold(rows):
    half = rows.shape[0] // 2
    return jnp.concatenate([rows[:half], rows[half:]], axis=1)


def fold(rows):
    half = rows.shape[0] // 2
    return jnp.concatenate([rows[:half], rows[half:]], axis=1)


def base_kernel(momentum, weight, packed):
    kept = momentum_rate * momentum[...] + decay_rate * weight[...]
    encode_fine(weight[...] - learn_rate * kept, packed)


def shared_rows(side, head, mid):
    return slice(head * (1 - side), head * (1 - side) + mid)


def kept_columns(value, side):
    quarter = value.shape[1] // 4
    blocks = [value[:, (2 * p + side) * quarter : (2 * p + side + 1) * quarter] for p in (0, 1)]
    return jnp.concatenate(blocks, axis=1)


def side_kernel(head, mid, info, own, far, give):
    rows = head + mid
    for x in range(2):

        @pl.when(info[1] == x)
        def _():
            span = shared_rows(x, head, mid)
            first = span.start // FINE
            for place, packed in enumerate((own, far)):
                values = packed[:rows, :].astype(jnp.int32)[span]
                powers = packed[rows:, :].astype(jnp.int32)[first : first + mid // FINE]
                missing = jnp.zeros((2 * FINE - powers.shape[0], powers.shape[1]), jnp.int32)
                all_rows = jnp.concatenate([values, powers, missing], axis=0)
                give[place] = kept_columns(all_rows, 1 - x).astype(jnp.int16)


def pack_kernel(head, mid, info, own, far, got, units):
    for x in range(2):

        @pl.when(info[1] == x)
        def _():
            for place, packed in enumerate((own, far)):
                values = decode_fine(packed, head + mid)
                shared = kept_columns(values[shared_rows(x, head, mid)], x)
                other = decode_fine(got.at[place], mid)
                both = (shared, other) if x == 0 else (other, shared)
                quarter = shared.shape[1] // 2
                pairs = []
                for piece in range(2):
                    pairs += [each[:, piece * quarter : (piece + 1) * quarter] for each in both]
                units[place, :head, :] = values[mid * x : mid * x + head]
                units[place, head:, :] = jnp.concatenate(pairs, axis=1)


def parts_of(value):
    upper = value.astype(bf16)
    return upper, (value - upper.astype(f32)).astype(bf16)


def dot_of(left, right):
    dot = lambda p, q: jnp.dot(p, q, preferred_element_type=f32)
    small = dot(left[0], right[1]) + dot(left[1], right[0])
    return dot(left[0], right[0]) + small


def picks_kernel(group_cols, info, sampled, acts, out_grad, picks, acts_buf, grad_buf, sems):
    group = info[0]
    block = 128
    span = grad_buf.shape[1]
    tokens, cols = acts.shape
    chunk = tokens // 4
    last = out_grad.shape[1] // block - span // block
    start = pl.multiple_of(jnp.minimum((group * group_cols) // block, last) * block, block)
    copies = []
    for part in range(4):
        some = pl.ds(part * chunk, chunk)
        copies.append(
            (
                pltpu.make_async_copy(acts.at[some, :], acts_buf.at[some, :], sems.at[part]),
                pltpu.make_async_copy(
                    out_grad.at[some, pl.ds(start, span)], grad_buf.at[some, :], sems.at[4 + part]
                ),
            )
        )
        for copy in copies[-1]:
            copy.start()
    drawn = sampled.shape[1]
    row = lax.broadcasted_iota(jnp.int32, (drawn, drawn), 0)
    col = lax.broadcasted_iota(jnp.int32, (drawn, drawn), 1)
    upright = jnp.sum(jnp.where(row == col, sampled[...], 0), axis=1, keepdims=True)
    found = jnp.zeros((drawn, cols), f32)
    grads = jnp.zeros((drawn, span), f32)
    for part in range(4):
        place = lax.broadcasted_iota(jnp.int32, (drawn, chunk), 1) + part * chunk
        chosen = (place == upright).astype(bf16)
        some = slice(part * chunk, (part + 1) * chunk)
        copies[part][0].wait()
        found += jnp.dot(chosen, acts_buf[some, :], preferred_element_type=f32)
        copies[part][1].wait()
        grads += jnp.dot(chosen, grad_buf[some, :], preferred_element_type=f32)
    picks[:, :cols] = found.astype(bf16)
    pad = jnp.zeros((drawn, picks.shape[1] - cols - group_cols), f32)
    for which in range(4):
        begin = min((which * group_cols) // block, last) * block
        offset = which * group_cols - begin

        @pl.when(group == which)
        def _():
            part = jnp.concatenate([grads[:, offset : offset + group_cols], pad], axis=1)
            picks[:, cols:] = part.astype(bf16)


def split_units(group, head, width_g):
    half = group.shape[1] // 2
    mid = width_g // 2
    middle = group[head : head + width_g]
    packed = [
        jnp.concatenate([middle[:mid, cols], middle[mid:, cols]], axis=1)
        for cols in (slice(0, half), slice(half, 2 * half))
    ]
    return (
        jnp.concatenate([group[:head], packed[0]], axis=0),
        jnp.concatenate([group[head + width_g :], packed[1]], axis=0),
    )


def partial_kernel(
    group_cols, width_g, info, out_grad, acts, send_a, keep_a, send_b, keep_b, grad_buf, acts_buf,
    raw, sems
):
    side, low = info[1], info[2]
    head = 2 * width_g
    outs = out_grad.shape[1]
    half = acts.shape[1] // 2
    block = outs // 5
    first = pltpu.make_async_copy(acts, acts_buf, sems.at[5])
    first.start()
    copies = []
    for step in range(5):
        columns = pl.ds(step * block, block)
        copies.append(
            pltpu.make_async_copy(out_grad.at[:, columns], grad_buf.at[:, columns], sems.at[step])
        )
        copies[-1].start()
    first.wait()
    for step in range(5):
        copies[step].wait()
        columns = slice(step * block, (step + 1) * block)
        raw[columns, :] = jnp.dot(
            grad_buf[:, columns].T, acts_buf[...], preferred_element_type=f32
        )
        if step == 0:
            continue
        place = step - 1
        span = slice(place * group_cols, (place + 1) * group_cols)
        zero, one = split_units(raw[span, :half], head, width_g)
        keep_a[place] = jnp.where(side == 0, zero, one)
        encode_to(send_a, place, jnp.where(side == 0, one, zero))
        if place % 2 == 0:
            continue
        before = slice((place - 1) * group_cols, place * group_cols)
        zero = split_units(raw[before, half:], head, width_g)
        one = split_units(raw[span, half:], head, width_g)
        for x in range(2):
            keep_b[place - 1 + x] = jnp.where(low == 0, zero[x], one[x])
            encode_to(send_b, place - 1 + x, jnp.where(low == 0, one[x], zero[x]))


def add_kernel(bit_at, inner, info, got, held, send, keep):
    bit = info[bit_at]
    rows = held.shape[1]
    count = send.shape[0]

    def place(j, value):
        return 2 * j + value if inner else value * count + j

    for j in range(count):
        away = place(j, 1 - bit)
        encode_to(send, j, held[away] + decode(got[away], rows))
    for j in range(count):
        home = place(j, bit)
        keep[j] = held[home] + decode(got[home], rows)


def last_add_kernel(info, got_a, held_a, got_b, held_b, send, keep):
    high = info[4]
    rows = keep.shape[1]
    for piece, (got, held) in enumerate(((got_a, held_a), (got_b, held_b))):
        encode_to(send, piece, held[1 - high] + decode(got[1 - high], rows))
        keep[piece] = held[high] + decode(got[high], rows)


def add_step(info, bit_at, inner, got, held):
    count = held.shape[0] // 2
    return pl.pallas_call(
        lambda *refs: add_kernel(bit_at, inner, *refs),
        in_specs=[smem, vmem, vmem],
        out_specs=[vmem, vmem],
        out_shape=[
            shaped((count,) + got.shape[1:], jnp.int16),
            shaped((count,) + held.shape[1:], f32),
        ],
        compiler_params=params(24),
        name="add",
    )(info, got, held)


def block_places(count_a, width_a, count_g, width_g):
    blocks, column, row = [], 0, 0
    for is_a, count, width in ((True, count_a, width_a), (False, count_g, width_g)):
        for place in range(count):
            blocks.append((is_a, place, width, column, row))
            column += width
            row += width + GROUP
    return blocks, row


def stats_kernel(blocks, info, own, one, two, packed, picks):
    place = 2 * info[4] + info[1]
    picks[place] = own[...]
    picks[place ^ 2] = one[...]
    picks[place ^ 1] = two[0]
    picks[place ^ 3] = two[1]
    everything = picks[...].reshape(picks.shape[0] * picks.shape[1], picks.shape[2])
    for _, _, width, column, row in blocks:
        rows = everything[:, column : column + width]
        stats = lax.dot_general(
            rows, rows, (((0,), (0,)), ((), ())), preferred_element_type=f32
        )
        missing = packed.shape[1] - width
        if missing:
            stats = jnp.concatenate([stats, jnp.zeros((width, missing), f32)], axis=1)

        def store(first, data):
            packed[row + first : row + first + GROUP, :] = data

        encode(stats, store)


def factor_kernel(
    share, blocks, info, own_a, own_g, packed, got, a_state, g_state, a_new, g_new, inv_a, needed,
    inv_g
):
    group = info[0]
    count_a, count_g = a_state.shape[0], g_state.shape[0]
    errors, inverses, scales = [], [], []
    for is_a, place, width, _, first in blocks:
        span = slice(first, first + width + GROUP)
        stats = decode(packed[span, :], width) + decode(got[span, :], width)
        stats = stats[:, :width]
        slot = own_a[group, place] if is_a else own_g[group, place]
        stored = (a_state if is_a else g_state)[slot]
        factor = factor_decay * stored + share * stats
        (a_new if is_a else g_new)[slot] = factor
        row = lax.broadcasted_iota(jnp.int32, (width, width), 0)
        col = lax.broadcasted_iota(jnp.int32, (width, width), 1)
        identity = (row == col).astype(f32)
        trace = jnp.sum(factor * identity) / width
        damped = factor + (damping_rate * trace) * identity
        bound = jnp.max(jnp.sum(jnp.abs(damped), axis=0))
        error = identity - damped / bound
        errors.append(error)
        inverses.append(identity + error)
        scales.append(bound)
    every = range(count_a + count_g)
    errors = [parts_of(errors[i]) for i in every]
    errors = [parts_of(dot_of(errors[i], errors[i])) for i in every]
    for step in range(1, NS_IT - 1):
        grown = [dot_of(parts_of(inverses[i]), errors[i]) for i in every]
        squares = [dot_of(errors[i], errors[i]) for i in every]
        inverses = [inverses[i] + grown[i] for i in every]
        errors = [parts_of(squares[i]) for i in every]
    grown = [dot_of(parts_of(inverses[i]), errors[i]) for i in every]
    inverses = [(inverses[i] + grown[i]) / scales[i] for i in every]
    for index in every:
        if index < count_a:
            inv_a[index] = inverses[index]
        else:
            inv_g[index - count_a] = inverses[index]
    side = info[1]
    for index, place in enumerate((3 * side, 1 + 3 * side, 2)):
        encode_to(needed, index, inv_g[place])


def precon_kernel(info, got, held, inv_g, inv_a, top, mid, total, coded):
    side = info[1]
    width_g, width_a = inv_g.shape[-1], inv_a.shape[-1]
    half = width_g // 2
    dot = lambda p, q: dot_of(parts_of(p), parts_of(q))
    left = [decode(inv_g[place], width_g) for place in range(3)]
    squares = jnp.zeros((width_g, width_a), f32)
    for piece in range(2):
        part = held[piece] + decode(got[piece], held.shape[1])
        for place in range(2):
            for block in range(2):
                values = dot(
                    left[place],
                    part[
                        place * width_g : (place + 1) * width_g,
                        block * width_a : (block + 1) * width_a,
                    ],
                )
                values = dot(values, inv_a[2 * piece + block])
                squares += values * values
                column = (2 * piece + block) * width_a
                top[place * width_g : (place + 1) * width_g, column : column + width_a] = values
        packed = part[2 * width_g : 2 * width_g + half, :]
        values = jnp.concatenate([packed[:, :width_a], packed[:, width_a:]], axis=0)
        values = dot(dot(left[2], values), inv_a[2 * piece + side])
        squares += values * values
        mid[:, piece * width_a : (piece + 1) * width_a] = values
    total[...] = jnp.full(total.shape, jnp.sum(squares), f32)
    width = mid.shape[1] // 2
    folded = [fold(mid[:, :width]), fold(mid[:, width:])]
    unit = jnp.concatenate([top[...], jnp.concatenate(folded, axis=1)], axis=0)
    encode_fine(unit, coded)


def round_kernel(
    entries, total, along_l, along_h, along_both, base, scaled, scaled_far, factor,
    rounded_a, rounded_b
):
    rows, half = rounded_a.shape[1:]
    sums = [each[0:1, :] for each in (total, along_l, along_h, along_both)]
    mean_sq = ((sums[0] + sums[1]) + (sums[2] + sums[3])) / entries
    norm = 1.0 / jnp.sqrt(mean_sq + epsilon_sq)
    norm = jnp.concatenate([norm, norm], axis=1)
    factor[...] = jnp.broadcast_to(norm, factor.shape)
    for place, moving in enumerate((scaled, scaled_far)):
        fresh = base[place] - (learn_rate * norm) * decode_fine(moving, rows)
        rounded_a[place] = fresh[:, :half].astype(bf16)
        rounded_b[place] = fresh[:, half:].astype(bf16)


def update_kernel(info, factor, top, middle, got, momentum, weight, momentum_new, weight_new):
    rows, cols = momentum.shape
    quarter = cols // 4
    head = top.shape[0]
    mid = rows - head
    norm = factor[0:1, :]

    def step(place, precon):
        span = slice(place, place + precon.shape[0])
        moved = momentum_rate * momentum[span, :] + precon * norm + decay_rate * weight[span, :]
        momentum_new[span, :] = moved
        weight_new[span, :] = weight[span, :] - learn_rate * moved

    for x in range(2):

        @pl.when(info[1] == x)
        def _():
            own = middle[mid * x : mid * (x + 1), :]
            pairs = []
            for piece in range(2):
                columns = slice(piece * quarter, (piece + 1) * quarter)
                both = [own[:, columns], got[:mid, columns]]
                pairs += both if x == 0 else both[::-1]
            step(head * (1 - x), jnp.concatenate(pairs, axis=1))
            step(mid * x, top[...])


def place_kernel(head, info, *refs):
    parts, out = refs[:6], refs[6]
    shard = info[3]
    rows, half = parts[0].shape[1:]
    mid = rows - head
    quarter = half // 2
    codes = ((0, 4), (2, 6), (1, 5, 3, 7), (0, 4), (1, 5), (2, 6, 3, 7))
    for index, (part, units) in enumerate(zip(parts, codes)):
        first = half * (index // 3)
        for place, code in enumerate(units):
            unit = shard ^ code
            side = unit & 1
            start = (unit >> 1) * (2 * rows)
            own = pl.multiple_of(start + side * (head + 2 * mid), 16)
            out[pl.ds(own, head), first : first + half] = part[place, :head, :]
            columns = pl.ds(pl.multiple_of(first + side * quarter, 128), quarter)
            for which in range(2):
                shared = pl.multiple_of(start + head + which * mid, 16)
                out[pl.ds(shared, mid), columns] = part[
                    place, head:, which * quarter : (which + 1) * quarter
                ]


def fast(acts, out_grad, sample_rows, own_a, own_g, a_state, g_state, momentum, weight):
    shard_pos = lax.axis_index("shard")
    tensor_pos = lax.axis_index("tensor")
    side, low, high = shard_pos & 1, (shard_pos >> 1) & 1, shard_pos >> 2
    count_a, width_a = a_state.shape[1], a_state.shape[2]
    count_g, width_g = g_state.shape[1], g_state.shape[2]
    group_cols = count_g * width_g
    tokens, cols = acts.shape
    outs = out_grad.shape[1]
    rows = momentum.shape[0]
    drawn = sample_rows.shape[0]
    samples = drawn * 8
    share = (1.0 - factor_decay) / samples
    half = cols // 2
    head = 2 * width_g
    mid = width_g // 2
    info = jnp.stack([tensor_pos, side, low, shard_pos, high])

    send_a, keep_a, send_b, keep_b = pl.pallas_call(
        lambda *refs: partial_kernel(group_cols, width_g, *refs),
        in_specs=[smem, main, main],
        out_specs=[vmem] * 4,
        out_shape=[
            shaped((4, rows + GROUP, half), jnp.int16),
            shaped((4, rows, half), f32),
        ]
        * 2,
        scratch_shapes=[
            pltpu.VMEM((tokens, outs), bf16),
            pltpu.VMEM((tokens, cols), bf16),
            pltpu.VMEM((outs, cols), f32),
            pltpu.SemaphoreType.DMA((6,)),
        ],
        compiler_params=params(56),
        name="partial",
    )(info, out_grad, acts)
    sample_rows, send_a, send_b = lax.optimization_barrier((sample_rows, send_a, send_b))
    got_a = swap(send_a, 1)
    got_b = swap(send_b, 2)

    wide = cols + -(-group_cols // 128) * 128
    picks = pl.pallas_call(
        lambda *refs: picks_kernel(group_cols, *refs),
        in_specs=[smem, vmem, main, main],
        out_specs=vmem,
        out_shape=shaped((drawn, wide), bf16),
        scratch_shapes=[
            pltpu.VMEM((tokens, cols), bf16),
            pltpu.VMEM((tokens, 640), bf16),
            pltpu.SemaphoreType.DMA((8,)),
        ],
        compiler_params=params(50),
        name="picks",
    )(info, sample_rows.reshape(1, -1), acts, out_grad)
    one = swap(picks, 4)

    base = pl.pallas_call(
        base_kernel,
        in_specs=[vmem, vmem],
        out_specs=vmem,
        out_shape=shaped((fine_rows(rows), cols), jnp.int16),
        compiler_params=params(16),
        name="base",
    )(momentum, weight)
    base_far = swap(base, 4)
    two = swap(jnp.stack([picks, one]), 1)

    send_a, keep_a = add_step(info, 2, True, got_a, keep_a)
    send_b, keep_b = add_step(info, 1, True, got_b, keep_b)
    send_a, send_b = lax.optimization_barrier((send_a, send_b))
    got_a = swap(send_a, 2)
    got_b = swap(send_b, 1)
    two, base_far = lax.optimization_barrier((two, base_far))
    blocks, packed_rows = block_places(count_a, width_a, count_g, width_g)
    packed = pl.pallas_call(
        lambda *refs: stats_kernel(blocks, *refs),
        in_specs=[smem] + [vmem] * 3,
        out_specs=vmem,
        out_shape=shaped((packed_rows, width_a), jnp.int16),
        scratch_shapes=[pltpu.VMEM((4, drawn, wide), bf16)],
        compiler_params=params(16),
        name="stats",
    )(info, picks, one, two)
    got_packed = swap(packed, 2)

    send, keep = pl.pallas_call(
        last_add_kernel,
        in_specs=[smem] + [vmem] * 4,
        out_specs=[vmem, vmem],
        out_shape=[
            shaped((2, rows + GROUP, half), jnp.int16),
            shaped((2, rows, half), f32),
        ],
        compiler_params=params(24),
        name="last_add",
    )(info, got_a, keep_a, got_b, keep_b)
    got = swap(send, 4)

    give = pl.pallas_call(
        lambda *refs: side_kernel(head, mid, *refs),
        in_specs=[smem] + [vmem] * 2,
        out_specs=vmem,
        out_shape=shaped((2, fine_rows(mid), half), jnp.int16),
        compiler_params=params(16),
        name="sides",
    )(info, base, base_far)
    base_units = pl.pallas_call(
        lambda *refs: pack_kernel(head, mid, *refs),
        in_specs=[smem] + [vmem] * 3,
        out_specs=vmem,
        out_shape=shaped((2, rows, cols), f32),
        compiler_params=params(16),
        name="pack",
    )(info, base, base_far, swap(give, 1))
    got_packed, base_units = lax.optimization_barrier((got_packed, base_units))

    new_a, new_g, inv_a, needed = pl.pallas_call(
        lambda *refs: factor_kernel(share, blocks, *refs),
        in_specs=[smem] * 3 + [vmem] * 4,
        out_specs=[vmem] * 4,
        out_shape=[
            shaped(a_state.shape[1:], f32),
            shaped(g_state.shape[1:], f32),
            shaped(a_state.shape[1:], f32),
            shaped((3, width_g + GROUP, width_g), jnp.int16),
        ],
        scratch_shapes=[pltpu.VMEM(g_state.shape[1:], f32)],
        compiler_params=params(24),
        name="factors",
    )(info, own_a, own_g, packed, got_packed, a_state[0], g_state[0])
    route = [
        ((2 * a + b) * 4 + c, (2 * c + b) * 4 + a)
        for a in range(4)
        for b in range(2)
        for c in range(4)
    ]
    inv_rows = lax.ppermute(needed, ("shard", "tensor"), route)

    top, middle, total, scaled = pl.pallas_call(
        precon_kernel,
        in_specs=[smem] + [vmem] * 4,
        out_specs=[vmem] * 4,
        out_shape=[
            shaped((head, cols), f32),
            shaped((width_g, half), f32),
            shaped((8, half), f32),
            shaped((fine_rows(rows), cols), jnp.int16),
        ],
        compiler_params=params(24),
        name="precon",
    )(info, got, keep, inv_rows, inv_a)

    scaled_far = swap(scaled, 4)
    give = pick(side, middle[mid:], middle[:mid])
    got = swap(jnp.concatenate([give, total], axis=0), 1)
    along_y = swap_t(total, 2)
    along_both = swap_both(total, 1, 2)
    total = (total + got[mid:]) + (along_y + along_both)
    total = total + swap_t(total, 1)
    others = [swap(total, bits) for bits in (2, 4, 6)]
    factor, rounded_a, rounded_b = pl.pallas_call(
        lambda *refs: round_kernel(rows * 8 * cols * 4, *refs),
        in_specs=[vmem] * 7,
        out_specs=[vmem] * 3,
        out_shape=[
            shaped((8, cols), f32),
            shaped((2, rows, half), bf16),
            shaped((2, rows, half), bf16),
        ],
        compiler_params=params(24),
        name="round",
    )(total, *others, base_units, scaled, scaled_far)

    along_l = swap(rounded_a, 2)
    along_x = swap(rounded_b, 1)
    momentum_new, weight_new = pl.pallas_call(
        update_kernel,
        in_specs=[smem] + [vmem] * 6,
        out_specs=[vmem] * 2,
        out_shape=[shaped((rows, cols), f32)] * 2,
        compiler_params=params(16),
        name="update",
    )(info, factor, top, middle, got, momentum, weight)
    along_l, along_x, momentum_new, weight_new = lax.optimization_barrier(
        (along_l, along_x, momentum_new, weight_new)
    )
    rest_a = swap(jnp.concatenate([rounded_a, along_l]), 1)
    rest_b = swap(jnp.concatenate([rounded_b, along_x]), 2)
    gathered = pl.pallas_call(
        lambda *refs: place_kernel(head, *refs),
        in_specs=[smem] + [vmem] * 6,
        out_specs=vmem,
        out_shape=shaped((rows * 8, cols), bf16),
        compiler_params=params(16),
        name="place",
    )(info, rounded_a, along_l, rest_a, rounded_b, along_x, rest_b)
    return (new_a[None], new_g[None], momentum_new, weight_new, gathered)


def local(acts, out_grad, sample_rows, own_a, own_g, a_state, g_state, momentum, weight):
    shapes_fit = (
        lax.axis_size("shard") == 8
        and lax.axis_size("tensor") == 4
        and a_state.shape[1:] == (4, 128, 128)
        and g_state.shape[1:] == (5, 96, 96)
    )
    plan = fast if shapes_fit else general
    return plan(acts, out_grad, sample_rows, own_a, own_g, a_state, g_state, momentum, weight)


def solution(mesh):
    return jax.shard_map(
        local,
        mesh=mesh,
        in_specs=(
            P("shard", "tensor"),
            P("shard", None),
            P("shard"),
            P(),
            P(),
            P("tensor", None, None, None),
            P("tensor", None, None, None),
            P("shard", "tensor"),
            P("shard", "tensor"),
        ),
        out_specs=(
            P("tensor", None, None, None),
            P("tensor", None, None, None),
            P("shard", "tensor"),
            P("shard", "tensor"),
            P(None, "tensor"),
        ),
        check_vma=False,
    )
```

```python
import jax
import jax.numpy as jnp
from jax import lax
from jax.experimental import pallas as pl
from jax.experimental.pallas import tpu as pltpu
from jax.sharding import PartitionSpec as P

NS_IT = 5


factor_decay = 0.8
damping_rate = 0.03
momentum_rate = 0.9
decay_rate = 0.01
learn_rate = 0.05
epsilon_sq = 1e-06
highest = lax.Precision.HIGHEST
f32 = jnp.float32
bf16 = jnp.bfloat16


def newton_inverse(factor):
    width = factor.shape[-1]
    identity = jnp.eye(width, dtype=jnp.float32)
    trace_mean = jnp.trace(factor, axis1=-2, axis2=-1) / width
    damped = factor + damping_rate * trace_mean[:, None, None] * identity
    bound = jnp.max(jnp.sum(jnp.abs(damped), axis=-1), axis=-1)
    guess = identity[None] / bound[:, None, None]
    for iteration in range(NS_IT):
        product = jnp.einsum("bij,bjk->bik", damped, guess, precision=highest)
        guess = jnp.einsum("bij,bjk->bik", guess, 2.0 * identity - product, precision=highest)
    return guess


def local_stats(rows, width):
    blocks = rows.reshape(rows.shape[0], -1, width)
    return jnp.einsum("sbi,sbj->bij", blocks, blocks, preferred_element_type=jnp.float32)


def owner_part(slots, shard_pos, shard_count):
    count = slots.shape[0]
    stride = shard_count // count
    slot_pos = jnp.minimum(shard_pos // stride, count - 1)
    mine = lax.dynamic_index_in_dim(slots, slot_pos, 0, keepdims=True)
    inverse = newton_inverse(mine)
    marker = (jnp.arange(count, dtype=jnp.int32) * stride == shard_pos).astype(jnp.float32)
    return marker[:, None, None] * inverse


def general(acts, out_grad, sample_rows, own_a, own_g, a_state, g_state, momentum, weight):
    shard_count = lax.axis_size("shard")
    tensor_count = lax.axis_size("tensor")
    shard_pos = lax.axis_index("shard")
    tensor_pos = lax.axis_index("tensor")
    block_a = a_state.shape[-1]
    block_g = g_state.shape[-1]
    samples = sample_rows.shape[0] * shard_count
    fresh_share = (1.0 - factor_decay) / samples
    picked_a = jnp.take(acts, sample_rows, axis=0)
    picked_g = jnp.take(out_grad, sample_rows, axis=0)
    group_cols = out_grad.shape[1] // tensor_count
    picked_g = lax.dynamic_slice_in_dim(picked_g, tensor_pos * group_cols, group_cols, 1)
    stats_a = local_stats(picked_a, block_a)
    stats_g = local_stats(picked_g, block_g)
    row_a = lax.dynamic_index_in_dim(own_a, tensor_pos, 0, keepdims=False)
    row_g = lax.dynamic_index_in_dim(own_g, tensor_pos, 0, keepdims=False)
    select_a = (row_a[None, :] == jnp.arange(row_a.shape[0], dtype=jnp.int32)[:, None]).astype(
        jnp.float32
    )
    select_g = (row_g[None, :] == jnp.arange(row_g.shape[0], dtype=jnp.int32)[:, None]).astype(
        jnp.float32
    )
    summed_a, summed_g = lax.psum((fresh_share * stats_a, fresh_share * stats_g), "shard")
    stored_a = jnp.einsum("sb,sij->bij", select_a, a_state[0], precision=highest)
    stored_g = jnp.einsum("sb,sij->bij", select_g, g_state[0], precision=highest)
    fac_a = factor_decay * stored_a + summed_a
    fac_g = factor_decay * stored_g + summed_g
    slots_a = jnp.einsum("sb,bij->sij", select_a, fac_a, precision=highest)
    slots_g = jnp.einsum("sb,bij->sij", select_g, fac_g, precision=highest)
    new_a_state = slots_a[None]
    new_g_state = slots_g[None]
    slot_inv_a, slot_inv_g = lax.psum(
        (owner_part(slots_a, shard_pos, shard_count), owner_part(slots_g, shard_pos, shard_count)),
        "shard",
    )
    inv_a = jnp.einsum("sb,sij->bij", select_a, slot_inv_a, precision=highest)
    local_inv_g = jnp.einsum("sb,sij->bij", select_g, slot_inv_g, precision=highest)
    inv_g = lax.all_gather(local_inv_g, "tensor", axis=0, tiled=True)
    raw_product = lax.dot_general(
        out_grad, acts, (((0,), (0,)), ((), ())), preferred_element_type=jnp.float32
    )
    left_done = jnp.einsum(
        "bij,bjd->bid", inv_g, raw_product.reshape(inv_g.shape[0], block_g, -1), precision=highest
    ).reshape(raw_product.shape)
    owned_rows = lax.psum_scatter(left_done, "shard", scatter_dimension=0, tiled=True)
    precon = jnp.einsum(
        "qbi,bij->qbj",
        owned_rows.reshape(owned_rows.shape[0], -1, block_a),
        inv_a,
        precision=highest,
    ).reshape(owned_rows.shape)
    square_total = lax.psum(jnp.sum(precon * precon), ("shard", "tensor"))
    mean_sq = square_total / (momentum.shape[0] * shard_count * momentum.shape[1] * tensor_count)
    update = precon / jnp.sqrt(mean_sq + epsilon_sq)
    momentum_new = momentum_rate * momentum + update + decay_rate * weight
    weight_new = weight - learn_rate * momentum_new
    gathered = lax.all_gather(weight_new.astype(jnp.bfloat16), "shard", axis=0, tiled=True)
    return (new_a_state, new_g_state, momentum_new, weight_new, gathered)


GROUP = 16
vmem = pl.BlockSpec(memory_space=pltpu.VMEM)
smem = pl.BlockSpec(memory_space=pltpu.SMEM)
main = pl.BlockSpec(memory_space=pl.ANY)


def params(mib):
    return pltpu.CompilerParams(vmem_limit_bytes=mib * 2**20)


def shaped(shape, kind):
    return jax.ShapeDtypeStruct(shape, kind)


def cost(flops, moved):
    return pl.CostEstimate(flops=flops, bytes_accessed=moved, transcendentals=0)


def swap(value, bit):
    return lax.ppermute(value, "shard", [(i, i ^ bit) for i in range(8)])


def swap_t(value, bit):
    return lax.ppermute(value, "tensor", [(i, i ^ bit) for i in range(4)])


def swap_both(value, bit, bit_t):
    route = [(4 * s + t, 4 * (s ^ bit) + (t ^ bit_t)) for s in range(8) for t in range(4)]
    return lax.ppermute(value, ("shard", "tensor"), route)


def pick(flag, if_zero, if_one):
    return jnp.where(flag == 0, if_zero, if_one)


def encode(value, store):
    rows, width = value.shape
    powers = []
    for first in range(0, rows, GROUP):
        part = value[first : first + GROUP]
        top = jnp.max(jnp.abs(part), axis=0, keepdims=True)
        power = jnp.floor(jnp.log2(jnp.maximum(top, 1e-30)))
        scaled = jnp.clip(jnp.round(part * jnp.exp2(14.0 - power)), -32767.0, 32767.0)
        store(first, scaled.astype(jnp.int32).astype(jnp.int16))
        powers.append(power)
    powers += [jnp.zeros((1, width), f32)] * (GROUP - len(powers))
    store(rows, jnp.concatenate(powers, axis=0).astype(jnp.int32).astype(jnp.int16))


def decode(packed, rows):
    whole = packed.astype(jnp.int32).astype(f32)
    scales = jnp.exp2(whole[rows : rows + GROUP] - 14.0)
    parts = [
        whole[first : first + GROUP] * scales[first // GROUP : first // GROUP + 1]
        for first in range(0, rows, GROUP)
    ]
    return jnp.concatenate(parts, axis=0)


def encode_to(ref, index, value):
    def store(first, data):
        ref[index, first : first + GROUP, :] = data

    encode(value, store)


FINE = 8
FULL = 32767.0
STEPS = 128.0


def encode_fine(value, ref):
    rows, width = value.shape
    powers = []
    for first in range(0, rows, 2 * FINE):
        scaled = []
        for start in (first, first + FINE):
            part = value[start : start + FINE]
            top = jnp.max(jnp.abs(part), axis=0, keepdims=True)
            power = jnp.ceil(jnp.log2(jnp.maximum(top, 1e-30)) * STEPS)
            scale = jnp.exp2(power * (-1.0 / STEPS)) * FULL
            scaled.append(jnp.clip(jnp.round(part * scale), -FULL, FULL))
            powers.append(power)
        ref[first : first + 2 * FINE, :] = (
            jnp.concatenate(scaled, axis=0).astype(jnp.int32).astype(jnp.int16)
        )
    powers += [jnp.zeros((1, width), f32)] * (-len(powers) % (2 * FINE))
    for first in range(0, len(powers), 2 * FINE):
        ref[rows + first : rows + first + 2 * FINE, :] = (
            jnp.concatenate(powers[first : first + 2 * FINE], axis=0)
            .astype(jnp.int32)
            .astype(jnp.int16)
        )


def decode_fine(ref, rows):
    values = ref[:rows, :].astype(jnp.int32).astype(f32)
    powers = ref[rows:, :].astype(jnp.int32).astype(f32)
    scales = jnp.exp2(powers * (1.0 / STEPS)) * (1.0 / FULL)
    parts = [
        values[first : first + FINE] * scales[first // FINE : first // FINE + 1]
        for first in range(0, rows, FINE)
    ]
    return jnp.concatenate(parts, axis=0)


def fine_rows(rows):
    return rows + -(-(rows // FINE) // (2 * FINE)) * 2 * FINE


def fold(rows):
    half = rows.shape[0] // 2
    return jnp.concatenate([rows[:half], rows[half:]], axis=1)


def fold(rows):
    half = rows.shape[0] // 2
    return jnp.concatenate([rows[:half], rows[half:]], axis=1)


def base_kernel(momentum, weight, packed):
    kept = momentum_rate * momentum[...] + decay_rate * weight[...]
    encode_fine(weight[...] - learn_rate * kept, packed)


def shared_rows(side, head, mid):
    return slice(head * (1 - side), head * (1 - side) + mid)


def kept_columns(value, side):
    quarter = value.shape[1] // 4
    blocks = [value[:, (2 * p + side) * quarter : (2 * p + side + 1) * quarter] for p in (0, 1)]
    return jnp.concatenate(blocks, axis=1)


def side_kernel(head, mid, info, own, far, give):
    rows = head + mid
    for x in range(2):

        @pl.when(info[1] == x)
        def _():
            span = shared_rows(x, head, mid)
            first = span.start // FINE
            for place, packed in enumerate((own, far)):
                values = packed[:rows, :].astype(jnp.int32)[span]
                powers = packed[rows:, :].astype(jnp.int32)[first : first + mid // FINE]
                missing = jnp.zeros((2 * FINE - powers.shape[0], powers.shape[1]), jnp.int32)
                all_rows = jnp.concatenate([values, powers, missing], axis=0)
                give[place] = kept_columns(all_rows, 1 - x).astype(jnp.int16)


def pack_kernel(head, mid, info, own, far, got, units):
    for x in range(2):

        @pl.when(info[1] == x)
        def _():
            for place, packed in enumerate((own, far)):
                values = decode_fine(packed, head + mid)
                shared = kept_columns(values[shared_rows(x, head, mid)], x)
                other = decode_fine(got.at[place], mid)
                both = (shared, other) if x == 0 else (other, shared)
                quarter = shared.shape[1] // 2
                pairs = []
                for piece in range(2):
                    pairs += [each[:, piece * quarter : (piece + 1) * quarter] for each in both]
                units[place, :head, :] = values[mid * x : mid * x + head]
                units[place, head:, :] = jnp.concatenate(pairs, axis=1)


def parts_of(value):
    upper = value.astype(bf16)
    return upper, (value - upper.astype(f32)).astype(bf16)


def dot_of(left, right):
    dot = lambda p, q: jnp.dot(p, q, preferred_element_type=f32)
    small = dot(left[0], right[1]) + dot(left[1], right[0])
    return dot(left[0], right[0]) + small


def picks_kernel(group_cols, info, sampled, acts, out_grad, picks, acts_buf, grad_buf, sems):
    group = info[0]
    block = 128
    span = grad_buf.shape[1]
    tokens, cols = acts.shape
    chunk = tokens // 4
    last = out_grad.shape[1] // block - span // block
    start = pl.multiple_of(jnp.minimum((group * group_cols) // block, last) * block, block)
    copies = []
    for part in range(4):
        some = pl.ds(part * chunk, chunk)
        copies.append(
            (
                pltpu.make_async_copy(acts.at[some, :], acts_buf.at[some, :], sems.at[part]),
                pltpu.make_async_copy(
                    out_grad.at[some, pl.ds(start, span)], grad_buf.at[some, :], sems.at[4 + part]
                ),
            )
        )
        for copy in copies[-1]:
            copy.start()
    drawn = sampled.shape[1]
    row = lax.broadcasted_iota(jnp.int32, (drawn, drawn), 0)
    col = lax.broadcasted_iota(jnp.int32, (drawn, drawn), 1)
    upright = jnp.sum(jnp.where(row == col, sampled[...], 0), axis=1, keepdims=True)
    found = jnp.zeros((drawn, cols), f32)
    grads = jnp.zeros((drawn, span), f32)
    for part in range(4):
        place = lax.broadcasted_iota(jnp.int32, (drawn, chunk), 1) + part * chunk
        chosen = (place == upright).astype(bf16)
        some = slice(part * chunk, (part + 1) * chunk)
        copies[part][0].wait()
        found += jnp.dot(chosen, acts_buf[some, :], preferred_element_type=f32)
        copies[part][1].wait()
        grads += jnp.dot(chosen, grad_buf[some, :], preferred_element_type=f32)
    picks[:, :cols] = found.astype(bf16)
    pad = jnp.zeros((drawn, picks.shape[1] - cols - group_cols), f32)
    for which in range(4):
        begin = min((which * group_cols) // block, last) * block
        offset = which * group_cols - begin

        @pl.when(group == which)
        def _():
            part = jnp.concatenate([grads[:, offset : offset + group_cols], pad], axis=1)
            picks[:, cols:] = part.astype(bf16)


def split_units(group, head, width_g):
    half = group.shape[1] // 2
    mid = width_g // 2
    middle = group[head : head + width_g]
    packed = [
        jnp.concatenate([middle[:mid, cols], middle[mid:, cols]], axis=1)
        for cols in (slice(0, half), slice(half, 2 * half))
    ]
    return (
        jnp.concatenate([group[:head], packed[0]], axis=0),
        jnp.concatenate([group[head + width_g :], packed[1]], axis=0),
    )


def partial_kernel(
    group_cols, width_g, info, out_grad, acts, send_a, keep_a, send_b, keep_b, grad_buf, acts_buf,
    raw, sems
):
    side, low = info[1], info[2]
    head = 2 * width_g
    outs = out_grad.shape[1]
    half = acts.shape[1] // 2
    block = outs // 5
    first = pltpu.make_async_copy(acts, acts_buf, sems.at[5])
    first.start()
    copies = []
    for step in range(5):
        columns = pl.ds(step * block, block)
        copies.append(
            pltpu.make_async_copy(out_grad.at[:, columns], grad_buf.at[:, columns], sems.at[step])
        )
        copies[-1].start()
    first.wait()
    for step in range(5):
        copies[step].wait()
        columns = slice(step * block, (step + 1) * block)
        raw[columns, :] = jnp.dot(
            grad_buf[:, columns].T, acts_buf[...], preferred_element_type=f32
        )
        if step == 0:
            continue
        place = step - 1
        span = slice(place * group_cols, (place + 1) * group_cols)
        zero, one = split_units(raw[span, :half], head, width_g)
        keep_a[place] = jnp.where(side == 0, zero, one)
        encode_to(send_a, place, jnp.where(side == 0, one, zero))
        if place % 2 == 0:
            continue
        before = slice((place - 1) * group_cols, place * group_cols)
        zero = split_units(raw[before, half:], head, width_g)
        one = split_units(raw[span, half:], head, width_g)
        for x in range(2):
            keep_b[place - 1 + x] = jnp.where(low == 0, zero[x], one[x])
            encode_to(send_b, place - 1 + x, jnp.where(low == 0, one[x], zero[x]))


def add_kernel(bit_at, inner, info, got, held, send, keep):
    bit = info[bit_at]
    rows = held.shape[1]
    count = send.shape[0]

    def place(j, value):
        return 2 * j + value if inner else value * count + j

    for j in range(count):
        away = place(j, 1 - bit)
        encode_to(send, j, held[away] + decode(got[away], rows))
    for j in range(count):
        home = place(j, bit)
        keep[j] = held[home] + decode(got[home], rows)


def last_add_kernel(info, got_a, held_a, got_b, held_b, send, keep):
    high = info[4]
    rows = keep.shape[1]
    for piece, (got, held) in enumerate(((got_a, held_a), (got_b, held_b))):
        encode_to(send, piece, held[1 - high] + decode(got[1 - high], rows))
        keep[piece] = held[high] + decode(got[high], rows)


def add_step(info, bit_at, inner, got, held):
    count = held.shape[0] // 2
    return pl.pallas_call(
        lambda *refs: add_kernel(bit_at, inner, *refs),
        in_specs=[smem, vmem, vmem],
        out_specs=[vmem, vmem],
        out_shape=[
            shaped((count,) + got.shape[1:], jnp.int16),
            shaped((count,) + held.shape[1:], f32),
        ],
        compiler_params=params(24),
        name="add",
    )(info, got, held)


def block_places(count_a, width_a, count_g, width_g):
    blocks, column, row = [], 0, 0
    for is_a, count, width in ((True, count_a, width_a), (False, count_g, width_g)):
        for place in range(count):
            blocks.append((is_a, place, width, column, row))
            column += width
            row += width + GROUP
    return blocks, row


def stats_kernel(blocks, info, own, one, two, packed, picks):
    place = 2 * info[4] + info[1]
    picks[place] = own[...]
    picks[place ^ 2] = one[...]
    picks[place ^ 1] = two[0]
    picks[place ^ 3] = two[1]
    everything = picks[...].reshape(picks.shape[0] * picks.shape[1], picks.shape[2])
    for _, _, width, column, row in blocks:
        rows = everything[:, column : column + width]
        stats = lax.dot_general(
            rows, rows, (((0,), (0,)), ((), ())), preferred_element_type=f32
        )
        missing = packed.shape[1] - width
        if missing:
            stats = jnp.concatenate([stats, jnp.zeros((width, missing), f32)], axis=1)

        def store(first, data):
            packed[row + first : row + first + GROUP, :] = data

        encode(stats, store)


def factor_kernel(
    share, blocks, info, own_a, own_g, packed, got, a_state, g_state, a_new, g_new, inv_a, needed,
    inv_g
):
    group = info[0]
    count_a, count_g = a_state.shape[0], g_state.shape[0]
    errors, inverses, scales = [], [], []
    for is_a, place, width, _, first in blocks:
        span = slice(first, first + width + GROUP)
        stats = decode(packed[span, :], width) + decode(got[span, :], width)
        stats = stats[:, :width]
        slot = own_a[group, place] if is_a else own_g[group, place]
        stored = (a_state if is_a else g_state)[slot]
        factor = factor_decay * stored + share * stats
        (a_new if is_a else g_new)[slot] = factor
        row = lax.broadcasted_iota(jnp.int32, (width, width), 0)
        col = lax.broadcasted_iota(jnp.int32, (width, width), 1)
        identity = (row == col).astype(f32)
        trace = jnp.sum(factor * identity) / width
        damped = factor + (damping_rate * trace) * identity
        bound = jnp.max(jnp.sum(jnp.abs(damped), axis=0))
        error = identity - damped / bound
        errors.append(error)
        inverses.append(identity + error)
        scales.append(bound)
    every = range(count_a + count_g)
    errors = [parts_of(errors[i]) for i in every]
    errors = [parts_of(dot_of(errors[i], errors[i])) for i in every]
    for step in range(1, NS_IT - 1):
        grown = [dot_of(parts_of(inverses[i]), errors[i]) for i in every]
        squares = [dot_of(errors[i], errors[i]) for i in every]
        inverses = [inverses[i] + grown[i] for i in every]
        errors = [parts_of(squares[i]) for i in every]
    grown = [dot_of(parts_of(inverses[i]), errors[i]) for i in every]
    inverses = [(inverses[i] + grown[i]) / scales[i] for i in every]
    for index in every:
        if index < count_a:
            inv_a[index] = inverses[index]
        else:
            inv_g[index - count_a] = inverses[index]
    side = info[1]
    for index, place in enumerate((3 * side, 1 + 3 * side, 2)):
        encode_to(needed, index, inv_g[place])


def precon_kernel(info, got, held, inv_g, inv_a, top, mid, total, coded):
    side = info[1]
    width_g, width_a = inv_g.shape[-1], inv_a.shape[-1]
    half = width_g // 2
    dot = lambda p, q: dot_of(parts_of(p), parts_of(q))
    left = [decode(inv_g[place], width_g) for place in range(3)]
    squares = jnp.zeros((width_g, width_a), f32)
    for piece in range(2):
        part = held[piece] + decode(got[piece], held.shape[1])
        for place in range(2):
            for block in range(2):
                values = dot(
                    left[place],
                    part[
                        place * width_g : (place + 1) * width_g,
                        block * width_a : (block + 1) * width_a,
                    ],
                )
                values = dot(values, inv_a[2 * piece + block])
                squares += values * values
                column = (2 * piece + block) * width_a
                top[place * width_g : (place + 1) * width_g, column : column + width_a] = values
        packed = part[2 * width_g : 2 * width_g + half, :]
        values = jnp.concatenate([packed[:, :width_a], packed[:, width_a:]], axis=0)
        values = dot(dot(left[2], values), inv_a[2 * piece + side])
        squares += values * values
        mid[:, piece * width_a : (piece + 1) * width_a] = values
    total[...] = jnp.full(total.shape, jnp.sum(squares), f32)
    width = mid.shape[1] // 2
    folded = [fold(mid[:, :width]), fold(mid[:, width:])]
    unit = jnp.concatenate([top[...], jnp.concatenate(folded, axis=1)], axis=0)
    encode_fine(unit, coded)


def round_kernel(
    entries, total, got_total, base, scaled, scaled_far, factor,
    rounded_a, rounded_b
):
    rows, half = rounded_a.shape[1:]
    mean_sq = (total[0:1, :] + got_total[0:1, :]) / entries
    norm = 1.0 / jnp.sqrt(mean_sq + epsilon_sq)
    norm = jnp.concatenate([norm, norm], axis=1)
    factor[...] = jnp.broadcast_to(norm, factor.shape)
    for place, moving in enumerate((scaled, scaled_far)):
        fresh = base[place] - (learn_rate * norm) * decode_fine(moving, rows)
        rounded_a[place] = fresh[:, :half].astype(bf16)
        rounded_b[place] = fresh[:, half:].astype(bf16)


def update_kernel(info, factor, top, middle, got, momentum, weight, momentum_new, weight_new):
    rows, cols = momentum.shape
    quarter = cols // 4
    head = top.shape[0]
    mid = rows - head
    norm = factor[0:1, :]

    def step(place, precon):
        span = slice(place, place + precon.shape[0])
        moved = momentum_rate * momentum[span, :] + precon * norm + decay_rate * weight[span, :]
        momentum_new[span, :] = moved
        weight_new[span, :] = weight[span, :] - learn_rate * moved

    for x in range(2):

        @pl.when(info[1] == x)
        def _():
            own = middle[mid * x : mid * (x + 1), :]
            pairs = []
            for piece in range(2):
                columns = slice(piece * quarter, (piece + 1) * quarter)
                both = [own[:, columns], got[:mid, columns]]
                pairs += both if x == 0 else both[::-1]
            step(head * (1 - x), jnp.concatenate(pairs, axis=1))
            step(mid * x, top[...])


def place_kernel(head, info, *refs):
    parts, out = refs[:6], refs[6]
    shard = info[3]
    rows, half = parts[0].shape[1:]
    mid = rows - head
    quarter = half // 2
    codes = ((0, 4), (2, 6), (1, 5, 3, 7), (0, 4), (1, 5), (2, 6, 3, 7))
    for index, (part, units) in enumerate(zip(parts, codes)):
        first = half * (index // 3)
        for place, code in enumerate(units):
            unit = shard ^ code
            side = unit & 1
            start = (unit >> 1) * (2 * rows)
            own = pl.multiple_of(start + side * (head + 2 * mid), 16)
            out[pl.ds(own, head), first : first + half] = part[place, :head, :]
            columns = pl.ds(pl.multiple_of(first + side * quarter, 128), quarter)
            for which in range(2):
                shared = pl.multiple_of(start + head + which * mid, 16)
                out[pl.ds(shared, mid), columns] = part[
                    place, head:, which * quarter : (which + 1) * quarter
                ]


def fast(acts, out_grad, sample_rows, own_a, own_g, a_state, g_state, momentum, weight):
    shard_pos = lax.axis_index("shard")
    tensor_pos = lax.axis_index("tensor")
    side, low, high = shard_pos & 1, (shard_pos >> 1) & 1, shard_pos >> 2
    count_a, width_a = a_state.shape[1], a_state.shape[2]
    count_g, width_g = g_state.shape[1], g_state.shape[2]
    group_cols = count_g * width_g
    tokens, cols = acts.shape
    outs = out_grad.shape[1]
    rows = momentum.shape[0]
    drawn = sample_rows.shape[0]
    samples = drawn * 8
    share = (1.0 - factor_decay) / samples
    half = cols // 2
    head = 2 * width_g
    mid = width_g // 2
    info = jnp.stack([tensor_pos, side, low, shard_pos, high])

    send_a, keep_a, send_b, keep_b = pl.pallas_call(
        lambda *refs: partial_kernel(group_cols, width_g, *refs),
        in_specs=[smem, main, main],
        out_specs=[vmem] * 4,
        out_shape=[
            shaped((4, rows + GROUP, half), jnp.int16),
            shaped((4, rows, half), f32),
        ]
        * 2,
        scratch_shapes=[
            pltpu.VMEM((tokens, outs), bf16),
            pltpu.VMEM((tokens, cols), bf16),
            pltpu.VMEM((outs, cols), f32),
            pltpu.SemaphoreType.DMA((6,)),
        ],
        compiler_params=params(56),
        name="partial",
    )(info, out_grad, acts)
    sample_rows, send_a, send_b = lax.optimization_barrier((sample_rows, send_a, send_b))
    got_a = swap(send_a, 1)
    got_b = swap(send_b, 2)

    wide = cols + -(-group_cols // 128) * 128
    picks = pl.pallas_call(
        lambda *refs: picks_kernel(group_cols, *refs),
        in_specs=[smem, vmem, main, main],
        out_specs=vmem,
        out_shape=shaped((drawn, wide), bf16),
        scratch_shapes=[
            pltpu.VMEM((tokens, cols), bf16),
            pltpu.VMEM((tokens, 640), bf16),
            pltpu.SemaphoreType.DMA((8,)),
        ],
        compiler_params=params(50),
        name="picks",
    )(info, sample_rows.reshape(1, -1), acts, out_grad)
    one = swap(picks, 4)

    base = pl.pallas_call(
        base_kernel,
        in_specs=[vmem, vmem],
        out_specs=vmem,
        out_shape=shaped((fine_rows(rows), cols), jnp.int16),
        compiler_params=params(16),
        name="base",
    )(momentum, weight)
    base_far = swap(base, 4)
    two = swap(jnp.stack([picks, one]), 1)

    send_a, keep_a = add_step(info, 2, True, got_a, keep_a)
    send_b, keep_b = add_step(info, 1, True, got_b, keep_b)
    send_a, send_b = lax.optimization_barrier((send_a, send_b))
    got_a = swap(send_a, 2)
    got_b = swap(send_b, 1)
    two, base_far = lax.optimization_barrier((two, base_far))
    blocks, packed_rows = block_places(count_a, width_a, count_g, width_g)
    packed = pl.pallas_call(
        lambda *refs: stats_kernel(blocks, *refs),
        in_specs=[smem] + [vmem] * 3,
        out_specs=vmem,
        out_shape=shaped((packed_rows, width_a), jnp.int16),
        scratch_shapes=[pltpu.VMEM((4, drawn, wide), bf16)],
        compiler_params=params(16),
        name="stats",
    )(info, picks, one, two)
    got_packed = swap(packed, 2)

    send, keep = pl.pallas_call(
        last_add_kernel,
        in_specs=[smem] + [vmem] * 4,
        out_specs=[vmem, vmem],
        out_shape=[
            shaped((2, rows + GROUP, half), jnp.int16),
            shaped((2, rows, half), f32),
        ],
        compiler_params=params(24),
        name="last_add",
    )(info, got_a, keep_a, got_b, keep_b)
    got = swap(send, 4)

    give = pl.pallas_call(
        lambda *refs: side_kernel(head, mid, *refs),
        in_specs=[smem] + [vmem] * 2,
        out_specs=vmem,
        out_shape=shaped((2, fine_rows(mid), half), jnp.int16),
        compiler_params=params(16),
        name="sides",
    )(info, base, base_far)
    base_units = pl.pallas_call(
        lambda *refs: pack_kernel(head, mid, *refs),
        in_specs=[smem] + [vmem] * 3,
        out_specs=vmem,
        out_shape=shaped((2, rows, cols), f32),
        compiler_params=params(16),
        name="pack",
    )(info, base, base_far, swap(give, 1))
    got_packed, base_units = lax.optimization_barrier((got_packed, base_units))

    new_a, new_g, inv_a, needed = pl.pallas_call(
        lambda *refs: factor_kernel(share, blocks, *refs),
        in_specs=[smem] * 3 + [vmem] * 4,
        out_specs=[vmem] * 4,
        out_shape=[
            shaped(a_state.shape[1:], f32),
            shaped(g_state.shape[1:], f32),
            shaped(a_state.shape[1:], f32),
            shaped((3, width_g + GROUP, width_g), jnp.int16),
        ],
        scratch_shapes=[pltpu.VMEM(g_state.shape[1:], f32)],
        compiler_params=params(24),
        name="factors",
    )(info, own_a, own_g, packed, got_packed, a_state[0], g_state[0])
    route = [
        ((2 * a + b) * 4 + c, (2 * c + b) * 4 + a)
        for a in range(4)
        for b in range(2)
        for c in range(4)
    ]
    inv_rows = lax.ppermute(needed, ("shard", "tensor"), route)

    top, middle, total, scaled = pl.pallas_call(
        precon_kernel,
        in_specs=[smem] + [vmem] * 4,
        out_specs=[vmem] * 4,
        out_shape=[
            shaped((head, cols), f32),
            shaped((width_g, half), f32),
            shaped((8, half), f32),
            shaped((fine_rows(rows), cols), jnp.int16),
        ],
        compiler_params=params(24),
        name="precon",
    )(info, got, keep, inv_rows, inv_a)

    scaled_far = swap(scaled, 4)
    give = pick(side, middle[mid:], middle[:mid])
    got = swap(jnp.concatenate([give, total], axis=0), 1)
    along_y = swap_t(total, 2)
    along_both = swap_both(total, 1, 2)
    total = (total + got[mid:]) + (along_y + along_both)
    total = total + swap_t(total, 1)
    total = total + swap(total, 4)
    factor, rounded_a, rounded_b = pl.pallas_call(
        lambda *refs: round_kernel(rows * 8 * cols * 4, *refs),
        in_specs=[vmem] * 5,
        out_specs=[vmem] * 3,
        out_shape=[
            shaped((8, cols), f32),
            shaped((2, rows, half), bf16),
            shaped((2, rows, half), bf16),
        ],
        compiler_params=params(24),
        name="round",
    )(total, swap(total, 2), base_units, scaled, scaled_far)

    along_l = swap(rounded_a, 2)
    along_x = swap(rounded_b, 1)
    momentum_new, weight_new = pl.pallas_call(
        update_kernel,
        in_specs=[smem] + [vmem] * 6,
        out_specs=[vmem] * 2,
        out_shape=[shaped((rows, cols), f32)] * 2,
        compiler_params=params(16),
        name="update",
    )(info, factor, top, middle, got, momentum, weight)
    along_l, along_x, momentum_new, weight_new = lax.optimization_barrier(
        (along_l, along_x, momentum_new, weight_new)
    )
    rest_a = swap(jnp.concatenate([rounded_a, along_l]), 1)
    rest_b = swap(jnp.concatenate([rounded_b, along_x]), 2)
    gathered = pl.pallas_call(
        lambda *refs: place_kernel(head, *refs),
        in_specs=[smem] + [vmem] * 6,
        out_specs=vmem,
        out_shape=shaped((rows * 8, cols), bf16),
        compiler_params=params(16),
        name="place",
    )(info, rounded_a, along_l, rest_a, rounded_b, along_x, rest_b)
    return (new_a[None], new_g[None], momentum_new, weight_new, gathered)


def local(acts, out_grad, sample_rows, own_a, own_g, a_state, g_state, momentum, weight):
    shapes_fit = (
        lax.axis_size("shard") == 8
        and lax.axis_size("tensor") == 4
        and a_state.shape[1:] == (4, 128, 128)
        and g_state.shape[1:] == (5, 96, 96)
    )
    plan = fast if shapes_fit else general
    return plan(acts, out_grad, sample_rows, own_a, own_g, a_state, g_state, momentum, weight)


def solution(mesh):
    return jax.shard_map(
        local,
        mesh=mesh,
        in_specs=(
            P("shard", "tensor"),
            P("shard", None),
            P("shard"),
            P(),
            P(),
            P("tensor", None, None, None),
            P("tensor", None, None, None),
            P("shard", "tensor"),
            P("shard", "tensor"),
        ),
        out_specs=(
            P("tensor", None, None, None),
            P("tensor", None, None, None),
            P("shard", "tensor"),
            P("shard", "tensor"),
            P(None, "tensor"),
        ),
        check_vma=False,
    )
```

```python
import jax
import jax.numpy as jnp
from jax import lax
from jax.experimental import pallas as pl
from jax.experimental.pallas import tpu as pltpu
from jax.sharding import PartitionSpec as P

NS_IT = 5


factor_decay = 0.8
damping_rate = 0.03
momentum_rate = 0.9
decay_rate = 0.01
learn_rate = 0.05
epsilon_sq = 1e-06
highest = lax.Precision.HIGHEST
f32 = jnp.float32
bf16 = jnp.bfloat16


def newton_inverse(factor):
    width = factor.shape[-1]
    identity = jnp.eye(width, dtype=jnp.float32)
    trace_mean = jnp.trace(factor, axis1=-2, axis2=-1) / width
    damped = factor + damping_rate * trace_mean[:, None, None] * identity
    bound = jnp.max(jnp.sum(jnp.abs(damped), axis=-1), axis=-1)
    guess = identity[None] / bound[:, None, None]
    for iteration in range(NS_IT):
        product = jnp.einsum("bij,bjk->bik", damped, guess, precision=highest)
        guess = jnp.einsum("bij,bjk->bik", guess, 2.0 * identity - product, precision=highest)
    return guess


def local_stats(rows, width):
    blocks = rows.reshape(rows.shape[0], -1, width)
    return jnp.einsum("sbi,sbj->bij", blocks, blocks, preferred_element_type=jnp.float32)


def owner_part(slots, shard_pos, shard_count):
    count = slots.shape[0]
    stride = shard_count // count
    slot_pos = jnp.minimum(shard_pos // stride, count - 1)
    mine = lax.dynamic_index_in_dim(slots, slot_pos, 0, keepdims=True)
    inverse = newton_inverse(mine)
    marker = (jnp.arange(count, dtype=jnp.int32) * stride == shard_pos).astype(jnp.float32)
    return marker[:, None, None] * inverse


def general(acts, out_grad, sample_rows, own_a, own_g, a_state, g_state, momentum, weight):
    shard_count = lax.axis_size("shard")
    tensor_count = lax.axis_size("tensor")
    shard_pos = lax.axis_index("shard")
    tensor_pos = lax.axis_index("tensor")
    block_a = a_state.shape[-1]
    block_g = g_state.shape[-1]
    samples = sample_rows.shape[0] * shard_count
    fresh_share = (1.0 - factor_decay) / samples
    picked_a = jnp.take(acts, sample_rows, axis=0)
    picked_g = jnp.take(out_grad, sample_rows, axis=0)
    group_cols = out_grad.shape[1] // tensor_count
    picked_g = lax.dynamic_slice_in_dim(picked_g, tensor_pos * group_cols, group_cols, 1)
    stats_a = local_stats(picked_a, block_a)
    stats_g = local_stats(picked_g, block_g)
    row_a = lax.dynamic_index_in_dim(own_a, tensor_pos, 0, keepdims=False)
    row_g = lax.dynamic_index_in_dim(own_g, tensor_pos, 0, keepdims=False)
    select_a = (row_a[None, :] == jnp.arange(row_a.shape[0], dtype=jnp.int32)[:, None]).astype(
        jnp.float32
    )
    select_g = (row_g[None, :] == jnp.arange(row_g.shape[0], dtype=jnp.int32)[:, None]).astype(
        jnp.float32
    )
    summed_a, summed_g = lax.psum((fresh_share * stats_a, fresh_share * stats_g), "shard")
    stored_a = jnp.einsum("sb,sij->bij", select_a, a_state[0], precision=highest)
    stored_g = jnp.einsum("sb,sij->bij", select_g, g_state[0], precision=highest)
    fac_a = factor_decay * stored_a + summed_a
    fac_g = factor_decay * stored_g + summed_g
    slots_a = jnp.einsum("sb,bij->sij", select_a, fac_a, precision=highest)
    slots_g = jnp.einsum("sb,bij->sij", select_g, fac_g, precision=highest)
    new_a_state = slots_a[None]
    new_g_state = slots_g[None]
    slot_inv_a, slot_inv_g = lax.psum(
        (owner_part(slots_a, shard_pos, shard_count), owner_part(slots_g, shard_pos, shard_count)),
        "shard",
    )
    inv_a = jnp.einsum("sb,sij->bij", select_a, slot_inv_a, precision=highest)
    local_inv_g = jnp.einsum("sb,sij->bij", select_g, slot_inv_g, precision=highest)
    inv_g = lax.all_gather(local_inv_g, "tensor", axis=0, tiled=True)
    raw_product = lax.dot_general(
        out_grad, acts, (((0,), (0,)), ((), ())), preferred_element_type=jnp.float32
    )
    left_done = jnp.einsum(
        "bij,bjd->bid", inv_g, raw_product.reshape(inv_g.shape[0], block_g, -1), precision=highest
    ).reshape(raw_product.shape)
    owned_rows = lax.psum_scatter(left_done, "shard", scatter_dimension=0, tiled=True)
    precon = jnp.einsum(
        "qbi,bij->qbj",
        owned_rows.reshape(owned_rows.shape[0], -1, block_a),
        inv_a,
        precision=highest,
    ).reshape(owned_rows.shape)
    square_total = lax.psum(jnp.sum(precon * precon), ("shard", "tensor"))
    mean_sq = square_total / (momentum.shape[0] * shard_count * momentum.shape[1] * tensor_count)
    update = precon / jnp.sqrt(mean_sq + epsilon_sq)
    momentum_new = momentum_rate * momentum + update + decay_rate * weight
    weight_new = weight - learn_rate * momentum_new
    gathered = lax.all_gather(weight_new.astype(jnp.bfloat16), "shard", axis=0, tiled=True)
    return (new_a_state, new_g_state, momentum_new, weight_new, gathered)


GROUP = 16
vmem = pl.BlockSpec(memory_space=pltpu.VMEM)
smem = pl.BlockSpec(memory_space=pltpu.SMEM)
main = pl.BlockSpec(memory_space=pl.ANY)


def params(mib):
    return pltpu.CompilerParams(vmem_limit_bytes=mib * 2**20)


def shaped(shape, kind):
    return jax.ShapeDtypeStruct(shape, kind)


def cost(flops, moved):
    return pl.CostEstimate(flops=flops, bytes_accessed=moved, transcendentals=0)


def swap(value, bit):
    return lax.ppermute(value, "shard", [(i, i ^ bit) for i in range(8)])


def swap_t(value, bit):
    return lax.ppermute(value, "tensor", [(i, i ^ bit) for i in range(4)])


def swap_both(value, bit, bit_t):
    route = [(4 * s + t, 4 * (s ^ bit) + (t ^ bit_t)) for s in range(8) for t in range(4)]
    return lax.ppermute(value, ("shard", "tensor"), route)


def pick(flag, if_zero, if_one):
    return jnp.where(flag == 0, if_zero, if_one)


def encode(value, store):
    rows, width = value.shape
    powers = []
    for first in range(0, rows, GROUP):
        part = value[first : first + GROUP]
        top = jnp.max(jnp.abs(part), axis=0, keepdims=True)
        power = jnp.floor(jnp.log2(jnp.maximum(top, 1e-30)))
        scaled = jnp.clip(jnp.round(part * jnp.exp2(14.0 - power)), -32767.0, 32767.0)
        store(first, scaled.astype(jnp.int32).astype(jnp.int16))
        powers.append(power)
    powers += [jnp.zeros((1, width), f32)] * (GROUP - len(powers))
    store(rows, jnp.concatenate(powers, axis=0).astype(jnp.int32).astype(jnp.int16))


def decode(packed, rows):
    whole = packed.astype(jnp.int32).astype(f32)
    scales = jnp.exp2(whole[rows : rows + GROUP] - 14.0)
    parts = [
        whole[first : first + GROUP] * scales[first // GROUP : first // GROUP + 1]
        for first in range(0, rows, GROUP)
    ]
    return jnp.concatenate(parts, axis=0)


def encode_to(ref, index, value):
    def store(first, data):
        ref[index, first : first + GROUP, :] = data

    encode(value, store)


FINE = 8
FULL = 32767.0
STEPS = 128.0


def encode_fine(value, ref):
    rows, width = value.shape
    powers = []
    for first in range(0, rows, 2 * FINE):
        scaled = []
        for start in (first, first + FINE):
            part = value[start : start + FINE]
            top = jnp.max(jnp.abs(part), axis=0, keepdims=True)
            power = jnp.ceil(jnp.log2(jnp.maximum(top, 1e-30)) * STEPS)
            scale = jnp.exp2(power * (-1.0 / STEPS)) * FULL
            scaled.append(jnp.clip(jnp.round(part * scale), -FULL, FULL))
            powers.append(power)
        ref[first : first + 2 * FINE, :] = (
            jnp.concatenate(scaled, axis=0).astype(jnp.int32).astype(jnp.int16)
        )
    powers += [jnp.zeros((1, width), f32)] * (-len(powers) % (2 * FINE))
    for first in range(0, len(powers), 2 * FINE):
        ref[rows + first : rows + first + 2 * FINE, :] = (
            jnp.concatenate(powers[first : first + 2 * FINE], axis=0)
            .astype(jnp.int32)
            .astype(jnp.int16)
        )


def decode_fine(ref, rows):
    values = ref[:rows, :].astype(jnp.int32).astype(f32)
    powers = ref[rows:, :].astype(jnp.int32).astype(f32)
    scales = jnp.exp2(powers * (1.0 / STEPS)) * (1.0 / FULL)
    parts = [
        values[first : first + FINE] * scales[first // FINE : first // FINE + 1]
        for first in range(0, rows, FINE)
    ]
    return jnp.concatenate(parts, axis=0)


def fine_rows(rows):
    return rows + -(-(rows // FINE) // (2 * FINE)) * 2 * FINE


def fold(rows):
    half = rows.shape[0] // 2
    return jnp.concatenate([rows[:half], rows[half:]], axis=1)


def fold(rows):
    half = rows.shape[0] // 2
    return jnp.concatenate([rows[:half], rows[half:]], axis=1)


def base_kernel(momentum, weight, packed):
    kept = momentum_rate * momentum[...] + decay_rate * weight[...]
    encode_fine(weight[...] - learn_rate * kept, packed)


def shared_rows(side, head, mid):
    return slice(head * (1 - side), head * (1 - side) + mid)


def kept_columns(value, side):
    quarter = value.shape[1] // 4
    blocks = [value[:, (2 * p + side) * quarter : (2 * p + side + 1) * quarter] for p in (0, 1)]
    return jnp.concatenate(blocks, axis=1)


def side_kernel(head, mid, info, own, far, give):
    rows = head + mid
    for x in range(2):

        @pl.when(info[1] == x)
        def _():
            span = shared_rows(x, head, mid)
            first = span.start // FINE
            for place, packed in enumerate((own, far)):
                values = packed[:rows, :].astype(jnp.int32)[span]
                powers = packed[rows:, :].astype(jnp.int32)[first : first + mid // FINE]
                missing = jnp.zeros((2 * FINE - powers.shape[0], powers.shape[1]), jnp.int32)
                all_rows = jnp.concatenate([values, powers, missing], axis=0)
                give[place] = kept_columns(all_rows, 1 - x).astype(jnp.int16)


def pack_kernel(head, mid, info, own, far, got, units):
    for x in range(2):

        @pl.when(info[1] == x)
        def _():
            for place, packed in enumerate((own, far)):
                values = decode_fine(packed, head + mid)
                shared = kept_columns(values[shared_rows(x, head, mid)], x)
                other = decode_fine(got.at[place], mid)
                both = (shared, other) if x == 0 else (other, shared)
                quarter = shared.shape[1] // 2
                pairs = []
                for piece in range(2):
                    pairs += [each[:, piece * quarter : (piece + 1) * quarter] for each in both]
                units[place, :head, :] = values[mid * x : mid * x + head]
                units[place, head:, :] = jnp.concatenate(pairs, axis=1)


def parts_of(value):
    upper = value.astype(bf16)
    return upper, (value - upper.astype(f32)).astype(bf16)


def dot_of(left, right):
    dot = lambda p, q: jnp.dot(p, q, preferred_element_type=f32)
    small = dot(left[0], right[1]) + dot(left[1], right[0])
    return dot(left[0], right[0]) + small


def picks_kernel(group_cols, info, sampled, acts, out_grad, picks, acts_buf, grad_buf, sems):
    group = info[0]
    block = 128
    span = grad_buf.shape[1]
    tokens, cols = acts.shape
    chunk = tokens // 4
    last = out_grad.shape[1] // block - span // block
    start = pl.multiple_of(jnp.minimum((group * group_cols) // block, last) * block, block)
    copies = []
    for part in range(4):
        some = pl.ds(part * chunk, chunk)
        copies.append(
            (
                pltpu.make_async_copy(acts.at[some, :], acts_buf.at[some, :], sems.at[part]),
                pltpu.make_async_copy(
                    out_grad.at[some, pl.ds(start, span)], grad_buf.at[some, :], sems.at[4 + part]
                ),
            )
        )
        for copy in copies[-1]:
            copy.start()
    drawn = sampled.shape[1]
    row = lax.broadcasted_iota(jnp.int32, (drawn, drawn), 0)
    col = lax.broadcasted_iota(jnp.int32, (drawn, drawn), 1)
    upright = jnp.sum(jnp.where(row == col, sampled[...], 0), axis=1, keepdims=True)
    found = jnp.zeros((drawn, cols), f32)
    grads = jnp.zeros((drawn, span), f32)
    for part in range(4):
        place = lax.broadcasted_iota(jnp.int32, (drawn, chunk), 1) + part * chunk
        chosen = (place == upright).astype(bf16)
        some = slice(part * chunk, (part + 1) * chunk)
        copies[part][0].wait()
        found += jnp.dot(chosen, acts_buf[some, :], preferred_element_type=f32)
        copies[part][1].wait()
        grads += jnp.dot(chosen, grad_buf[some, :], preferred_element_type=f32)
    picks[:, :cols] = found.astype(bf16)
    pad = jnp.zeros((drawn, picks.shape[1] - cols - group_cols), f32)
    for which in range(4):
        begin = min((which * group_cols) // block, last) * block
        offset = which * group_cols - begin

        @pl.when(group == which)
        def _():
            part = jnp.concatenate([grads[:, offset : offset + group_cols], pad], axis=1)
            picks[:, cols:] = part.astype(bf16)


def split_units(group, head, width_g):
    half = group.shape[1] // 2
    mid = width_g // 2
    middle = group[head : head + width_g]
    packed = [
        jnp.concatenate([middle[:mid, cols], middle[mid:, cols]], axis=1)
        for cols in (slice(0, half), slice(half, 2 * half))
    ]
    return (
        jnp.concatenate([group[:head], packed[0]], axis=0),
        jnp.concatenate([group[head + width_g :], packed[1]], axis=0),
    )


def partial_kernel(
    group_cols, width_g, info, out_grad, acts, send_a, keep_a, send_b, keep_b, grad_buf, acts_buf,
    raw, sems
):
    side, low = info[1], info[2]
    head = 2 * width_g
    outs = out_grad.shape[1]
    half = acts.shape[1] // 2
    block = outs // 5
    first = pltpu.make_async_copy(acts, acts_buf, sems.at[5])
    first.start()
    copies = []
    for step in range(5):
        columns = pl.ds(step * block, block)
        copies.append(
            pltpu.make_async_copy(out_grad.at[:, columns], grad_buf.at[:, columns], sems.at[step])
        )
        copies[-1].start()
    first.wait()
    for step in range(5):
        copies[step].wait()
        columns = slice(step * block, (step + 1) * block)
        raw[columns, :] = jnp.dot(
            grad_buf[:, columns].T, acts_buf[...], preferred_element_type=f32
        )
        if step == 0:
            continue
        place = step - 1
        span = slice(place * group_cols, (place + 1) * group_cols)
        zero, one = split_units(raw[span, :half], head, width_g)
        keep_a[place] = jnp.where(side == 0, zero, one)
        encode_to(send_a, place, jnp.where(side == 0, one, zero))
        if place % 2 == 0:
            continue
        before = slice((place - 1) * group_cols, place * group_cols)
        zero = split_units(raw[before, half:], head, width_g)
        one = split_units(raw[span, half:], head, width_g)
        for x in range(2):
            keep_b[place - 1 + x] = jnp.where(low == 0, zero[x], one[x])
            encode_to(send_b, place - 1 + x, jnp.where(low == 0, one[x], zero[x]))


def add_kernel(bit_at, inner, info, got, held, send, keep):
    bit = info[bit_at]
    rows = held.shape[1]
    count = send.shape[0]

    def place(j, value):
        return 2 * j + value if inner else value * count + j

    for j in range(count):
        away = place(j, 1 - bit)
        encode_to(send, j, held[away] + decode(got[away], rows))
    for j in range(count):
        home = place(j, bit)
        keep[j] = held[home] + decode(got[home], rows)


def last_add_kernel(info, got_a, held_a, got_b, held_b, send, keep):
    high = info[4]
    rows = keep.shape[1]
    for piece, (got, held) in enumerate(((got_a, held_a), (got_b, held_b))):
        encode_to(send, piece, held[1 - high] + decode(got[1 - high], rows))
        keep[piece] = held[high] + decode(got[high], rows)


def add_step(info, bit_at, inner, got, held):
    count = held.shape[0] // 2
    return pl.pallas_call(
        lambda *refs: add_kernel(bit_at, inner, *refs),
        in_specs=[smem, vmem, vmem],
        out_specs=[vmem, vmem],
        out_shape=[
            shaped((count,) + got.shape[1:], jnp.int16),
            shaped((count,) + held.shape[1:], f32),
        ],
        compiler_params=params(24),
        name="add",
    )(info, got, held)


def block_places(count_a, width_a, count_g, width_g):
    blocks, column, row = [], 0, 0
    for is_a, count, width in ((True, count_a, width_a), (False, count_g, width_g)):
        for place in range(count):
            blocks.append((is_a, place, width, column, row))
            column += width
            row += width + GROUP
    return blocks, row


def stats_kernel(blocks, info, own, one, two, packed, picks):
    place = 2 * info[4] + info[1]
    picks[place] = own[...]
    picks[place ^ 2] = one[...]
    picks[place ^ 1] = two[0]
    picks[place ^ 3] = two[1]
    everything = picks[...].reshape(picks.shape[0] * picks.shape[1], picks.shape[2])
    for _, _, width, column, row in blocks:
        rows = everything[:, column : column + width]
        stats = lax.dot_general(
            rows, rows, (((0,), (0,)), ((), ())), preferred_element_type=f32
        )
        missing = packed.shape[1] - width
        if missing:
            stats = jnp.concatenate([stats, jnp.zeros((width, missing), f32)], axis=1)

        def store(first, data):
            packed[row + first : row + first + GROUP, :] = data

        encode(stats, store)


def factor_kernel(
    share, blocks, info, own_a, own_g, packed, got, a_state, g_state, a_new, g_new, inv_a, needed,
    inv_g
):
    group = info[0]
    count_a, count_g = a_state.shape[0], g_state.shape[0]
    errors, inverses, scales = [], [], []
    for is_a, place, width, _, first in blocks:
        span = slice(first, first + width + GROUP)
        stats = decode(packed[span, :], width) + decode(got[span, :], width)
        stats = stats[:, :width]
        slot = own_a[group, place] if is_a else own_g[group, place]
        stored = (a_state if is_a else g_state)[slot]
        factor = factor_decay * stored + share * stats
        (a_new if is_a else g_new)[slot] = factor
        row = lax.broadcasted_iota(jnp.int32, (width, width), 0)
        col = lax.broadcasted_iota(jnp.int32, (width, width), 1)
        identity = (row == col).astype(f32)
        trace = jnp.sum(factor * identity) / width
        damped = factor + (damping_rate * trace) * identity
        bound = jnp.max(jnp.sum(jnp.abs(damped), axis=0))
        error = identity - damped / bound
        errors.append(error)
        inverses.append(identity + error)
        scales.append(bound)
    every = range(count_a + count_g)
    errors = [parts_of(errors[i]) for i in every]
    errors = [parts_of(dot_of(errors[i], errors[i])) for i in every]
    for step in range(1, NS_IT - 1):
        grown = [dot_of(parts_of(inverses[i]), errors[i]) for i in every]
        squares = [dot_of(errors[i], errors[i]) for i in every]
        inverses = [inverses[i] + grown[i] for i in every]
        errors = [parts_of(squares[i]) for i in every]
    grown = [dot_of(parts_of(inverses[i]), errors[i]) for i in every]
    inverses = [(inverses[i] + grown[i]) / scales[i] for i in every]
    for index in every:
        if index < count_a:
            inv_a[index] = inverses[index]
        else:
            inv_g[index - count_a] = inverses[index]
    side = info[1]
    for index, place in enumerate((3 * side, 1 + 3 * side, 2)):
        encode_to(needed, index, inv_g[place])


def precon_kernel(info, got, held, inv_g, inv_a, top, mid, total, coded):
    side = info[1]
    width_g, width_a = inv_g.shape[-1], inv_a.shape[-1]
    half = width_g // 2
    dot = lambda p, q: dot_of(parts_of(p), parts_of(q))
    left = [decode(inv_g[place], width_g) for place in range(3)]
    squares = jnp.zeros((width_g, width_a), f32)
    for piece in range(2):
        part = held[piece] + decode(got[piece], held.shape[1])
        for place in range(2):
            for block in range(2):
                values = dot(
                    left[place],
                    part[
                        place * width_g : (place + 1) * width_g,
                        block * width_a : (block + 1) * width_a,
                    ],
                )
                values = dot(values, inv_a[2 * piece + block])
                squares += values * values
                column = (2 * piece + block) * width_a
                top[place * width_g : (place + 1) * width_g, column : column + width_a] = values
        packed = part[2 * width_g : 2 * width_g + half, :]
        values = jnp.concatenate([packed[:, :width_a], packed[:, width_a:]], axis=0)
        values = dot(dot(left[2], values), inv_a[2 * piece + side])
        squares += values * values
        mid[:, piece * width_a : (piece + 1) * width_a] = values
    total[...] = jnp.full(total.shape, jnp.sum(squares), f32)
    width = mid.shape[1] // 2
    folded = [fold(mid[:, :width]), fold(mid[:, width:])]
    unit = jnp.concatenate([top[...], jnp.concatenate(folded, axis=1)], axis=0)
    encode_fine(unit, coded)


def round_kernel(
    entries, total, got_total, base, scaled, scaled_far, factor,
    rounded_a, rounded_b
):
    rows, half = rounded_a.shape[1:]
    mean_sq = (total[0:1, :] + got_total[0:1, :]) / entries
    norm = 1.0 / jnp.sqrt(mean_sq + epsilon_sq)
    norm = jnp.concatenate([norm, norm], axis=1)
    factor[...] = jnp.broadcast_to(norm, factor.shape)
    for place, moving in enumerate((scaled, scaled_far)):
        fresh = base[place] - (learn_rate * norm) * decode_fine(moving, rows)
        rounded_a[place] = fresh[:, :half].astype(bf16)
        rounded_b[place] = fresh[:, half:].astype(bf16)


def update_kernel(info, factor, top, middle, got, momentum, weight, momentum_new, weight_new):
    rows, cols = momentum.shape
    quarter = cols // 4
    head = top.shape[0]
    mid = rows - head
    norm = factor[0:1, :]

    def step(place, precon):
        span = slice(place, place + precon.shape[0])
        moved = momentum_rate * momentum[span, :] + precon * norm + decay_rate * weight[span, :]
        momentum_new[span, :] = moved
        weight_new[span, :] = weight[span, :] - learn_rate * moved

    for x in range(2):

        @pl.when(info[1] == x)
        def _():
            own = middle[mid * x : mid * (x + 1), :]
            pairs = []
            for piece in range(2):
                columns = slice(piece * quarter, (piece + 1) * quarter)
                both = [own[:, columns], got[:mid, columns]]
                pairs += both if x == 0 else both[::-1]
            step(head * (1 - x), jnp.concatenate(pairs, axis=1))
            step(mid * x, top[...])


def place_kernel(head, info, *refs):
    parts, out = refs[:6], refs[6]
    shard = info[3]
    rows, half = parts[0].shape[1:]
    mid = rows - head
    quarter = half // 2
    codes = ((0, 4), (2, 6), (1, 5, 3, 7), (0, 4), (1, 5), (2, 6, 3, 7))
    for index, (part, units) in enumerate(zip(parts, codes)):
        first = half * (index // 3)
        for place, code in enumerate(units):
            unit = shard ^ code
            side = unit & 1
            start = (unit >> 1) * (2 * rows)
            own = pl.multiple_of(start + side * (head + 2 * mid), 16)
            out[pl.ds(own, head), first : first + half] = part[place, :head, :]
            columns = pl.ds(pl.multiple_of(first + side * quarter, 128), quarter)
            for which in range(2):
                shared = pl.multiple_of(start + head + which * mid, 16)
                out[pl.ds(shared, mid), columns] = part[
                    place, head:, which * quarter : (which + 1) * quarter
                ]


def fast(acts, out_grad, sample_rows, own_a, own_g, a_state, g_state, momentum, weight):
    shard_pos = lax.axis_index("shard")
    tensor_pos = lax.axis_index("tensor")
    side, low, high = shard_pos & 1, (shard_pos >> 1) & 1, shard_pos >> 2
    count_a, width_a = a_state.shape[1], a_state.shape[2]
    count_g, width_g = g_state.shape[1], g_state.shape[2]
    group_cols = count_g * width_g
    tokens, cols = acts.shape
    outs = out_grad.shape[1]
    rows = momentum.shape[0]
    drawn = sample_rows.shape[0]
    samples = drawn * 8
    share = (1.0 - factor_decay) / samples
    half = cols // 2
    head = 2 * width_g
    mid = width_g // 2
    info = jnp.stack([tensor_pos, side, low, shard_pos, high])

    send_a, keep_a, send_b, keep_b = pl.pallas_call(
        lambda *refs: partial_kernel(group_cols, width_g, *refs),
        in_specs=[smem, main, main],
        out_specs=[vmem] * 4,
        out_shape=[
            shaped((4, rows + GROUP, half), jnp.int16),
            shaped((4, rows, half), f32),
        ]
        * 2,
        scratch_shapes=[
            pltpu.VMEM((tokens, outs), bf16),
            pltpu.VMEM((tokens, cols), bf16),
            pltpu.VMEM((outs, cols), f32),
            pltpu.SemaphoreType.DMA((6,)),
        ],
        compiler_params=params(56),
        name="partial",
    )(info, out_grad, acts)
    sample_rows, send_a, send_b = lax.optimization_barrier((sample_rows, send_a, send_b))
    got_a = swap(send_a, 1)
    got_b = swap(send_b, 2)

    wide = cols + -(-group_cols // 128) * 128
    picks = pl.pallas_call(
        lambda *refs: picks_kernel(group_cols, *refs),
        in_specs=[smem, vmem, main, main],
        out_specs=vmem,
        out_shape=shaped((drawn, wide), bf16),
        scratch_shapes=[
            pltpu.VMEM((tokens, cols), bf16),
            pltpu.VMEM((tokens, 640), bf16),
            pltpu.SemaphoreType.DMA((8,)),
        ],
        compiler_params=params(50),
        name="picks",
    )(info, sample_rows.reshape(1, -1), acts, out_grad)
    one = swap(picks, 4)

    base = pl.pallas_call(
        base_kernel,
        in_specs=[vmem, vmem],
        out_specs=vmem,
        out_shape=shaped((fine_rows(rows), cols), jnp.int16),
        compiler_params=params(16),
        name="base",
    )(momentum, weight)
    base_far = swap(base, 4)
    two = swap(jnp.stack([picks, one]), 1)

    send_a, keep_a = add_step(info, 2, True, got_a, keep_a)
    send_b, keep_b = add_step(info, 1, True, got_b, keep_b)
    send_a, send_b = lax.optimization_barrier((send_a, send_b))
    got_a = swap(send_a, 2)
    got_b = swap(send_b, 1)
    two, base_far = lax.optimization_barrier((two, base_far))
    blocks, packed_rows = block_places(count_a, width_a, count_g, width_g)
    packed = pl.pallas_call(
        lambda *refs: stats_kernel(blocks, *refs),
        in_specs=[smem] + [vmem] * 3,
        out_specs=vmem,
        out_shape=shaped((packed_rows, width_a), jnp.int16),
        scratch_shapes=[pltpu.VMEM((4, drawn, wide), bf16)],
        compiler_params=params(16),
        name="stats",
    )(info, picks, one, two)
    got_packed = swap(packed, 2)

    send, keep = pl.pallas_call(
        last_add_kernel,
        in_specs=[smem] + [vmem] * 4,
        out_specs=[vmem, vmem],
        out_shape=[
            shaped((2, rows + GROUP, half), jnp.int16),
            shaped((2, rows, half), f32),
        ],
        compiler_params=params(24),
        name="last_add",
    )(info, got_a, keep_a, got_b, keep_b)
    got = swap(send, 4)

    give = pl.pallas_call(
        lambda *refs: side_kernel(head, mid, *refs),
        in_specs=[smem] + [vmem] * 2,
        out_specs=vmem,
        out_shape=shaped((2, fine_rows(mid), half), jnp.int16),
        compiler_params=params(16),
        name="sides",
    )(info, base, base_far)
    base_units = pl.pallas_call(
        lambda *refs: pack_kernel(head, mid, *refs),
        in_specs=[smem] + [vmem] * 3,
        out_specs=vmem,
        out_shape=shaped((2, rows, cols), f32),
        compiler_params=params(16),
        name="pack",
    )(info, base, base_far, swap(give, 1))
    got_packed, base_units = lax.optimization_barrier((got_packed, base_units))

    new_a, new_g, inv_a, needed = pl.pallas_call(
        lambda *refs: factor_kernel(share, blocks, *refs),
        in_specs=[smem] * 3 + [vmem] * 4,
        out_specs=[vmem] * 4,
        out_shape=[
            shaped(a_state.shape[1:], f32),
            shaped(g_state.shape[1:], f32),
            shaped(a_state.shape[1:], f32),
            shaped((3, width_g + GROUP, width_g), jnp.int16),
        ],
        scratch_shapes=[pltpu.VMEM(g_state.shape[1:], f32)],
        compiler_params=params(24),
        name="factors",
    )(info, own_a, own_g, packed, got_packed, a_state[0], g_state[0])
    route = [
        ((2 * a + b) * 4 + c, (2 * c + b) * 4 + (a ^ 2))
        for a in range(4)
        for b in range(2)
        for c in range(4)
    ]
    inv_rows = lax.ppermute(needed, ("shard", "tensor"), route)

    top, middle, total, scaled = pl.pallas_call(
        precon_kernel,
        in_specs=[smem] + [vmem] * 4,
        out_specs=[vmem] * 4,
        out_shape=[
            shaped((head, cols), f32),
            shaped((width_g, half), f32),
            shaped((8, half), f32),
            shaped((fine_rows(rows), cols), jnp.int16),
        ],
        compiler_params=params(24),
        name="precon",
    )(info, got, keep, inv_rows, inv_a)

    scaled_far = swap(scaled, 4)
    give = pick(side, middle[mid:], middle[:mid])
    got = swap(jnp.concatenate([give, total], axis=0), 1)
    along_y = swap_t(total, 2)
    along_both = swap_both(total, 1, 2)
    total = (total + got[mid:]) + (along_y + along_both)
    total = total + swap_t(total, 1)
    total = total + swap(total, 4)
    factor, rounded_a, rounded_b = pl.pallas_call(
        lambda *refs: round_kernel(rows * 8 * cols * 4, *refs),
        in_specs=[vmem] * 5,
        out_specs=[vmem] * 3,
        out_shape=[
            shaped((8, cols), f32),
            shaped((2, rows, half), bf16),
            shaped((2, rows, half), bf16),
        ],
        compiler_params=params(24),
        name="round",
    )(total, swap(total, 2), base_units, scaled, scaled_far)

    along_l = swap(rounded_a, 2)
    along_x = swap(rounded_b, 1)
    momentum_new, weight_new = pl.pallas_call(
        update_kernel,
        in_specs=[smem] + [vmem] * 6,
        out_specs=[vmem] * 2,
        out_shape=[shaped((rows, cols), f32)] * 2,
        compiler_params=params(16),
        name="update",
    )(info, factor, top, middle, got, momentum, weight)
    along_l, along_x, momentum_new, weight_new = lax.optimization_barrier(
        (along_l, along_x, momentum_new, weight_new)
    )
    rest_a = swap(jnp.concatenate([rounded_a, along_l]), 1)
    rest_b = swap(jnp.concatenate([rounded_b, along_x]), 2)
    gathered = pl.pallas_call(
        lambda *refs: place_kernel(head, *refs),
        in_specs=[smem] + [vmem] * 6,
        out_specs=vmem,
        out_shape=shaped((rows * 8, cols), bf16),
        compiler_params=params(16),
        name="place",
    )(info, rounded_a, along_l, rest_a, rounded_b, along_x, rest_b)
    return (new_a[None], new_g[None], momentum_new, weight_new, gathered)


def local(acts, out_grad, sample_rows, own_a, own_g, a_state, g_state, momentum, weight):
    shapes_fit = (
        lax.axis_size("shard") == 8
        and lax.axis_size("tensor") == 4
        and a_state.shape[1:] == (4, 128, 128)
        and g_state.shape[1:] == (5, 96, 96)
    )
    plan = fast if shapes_fit else general
    return plan(acts, out_grad, sample_rows, own_a, own_g, a_state, g_state, momentum, weight)


def solution(mesh):
    return jax.shard_map(
        local,
        mesh=mesh,
        in_specs=(
            P("shard", "tensor"),
            P("shard", None),
            P("shard"),
            P(),
            P(),
            P("tensor", None, None, None),
            P("tensor", None, None, None),
            P("shard", "tensor"),
            P("shard", "tensor"),
        ),
        out_specs=(
            P("tensor", None, None, None),
            P("tensor", None, None, None),
            P("shard", "tensor"),
            P("shard", "tensor"),
            P(None, "tensor"),
        ),
        check_vma=False,
    )
```

```python
import jax
import jax.numpy as jnp
from jax import lax
from jax.experimental import pallas as pl
from jax.experimental.pallas import tpu as pltpu
from jax.sharding import PartitionSpec as P

NS_IT = 5


factor_decay = 0.8
damping_rate = 0.03
momentum_rate = 0.9
decay_rate = 0.01
learn_rate = 0.05
epsilon_sq = 1e-06
highest = lax.Precision.HIGHEST
f32 = jnp.float32
bf16 = jnp.bfloat16


def newton_inverse(factor):
    width = factor.shape[-1]
    identity = jnp.eye(width, dtype=jnp.float32)
    trace_mean = jnp.trace(factor, axis1=-2, axis2=-1) / width
    damped = factor + damping_rate * trace_mean[:, None, None] * identity
    bound = jnp.max(jnp.sum(jnp.abs(damped), axis=-1), axis=-1)
    guess = identity[None] / bound[:, None, None]
    for iteration in range(NS_IT):
        product = jnp.einsum("bij,bjk->bik", damped, guess, precision=highest)
        guess = jnp.einsum("bij,bjk->bik", guess, 2.0 * identity - product, precision=highest)
    return guess


def local_stats(rows, width):
    blocks = rows.reshape(rows.shape[0], -1, width)
    return jnp.einsum("sbi,sbj->bij", blocks, blocks, preferred_element_type=jnp.float32)


def owner_part(slots, shard_pos, shard_count):
    count = slots.shape[0]
    stride = shard_count // count
    slot_pos = jnp.minimum(shard_pos // stride, count - 1)
    mine = lax.dynamic_index_in_dim(slots, slot_pos, 0, keepdims=True)
    inverse = newton_inverse(mine)
    marker = (jnp.arange(count, dtype=jnp.int32) * stride == shard_pos).astype(jnp.float32)
    return marker[:, None, None] * inverse


def general(acts, out_grad, sample_rows, own_a, own_g, a_state, g_state, momentum, weight):
    shard_count = lax.axis_size("shard")
    tensor_count = lax.axis_size("tensor")
    shard_pos = lax.axis_index("shard")
    tensor_pos = lax.axis_index("tensor")
    block_a = a_state.shape[-1]
    block_g = g_state.shape[-1]
    samples = sample_rows.shape[0] * shard_count
    fresh_share = (1.0 - factor_decay) / samples
    picked_a = jnp.take(acts, sample_rows, axis=0)
    picked_g = jnp.take(out_grad, sample_rows, axis=0)
    group_cols = out_grad.shape[1] // tensor_count
    picked_g = lax.dynamic_slice_in_dim(picked_g, tensor_pos * group_cols, group_cols, 1)
    stats_a = local_stats(picked_a, block_a)
    stats_g = local_stats(picked_g, block_g)
    row_a = lax.dynamic_index_in_dim(own_a, tensor_pos, 0, keepdims=False)
    row_g = lax.dynamic_index_in_dim(own_g, tensor_pos, 0, keepdims=False)
    select_a = (row_a[None, :] == jnp.arange(row_a.shape[0], dtype=jnp.int32)[:, None]).astype(
        jnp.float32
    )
    select_g = (row_g[None, :] == jnp.arange(row_g.shape[0], dtype=jnp.int32)[:, None]).astype(
        jnp.float32
    )
    summed_a, summed_g = lax.psum((fresh_share * stats_a, fresh_share * stats_g), "shard")
    stored_a = jnp.einsum("sb,sij->bij", select_a, a_state[0], precision=highest)
    stored_g = jnp.einsum("sb,sij->bij", select_g, g_state[0], precision=highest)
    fac_a = factor_decay * stored_a + summed_a
    fac_g = factor_decay * stored_g + summed_g
    slots_a = jnp.einsum("sb,bij->sij", select_a, fac_a, precision=highest)
    slots_g = jnp.einsum("sb,bij->sij", select_g, fac_g, precision=highest)
    new_a_state = slots_a[None]
    new_g_state = slots_g[None]
    slot_inv_a, slot_inv_g = lax.psum(
        (owner_part(slots_a, shard_pos, shard_count), owner_part(slots_g, shard_pos, shard_count)),
        "shard",
    )
    inv_a = jnp.einsum("sb,sij->bij", select_a, slot_inv_a, precision=highest)
    local_inv_g = jnp.einsum("sb,sij->bij", select_g, slot_inv_g, precision=highest)
    inv_g = lax.all_gather(local_inv_g, "tensor", axis=0, tiled=True)
    raw_product = lax.dot_general(
        out_grad, acts, (((0,), (0,)), ((), ())), preferred_element_type=jnp.float32
    )
    left_done = jnp.einsum(
        "bij,bjd->bid", inv_g, raw_product.reshape(inv_g.shape[0], block_g, -1), precision=highest
    ).reshape(raw_product.shape)
    owned_rows = lax.psum_scatter(left_done, "shard", scatter_dimension=0, tiled=True)
    precon = jnp.einsum(
        "qbi,bij->qbj",
        owned_rows.reshape(owned_rows.shape[0], -1, block_a),
        inv_a,
        precision=highest,
    ).reshape(owned_rows.shape)
    square_total = lax.psum(jnp.sum(precon * precon), ("shard", "tensor"))
    mean_sq = square_total / (momentum.shape[0] * shard_count * momentum.shape[1] * tensor_count)
    update = precon / jnp.sqrt(mean_sq + epsilon_sq)
    momentum_new = momentum_rate * momentum + update + decay_rate * weight
    weight_new = weight - learn_rate * momentum_new
    gathered = lax.all_gather(weight_new.astype(jnp.bfloat16), "shard", axis=0, tiled=True)
    return (new_a_state, new_g_state, momentum_new, weight_new, gathered)


GROUP = 16
vmem = pl.BlockSpec(memory_space=pltpu.VMEM)
smem = pl.BlockSpec(memory_space=pltpu.SMEM)
main = pl.BlockSpec(memory_space=pl.ANY)


def params(mib):
    return pltpu.CompilerParams(vmem_limit_bytes=mib * 2**20)


def shaped(shape, kind):
    return jax.ShapeDtypeStruct(shape, kind)


def cost(flops, moved):
    return pl.CostEstimate(flops=flops, bytes_accessed=moved, transcendentals=0)


def swap(value, bit):
    return lax.ppermute(value, "shard", [(i, i ^ bit) for i in range(8)])


def swap_t(value, bit):
    return lax.ppermute(value, "tensor", [(i, i ^ bit) for i in range(4)])


def swap_both(value, bit, bit_t):
    route = [(4 * s + t, 4 * (s ^ bit) + (t ^ bit_t)) for s in range(8) for t in range(4)]
    return lax.ppermute(value, ("shard", "tensor"), route)


def pick(flag, if_zero, if_one):
    return jnp.where(flag == 0, if_zero, if_one)


def encode(value, store):
    rows, width = value.shape
    powers = []
    for first in range(0, rows, GROUP):
        part = value[first : first + GROUP]
        top = jnp.max(jnp.abs(part), axis=0, keepdims=True)
        power = jnp.floor(jnp.log2(jnp.maximum(top, 1e-30)))
        scaled = jnp.clip(jnp.round(part * jnp.exp2(14.0 - power)), -32767.0, 32767.0)
        store(first, scaled.astype(jnp.int32).astype(jnp.int16))
        powers.append(power)
    powers += [jnp.zeros((1, width), f32)] * (GROUP - len(powers))
    store(rows, jnp.concatenate(powers, axis=0).astype(jnp.int32).astype(jnp.int16))


def decode(packed, rows):
    whole = packed.astype(jnp.int32).astype(f32)
    scales = jnp.exp2(whole[rows : rows + GROUP] - 14.0)
    parts = [
        whole[first : first + GROUP] * scales[first // GROUP : first // GROUP + 1]
        for first in range(0, rows, GROUP)
    ]
    return jnp.concatenate(parts, axis=0)


def encode_to(ref, index, value):
    def store(first, data):
        ref[index, first : first + GROUP, :] = data

    encode(value, store)


FINE = 8
FULL = 32767.0
STEPS = 128.0


def encode_fine(value, ref):
    rows, width = value.shape
    powers = []
    for first in range(0, rows, 2 * FINE):
        scaled = []
        for start in (first, first + FINE):
            part = value[start : start + FINE]
            top = jnp.max(jnp.abs(part), axis=0, keepdims=True)
            power = jnp.ceil(jnp.log2(jnp.maximum(top, 1e-30)) * STEPS)
            scale = jnp.exp2(power * (-1.0 / STEPS)) * FULL
            scaled.append(jnp.clip(jnp.round(part * scale), -FULL, FULL))
            powers.append(power)
        ref[first : first + 2 * FINE, :] = (
            jnp.concatenate(scaled, axis=0).astype(jnp.int32).astype(jnp.int16)
        )
    powers += [jnp.zeros((1, width), f32)] * (-len(powers) % (2 * FINE))
    for first in range(0, len(powers), 2 * FINE):
        ref[rows + first : rows + first + 2 * FINE, :] = (
            jnp.concatenate(powers[first : first + 2 * FINE], axis=0)
            .astype(jnp.int32)
            .astype(jnp.int16)
        )


def decode_fine(ref, rows):
    values = ref[:rows, :].astype(jnp.int32).astype(f32)
    powers = ref[rows:, :].astype(jnp.int32).astype(f32)
    scales = jnp.exp2(powers * (1.0 / STEPS)) * (1.0 / FULL)
    parts = [
        values[first : first + FINE] * scales[first // FINE : first // FINE + 1]
        for first in range(0, rows, FINE)
    ]
    return jnp.concatenate(parts, axis=0)


def fine_rows(rows):
    return rows + -(-(rows // FINE) // (2 * FINE)) * 2 * FINE


def fold(rows):
    half = rows.shape[0] // 2
    return jnp.concatenate([rows[:half], rows[half:]], axis=1)


def fold(rows):
    half = rows.shape[0] // 2
    return jnp.concatenate([rows[:half], rows[half:]], axis=1)


def base_kernel(momentum, weight, packed):
    kept = momentum_rate * momentum[...] + decay_rate * weight[...]
    encode_fine(weight[...] - learn_rate * kept, packed)


def shared_rows(side, head, mid):
    return slice(head * (1 - side), head * (1 - side) + mid)


def kept_columns(value, side):
    quarter = value.shape[1] // 4
    blocks = [value[:, (2 * p + side) * quarter : (2 * p + side + 1) * quarter] for p in (0, 1)]
    return jnp.concatenate(blocks, axis=1)


def side_kernel(head, mid, info, own, far, give):
    rows = head + mid
    for x in range(2):

        @pl.when(info[1] == x)
        def _():
            span = shared_rows(x, head, mid)
            first = span.start // FINE
            for place, packed in enumerate((own, far)):
                values = packed[:rows, :].astype(jnp.int32)[span]
                powers = packed[rows:, :].astype(jnp.int32)[first : first + mid // FINE]
                missing = jnp.zeros((2 * FINE - powers.shape[0], powers.shape[1]), jnp.int32)
                all_rows = jnp.concatenate([values, powers, missing], axis=0)
                give[place] = kept_columns(all_rows, 1 - x).astype(jnp.int16)


def pack_kernel(head, mid, info, own, far, got, units):
    for x in range(2):

        @pl.when(info[1] == x)
        def _():
            for place, packed in enumerate((own, far)):
                values = decode_fine(packed, head + mid)
                shared = kept_columns(values[shared_rows(x, head, mid)], x)
                other = decode_fine(got.at[place], mid)
                both = (shared, other) if x == 0 else (other, shared)
                quarter = shared.shape[1] // 2
                pairs = []
                for piece in range(2):
                    pairs += [each[:, piece * quarter : (piece + 1) * quarter] for each in both]
                units[place, :head, :] = values[mid * x : mid * x + head]
                units[place, head:, :] = jnp.concatenate(pairs, axis=1)


def parts_of(value):
    upper = value.astype(bf16)
    return upper, (value - upper.astype(f32)).astype(bf16)


def dot_of(left, right):
    dot = lambda p, q: jnp.dot(p, q, preferred_element_type=f32)
    small = dot(left[0], right[1]) + dot(left[1], right[0])
    return dot(left[0], right[0]) + small


def picks_kernel(group_cols, info, sampled, acts, out_grad, picks, acts_buf, grad_buf, sems):
    group = info[0]
    block = 128
    span = grad_buf.shape[1]
    tokens, cols = acts.shape
    chunk = tokens // 4
    last = out_grad.shape[1] // block - span // block
    start = pl.multiple_of(jnp.minimum((group * group_cols) // block, last) * block, block)
    copies = []
    for part in range(4):
        some = pl.ds(part * chunk, chunk)
        copies.append(
            (
                pltpu.make_async_copy(acts.at[some, :], acts_buf.at[some, :], sems.at[part]),
                pltpu.make_async_copy(
                    out_grad.at[some, pl.ds(start, span)], grad_buf.at[some, :], sems.at[4 + part]
                ),
            )
        )
        for copy in copies[-1]:
            copy.start()
    drawn = sampled.shape[1]
    row = lax.broadcasted_iota(jnp.int32, (drawn, drawn), 0)
    col = lax.broadcasted_iota(jnp.int32, (drawn, drawn), 1)
    upright = jnp.sum(jnp.where(row == col, sampled[...], 0), axis=1, keepdims=True)
    found = jnp.zeros((drawn, cols), f32)
    grads = jnp.zeros((drawn, span), f32)
    for part in range(4):
        place = lax.broadcasted_iota(jnp.int32, (drawn, chunk), 1) + part * chunk
        chosen = (place == upright).astype(bf16)
        some = slice(part * chunk, (part + 1) * chunk)
        copies[part][0].wait()
        found += jnp.dot(chosen, acts_buf[some, :], preferred_element_type=f32)
        copies[part][1].wait()
        grads += jnp.dot(chosen, grad_buf[some, :], preferred_element_type=f32)
    picks[:, :cols] = found.astype(bf16)
    pad = jnp.zeros((drawn, picks.shape[1] - cols - group_cols), f32)
    for which in range(4):
        begin = min((which * group_cols) // block, last) * block
        offset = which * group_cols - begin

        @pl.when(group == which)
        def _():
            part = jnp.concatenate([grads[:, offset : offset + group_cols], pad], axis=1)
            picks[:, cols:] = part.astype(bf16)


def split_units(group, head, width_g):
    half = group.shape[1] // 2
    mid = width_g // 2
    middle = group[head : head + width_g]
    packed = [
        jnp.concatenate([middle[:mid, cols], middle[mid:, cols]], axis=1)
        for cols in (slice(0, half), slice(half, 2 * half))
    ]
    return (
        jnp.concatenate([group[:head], packed[0]], axis=0),
        jnp.concatenate([group[head + width_g :], packed[1]], axis=0),
    )


def partial_kernel(
    group_cols, width_g, info, out_grad, acts, send_a, keep_a, send_b, keep_b, grad_buf, acts_buf,
    raw, sems
):
    side, low = info[1], info[2]
    head = 2 * width_g
    outs = out_grad.shape[1]
    half = acts.shape[1] // 2
    block = outs // 5
    first = pltpu.make_async_copy(acts, acts_buf, sems.at[5])
    first.start()
    copies = []
    for step in range(5):
        columns = pl.ds(step * block, block)
        copies.append(
            pltpu.make_async_copy(out_grad.at[:, columns], grad_buf.at[:, columns], sems.at[step])
        )
        copies[-1].start()
    first.wait()
    for step in range(5):
        copies[step].wait()
        columns = slice(step * block, (step + 1) * block)
        raw[columns, :] = jnp.dot(
            grad_buf[:, columns].T, acts_buf[...], preferred_element_type=f32
        )
        if step == 0:
            continue
        place = step - 1
        span = slice(place * group_cols, (place + 1) * group_cols)
        zero, one = split_units(raw[span, :half], head, width_g)
        keep_a[place] = jnp.where(side == 0, zero, one)
        encode_to(send_a, place, jnp.where(side == 0, one, zero))
        if place % 2 == 0:
            continue
        before = slice((place - 1) * group_cols, place * group_cols)
        zero = split_units(raw[before, half:], head, width_g)
        one = split_units(raw[span, half:], head, width_g)
        for x in range(2):
            keep_b[place - 1 + x] = jnp.where(low == 0, zero[x], one[x])
            encode_to(send_b, place - 1 + x, jnp.where(low == 0, one[x], zero[x]))


def add_kernel(bit_at, inner, info, got, held, send, keep):
    bit = info[bit_at]
    rows = held.shape[1]
    count = send.shape[0]

    def place(j, value):
        return 2 * j + value if inner else value * count + j

    for j in range(count):
        away = place(j, 1 - bit)
        encode_to(send, j, held[away] + decode(got[away], rows))
    for j in range(count):
        home = place(j, bit)
        keep[j] = held[home] + decode(got[home], rows)


def last_add_kernel(info, got_a, held_a, got_b, held_b, send, keep):
    high = info[4]
    rows = keep.shape[1]
    for piece, (got, held) in enumerate(((got_a, held_a), (got_b, held_b))):
        encode_to(send, piece, held[1 - high] + decode(got[1 - high], rows))
        keep[piece] = held[high] + decode(got[high], rows)


def add_step(info, bit_at, inner, got, held):
    count = held.shape[0] // 2
    return pl.pallas_call(
        lambda *refs: add_kernel(bit_at, inner, *refs),
        in_specs=[smem, vmem, vmem],
        out_specs=[vmem, vmem],
        out_shape=[
            shaped((count,) + got.shape[1:], jnp.int16),
            shaped((count,) + held.shape[1:], f32),
        ],
        compiler_params=params(24),
        name="add",
    )(info, got, held)


def block_places(count_a, width_a, count_g, width_g):
    blocks, column, row = [], 0, 0
    for is_a, count, width in ((True, count_a, width_a), (False, count_g, width_g)):
        for place in range(count):
            blocks.append((is_a, place, width, column, row))
            column += width
            row += width + GROUP
    return blocks, row


def stats_kernel(blocks, info, own, one, two, packed, picks):
    place = 2 * info[4] + info[1]
    picks[place] = own[...]
    picks[place ^ 2] = one[...]
    picks[place ^ 1] = two[0]
    picks[place ^ 3] = two[1]
    everything = picks[...].reshape(picks.shape[0] * picks.shape[1], picks.shape[2])
    for _, _, width, column, row in blocks:
        rows = everything[:, column : column + width]
        stats = lax.dot_general(
            rows, rows, (((0,), (0,)), ((), ())), preferred_element_type=f32
        )
        missing = packed.shape[1] - width
        if missing:
            stats = jnp.concatenate([stats, jnp.zeros((width, missing), f32)], axis=1)

        def store(first, data):
            packed[row + first : row + first + GROUP, :] = data

        encode(stats, store)


def factor_kernel(
    share, blocks, info, own_a, own_g, packed, got, a_state, g_state, a_new, g_new, inv_a, needed,
    inv_g
):
    group = info[0]
    count_a, count_g = a_state.shape[0], g_state.shape[0]
    errors, inverses, scales = [], [], []
    for is_a, place, width, _, first in blocks:
        span = slice(first, first + width + GROUP)
        stats = decode(packed[span, :], width) + decode(got[span, :], width)
        stats = stats[:, :width]
        slot = own_a[group, place] if is_a else own_g[group, place]
        stored = (a_state if is_a else g_state)[slot]
        factor = factor_decay * stored + share * stats
        (a_new if is_a else g_new)[slot] = factor
        row = lax.broadcasted_iota(jnp.int32, (width, width), 0)
        col = lax.broadcasted_iota(jnp.int32, (width, width), 1)
        identity = (row == col).astype(f32)
        trace = jnp.sum(factor * identity) / width
        damped = factor + (damping_rate * trace) * identity
        bound = jnp.max(jnp.sum(jnp.abs(damped), axis=0))
        error = identity - damped / bound
        errors.append(error)
        inverses.append(identity + error)
        scales.append(bound)
    every = range(count_a + count_g)
    errors = [parts_of(errors[i]) for i in every]
    errors = [parts_of(dot_of(errors[i], errors[i])) for i in every]
    for step in range(1, NS_IT - 1):
        grown = [dot_of(parts_of(inverses[i]), errors[i]) for i in every]
        squares = [dot_of(errors[i], errors[i]) for i in every]
        inverses = [inverses[i] + grown[i] for i in every]
        errors = [parts_of(squares[i]) for i in every]
    grown = [dot_of(parts_of(inverses[i]), errors[i]) for i in every]
    inverses = [(inverses[i] + grown[i]) / scales[i] for i in every]
    for index in every:
        if index < count_a:
            inv_a[index] = inverses[index]
        else:
            inv_g[index - count_a] = inverses[index]
    side = info[1]
    for index, place in enumerate((3 * side, 1 + 3 * side, 2)):
        encode_to(needed, index, inv_g[place])


def precon_kernel(info, got, held, inv_g, inv_a, top, mid, total, coded):
    side = info[1]
    width_g, width_a = inv_g.shape[-1], inv_a.shape[-1]
    half = width_g // 2
    dot = lambda p, q: dot_of(parts_of(p), parts_of(q))
    left = [decode(inv_g[place], width_g) for place in range(3)]
    squares = jnp.zeros((width_g, width_a), f32)
    for piece in range(2):
        part = held[piece] + decode(got[piece], held.shape[1])
        for place in range(2):
            for block in range(2):
                values = dot(
                    left[place],
                    part[
                        place * width_g : (place + 1) * width_g,
                        block * width_a : (block + 1) * width_a,
                    ],
                )
                values = dot(values, inv_a[2 * piece + block])
                squares += values * values
                column = (2 * piece + block) * width_a
                top[place * width_g : (place + 1) * width_g, column : column + width_a] = values
        packed = part[2 * width_g : 2 * width_g + half, :]
        values = jnp.concatenate([packed[:, :width_a], packed[:, width_a:]], axis=0)
        values = dot(dot(left[2], values), inv_a[2 * piece + side])
        squares += values * values
        mid[:, piece * width_a : (piece + 1) * width_a] = values
    total[...] = jnp.full(total.shape, jnp.sum(squares), f32)
    width = mid.shape[1] // 2
    folded = [fold(mid[:, :width]), fold(mid[:, width:])]
    unit = jnp.concatenate([top[...], jnp.concatenate(folded, axis=1)], axis=0)
    encode_fine(unit, coded)


def round_kernel(
    entries, total, along_l, along_h, along_both, base, scaled, scaled_far, factor,
    rounded_a, rounded_b
):
    rows, half = rounded_a.shape[1:]
    sums = [each[0:1, :] for each in (total, along_l, along_h, along_both)]
    mean_sq = ((sums[0] + sums[1]) + (sums[2] + sums[3])) / entries
    norm = 1.0 / jnp.sqrt(mean_sq + epsilon_sq)
    norm = jnp.concatenate([norm, norm], axis=1)
    factor[...] = jnp.broadcast_to(norm, factor.shape)
    for place, moving in enumerate((scaled, scaled_far)):
        fresh = base[place] - (learn_rate * norm) * decode_fine(moving, rows)
        rounded_a[place] = fresh[:, :half].astype(bf16)
        rounded_b[place] = fresh[:, half:].astype(bf16)


def update_kernel(info, factor, top, middle, got, momentum, weight, momentum_new, weight_new):
    rows, cols = momentum.shape
    quarter = cols // 4
    head = top.shape[0]
    mid = rows - head
    norm = factor[0:1, :]

    def step(place, precon):
        span = slice(place, place + precon.shape[0])
        moved = momentum_rate * momentum[span, :] + precon * norm + decay_rate * weight[span, :]
        momentum_new[span, :] = moved
        weight_new[span, :] = weight[span, :] - learn_rate * moved

    for x in range(2):

        @pl.when(info[1] == x)
        def _():
            own = middle[mid * x : mid * (x + 1), :]
            pairs = []
            for piece in range(2):
                columns = slice(piece * quarter, (piece + 1) * quarter)
                both = [own[:, columns], got[:mid, columns]]
                pairs += both if x == 0 else both[::-1]
            step(head * (1 - x), jnp.concatenate(pairs, axis=1))
            step(mid * x, top[...])


def place_kernel(head, info, *refs):
    parts, out = refs[:6], refs[6]
    shard = info[3]
    rows, half = parts[0].shape[1:]
    mid = rows - head
    quarter = half // 2
    codes = ((0, 4), (2, 6), (1, 5, 3, 7), (0, 4), (1, 5), (2, 6, 3, 7))
    for index, (part, units) in enumerate(zip(parts, codes)):
        first = half * (index // 3)
        for place, code in enumerate(units):
            unit = shard ^ code
            side = unit & 1
            start = (unit >> 1) * (2 * rows)
            own = pl.multiple_of(start + side * (head + 2 * mid), 16)
            out[pl.ds(own, head), first : first + half] = part[place, :head, :]
            columns = pl.ds(pl.multiple_of(first + side * quarter, 128), quarter)
            for which in range(2):
                shared = pl.multiple_of(start + head + which * mid, 16)
                out[pl.ds(shared, mid), columns] = part[
                    place, head:, which * quarter : (which + 1) * quarter
                ]


def fast(acts, out_grad, sample_rows, own_a, own_g, a_state, g_state, momentum, weight):
    shard_pos = lax.axis_index("shard")
    tensor_pos = lax.axis_index("tensor")
    side, low, high = shard_pos & 1, (shard_pos >> 1) & 1, shard_pos >> 2
    count_a, width_a = a_state.shape[1], a_state.shape[2]
    count_g, width_g = g_state.shape[1], g_state.shape[2]
    group_cols = count_g * width_g
    tokens, cols = acts.shape
    outs = out_grad.shape[1]
    rows = momentum.shape[0]
    drawn = sample_rows.shape[0]
    samples = drawn * 8
    share = (1.0 - factor_decay) / samples
    half = cols // 2
    head = 2 * width_g
    mid = width_g // 2
    info = jnp.stack([tensor_pos, side, low, shard_pos, high])

    send_a, keep_a, send_b, keep_b = pl.pallas_call(
        lambda *refs: partial_kernel(group_cols, width_g, *refs),
        in_specs=[smem, main, main],
        out_specs=[vmem] * 4,
        out_shape=[
            shaped((4, rows + GROUP, half), jnp.int16),
            shaped((4, rows, half), f32),
        ]
        * 2,
        scratch_shapes=[
            pltpu.VMEM((tokens, outs), bf16),
            pltpu.VMEM((tokens, cols), bf16),
            pltpu.VMEM((outs, cols), f32),
            pltpu.SemaphoreType.DMA((6,)),
        ],
        compiler_params=params(56),
        name="partial",
    )(info, out_grad, acts)
    sample_rows, send_a, send_b = lax.optimization_barrier((sample_rows, send_a, send_b))
    got_a = swap(send_a, 1)
    got_b = swap(send_b, 2)

    wide = cols + -(-group_cols // 128) * 128
    picks = pl.pallas_call(
        lambda *refs: picks_kernel(group_cols, *refs),
        in_specs=[smem, vmem, main, main],
        out_specs=vmem,
        out_shape=shaped((drawn, wide), bf16),
        scratch_shapes=[
            pltpu.VMEM((tokens, cols), bf16),
            pltpu.VMEM((tokens, 640), bf16),
            pltpu.SemaphoreType.DMA((8,)),
        ],
        compiler_params=params(50),
        name="picks",
    )(info, sample_rows.reshape(1, -1), acts, out_grad)
    one = swap(picks, 4)

    base = pl.pallas_call(
        base_kernel,
        in_specs=[vmem, vmem],
        out_specs=vmem,
        out_shape=shaped((fine_rows(rows), cols), jnp.int16),
        compiler_params=params(16),
        name="base",
    )(momentum, weight)
    base_far = swap(base, 4)
    two = swap(jnp.stack([picks, one]), 1)

    send_a, keep_a = add_step(info, 2, True, got_a, keep_a)
    send_b, keep_b = add_step(info, 1, True, got_b, keep_b)
    send_a, send_b = lax.optimization_barrier((send_a, send_b))
    got_a = swap(send_a, 2)
    got_b = swap(send_b, 1)
    two, base_far = lax.optimization_barrier((two, base_far))
    blocks, packed_rows = block_places(count_a, width_a, count_g, width_g)
    packed = pl.pallas_call(
        lambda *refs: stats_kernel(blocks, *refs),
        in_specs=[smem] + [vmem] * 3,
        out_specs=vmem,
        out_shape=shaped((packed_rows, width_a), jnp.int16),
        scratch_shapes=[pltpu.VMEM((4, drawn, wide), bf16)],
        compiler_params=params(16),
        name="stats",
    )(info, picks, one, two)
    got_packed = swap(packed, 2)

    send, keep = pl.pallas_call(
        last_add_kernel,
        in_specs=[smem] + [vmem] * 4,
        out_specs=[vmem, vmem],
        out_shape=[
            shaped((2, rows + GROUP, half), jnp.int16),
            shaped((2, rows, half), f32),
        ],
        compiler_params=params(24),
        name="last_add",
    )(info, got_a, keep_a, got_b, keep_b)
    got = swap(send, 4)

    give = pl.pallas_call(
        lambda *refs: side_kernel(head, mid, *refs),
        in_specs=[smem] + [vmem] * 2,
        out_specs=vmem,
        out_shape=shaped((2, fine_rows(mid), half), jnp.int16),
        compiler_params=params(16),
        name="sides",
    )(info, base, base_far)
    base_units = pl.pallas_call(
        lambda *refs: pack_kernel(head, mid, *refs),
        in_specs=[smem] + [vmem] * 3,
        out_specs=vmem,
        out_shape=shaped((2, rows, cols), f32),
        compiler_params=params(16),
        name="pack",
    )(info, base, base_far, swap(give, 1))
    got_packed, base_units = lax.optimization_barrier((got_packed, base_units))

    new_a, new_g, inv_a, needed = pl.pallas_call(
        lambda *refs: factor_kernel(share, blocks, *refs),
        in_specs=[smem] * 3 + [vmem] * 4,
        out_specs=[vmem] * 4,
        out_shape=[
            shaped(a_state.shape[1:], f32),
            shaped(g_state.shape[1:], f32),
            shaped(a_state.shape[1:], f32),
            shaped((3, width_g + GROUP, width_g), jnp.int16),
        ],
        scratch_shapes=[pltpu.VMEM(g_state.shape[1:], f32)],
        compiler_params=params(24),
        name="factors",
    )(info, own_a, own_g, packed, got_packed, a_state[0], g_state[0])
    route = [
        ((2 * a + b) * 4 + c, (2 * c + b) * 4 + (a ^ 2))
        for a in range(4)
        for b in range(2)
        for c in range(4)
    ]
    inv_rows = lax.ppermute(needed, ("shard", "tensor"), route)

    top, middle, total, scaled = pl.pallas_call(
        precon_kernel,
        in_specs=[smem] + [vmem] * 4,
        out_specs=[vmem] * 4,
        out_shape=[
            shaped((head, cols), f32),
            shaped((width_g, half), f32),
            shaped((8, half), f32),
            shaped((fine_rows(rows), cols), jnp.int16),
        ],
        compiler_params=params(24),
        name="precon",
    )(info, got, keep, inv_rows, inv_a)

    scaled_far = swap(scaled, 4)
    give = pick(side, middle[mid:], middle[:mid])
    got = swap(jnp.concatenate([give, total], axis=0), 1)
    along_y = swap_t(total, 2)
    along_both = swap_both(total, 1, 2)
    total = (total + got[mid:]) + (along_y + along_both)
    total = total + swap_t(total, 1)
    others = [swap(total, bits) for bits in (2, 4, 6)]
    factor, rounded_a, rounded_b = pl.pallas_call(
        lambda *refs: round_kernel(rows * 8 * cols * 4, *refs),
        in_specs=[vmem] * 7,
        out_specs=[vmem] * 3,
        out_shape=[
            shaped((8, cols), f32),
            shaped((2, rows, half), bf16),
            shaped((2, rows, half), bf16),
        ],
        compiler_params=params(24),
        name="round",
    )(total, *others, base_units, scaled, scaled_far)

    along_l = swap(rounded_a, 2)
    along_x = swap(rounded_b, 1)
    momentum_new, weight_new = pl.pallas_call(
        update_kernel,
        in_specs=[smem] + [vmem] * 6,
        out_specs=[vmem] * 2,
        out_shape=[shaped((rows, cols), f32)] * 2,
        compiler_params=params(16),
        name="update",
    )(info, factor, top, middle, got, momentum, weight)
    along_l, along_x, momentum_new, weight_new = lax.optimization_barrier(
        (along_l, along_x, momentum_new, weight_new)
    )
    rest_a = swap(jnp.concatenate([rounded_a, along_l]), 1)
    rest_b = swap(jnp.concatenate([rounded_b, along_x]), 2)
    gathered = pl.pallas_call(
        lambda *refs: place_kernel(head, *refs),
        in_specs=[smem] + [vmem] * 6,
        out_specs=vmem,
        out_shape=shaped((rows * 8, cols), bf16),
        compiler_params=params(16),
        name="place",
    )(info, rounded_a, along_l, rest_a, rounded_b, along_x, rest_b)
    return (new_a[None], new_g[None], momentum_new, weight_new, gathered)


def local(acts, out_grad, sample_rows, own_a, own_g, a_state, g_state, momentum, weight):
    shapes_fit = (
        lax.axis_size("shard") == 8
        and lax.axis_size("tensor") == 4
        and a_state.shape[1:] == (4, 128, 128)
        and g_state.shape[1:] == (5, 96, 96)
    )
    plan = fast if shapes_fit else general
    return plan(acts, out_grad, sample_rows, own_a, own_g, a_state, g_state, momentum, weight)


def solution(mesh):
    return jax.shard_map(
        local,
        mesh=mesh,
        in_specs=(
            P("shard", "tensor"),
            P("shard", None),
            P("shard"),
            P(),
            P(),
            P("tensor", None, None, None),
            P("tensor", None, None, None),
            P("shard", "tensor"),
            P("shard", "tensor"),
        ),
        out_specs=(
            P("tensor", None, None, None),
            P("tensor", None, None, None),
            P("shard", "tensor"),
            P("shard", "tensor"),
            P(None, "tensor"),
        ),
        check_vma=False,
    )
```
